128 devices in a mesh: frame: 4 (over z), patch: 32 (over x, y, core).
Axes of the slice: x: 4, y: 4, z: 4, core: 2. Of those that a mesh axis runs over, the one named last changes fastest.
Arguments:
- video: bfloat16 [8, 2048, 1152], P('frame', 'patch'), may hold values from -6 to 6
- cotangent: bfloat16 [8, 2048, 1152], P('frame', 'patch'), may hold values from -6 to 6
- frame_mask: int32 [8], replicated, may hold values 0 or 1
- spatial_project: bfloat16 [1152, 3456], replicated, may hold values from -0.1875 to 0.1875
- spatial_output: bfloat16 [1152, 1152], replicated, may hold values from -0.1875 to 0.1875
- temporal_project: bfloat16 [1152, 3456], replicated, may hold values from -0.1875 to 0.1875
- temporal_output: bfloat16 [1152, 1152], replicated, may hold values from -0.1875 to 0.1875
- spatial_inward: float32 [36, 32, 32], replicated, may hold values from -0.25 to 1.25, as said below
- spatial_outward: float32 [36, 32, 32], replicated, may hold values from -0.25 to 1.25, as said below
- temporal_inward: float32 [36, 32, 32], replicated, may hold values from -0.25 to 1.25, as said below
- temporal_outward: float32 [36, 32, 32], replicated, may hold values from -0.25 to 1.25, as said below
Outputs:
- video_gradient: bfloat16 [8, 2048, 1152], P('frame', 'patch')
- gradient_spatial_inward: float32 [36, 32, 32], replicated
- gradient_spatial_outward: float32 [36, 32, 32], replicated
- gradient_temporal_inward: float32 [36, 32, 32], replicated
- gradient_temporal_outward: float32 [36, 32, 32], replicated
The draws below stay inside these ranges and needn't reach their ends.
Inputs may be any that keep to these rules, and one draw needn't show every extreme that they name: `spatial_inward`: identity blocks plus independent entries. `spatial_outward`: identity blocks plus independent entries. `temporal_inward`: identity blocks plus independent entries. `temporal_outward`: identity blocks plus independent entries.
All inputs are finite; a program needn't handle non-finite values.
Results may differ from the reference program's by a relative error of at most 0.028.
Values may be sent and summed in bfloat16 or wider, within the bound.
A program may use at most 192 MiB of HBM per device.

```python
import math
import jax
import jax.numpy as jnp
from jax import lax

D = 1152
HEADS = 16
HEAD_DIM = 72
BLOCK = 32
NBLOCK = 36
FRAMES = 8
PATCHES = 2048


def rotation_blocks(noise):
    return jnp.eye(BLOCK, dtype=jnp.float32)[None, :, :] + noise / math.sqrt(BLOCK)


def draw_spatial_inward(key, part):
    key = jax.random.fold_in(key, 11)
    noise = 0.4 * jax.random.truncated_normal(key, -1.75, 1.75, (NBLOCK, BLOCK, BLOCK), jnp.float32)
    return rotation_blocks(noise)


def draw_spatial_outward(key, part):
    key = jax.random.fold_in(key, 12)
    noise = 0.4 * jax.random.truncated_normal(key, -1.75, 1.75, (NBLOCK, BLOCK, BLOCK), jnp.float32)
    return rotation_blocks(noise)


def draw_temporal_inward(key, part):
    key = jax.random.fold_in(key, 13)
    noise = 0.4 * jax.random.truncated_normal(key, -1.75, 1.75, (NBLOCK, BLOCK, BLOCK), jnp.float32)
    return rotation_blocks(noise)


def draw_temporal_outward(key, part):
    key = jax.random.fold_in(key, 14)
    noise = 0.4 * jax.random.truncated_normal(key, -1.75, 1.75, (NBLOCK, BLOCK, BLOCK), jnp.float32)
    return rotation_blocks(noise)


def set_ends(drawn, rng, low, high):
    spot = [jax.random.randint(jax.random.fold_in(rng, axis), (), 0, length) for axis, length in enumerate(drawn.shape)]
    widest = drawn.shape.index(max(drawn.shape))
    next_to = spot[:widest] + [(spot[widest] + 1) % drawn.shape[widest]] + spot[widest + 1:]
    return drawn.at[tuple(spot)].set(low).at[tuple(next_to)].set(high)


def block_levels(own_key, dims, shards, smallest, top_value):
    def one(dim, shards_of):
        heights = jax.random.uniform(jax.random.fold_in(jax.random.fold_in(own_key, 6), dim), (shards_of,), jnp.float32, smallest / len(shards), top_value / len(shards))
        return jnp.repeat(jnp.exp(heights), dims[dim] // shards_of).reshape((-1,) + (1,) * (len(dims) - dim - 1))

    gain = one(*shards[0])
    for cut in shards[1:]:
        gain = gain * one(*cut)
    return gain


def gaussian(rng, shape, scale, limit, split=(), held_as=jnp.bfloat16):
    loudness = block_levels(rng, shape, split, -0.22, 0.18) if split else 1.0
    entries = jax.random.normal(rng, shape, jnp.float32) * scale * loudness
    return jnp.minimum(jnp.maximum(entries, -limit), limit).astype(held_as)


def setup_inputs(seed: int = 0) -> dict:
    keys = jax.random.split(jax.random.key(seed), 12)
    video = gaussian(keys[0], (FRAMES, PATCHES, D), 1.0, 6.0, ((0, 4), (1, 32)))
    cotangent = gaussian(keys[1], (FRAMES, PATCHES, D), 1.0, 6.0, ((0, 4), (1, 32)))
    frame_mask = set_ends((jax.random.randint(keys[2], (FRAMES,), 0, 64) < 51).astype(jnp.int32), jax.random.fold_in(keys[2], 1), 0, 1)
    spatial_project = gaussian(keys[3], (D, 3 * D), D ** -0.5, 0.1875)
    spatial_output = gaussian(keys[4], (D, D), D ** -0.5, 0.1875)
    temporal_project = gaussian(keys[5], (D, 3 * D), D ** -0.5, 0.1875)
    temporal_output = gaussian(keys[6], (D, D), D ** -0.5, 0.1875)
    spatial_inward = draw_spatial_inward(jax.random.fold_in(keys[11], 71), 0)
    spatial_outward = draw_spatial_outward(jax.random.fold_in(keys[11], 71), 0)
    temporal_inward = draw_temporal_inward(jax.random.fold_in(keys[11], 71), 0)
    temporal_outward = draw_temporal_outward(jax.random.fold_in(keys[11], 71), 0)
    return dict(video=video, cotangent=cotangent, frame_mask=frame_mask, spatial_project=spatial_project, spatial_output=spatial_output, temporal_project=temporal_project, temporal_output=temporal_output, spatial_inward=spatial_inward, spatial_outward=spatial_outward, temporal_inward=temporal_inward, temporal_outward=temporal_outward)


EPSILON = 1e-06
NEGATIVE = -1e+30

def normalize(inputs):
    average = lax.optimization_barrier(jnp.mean(inputs, axis=-1, keepdims=True))
    centered = inputs - average
    variance = lax.optimization_barrier(jnp.mean(centered * centered, axis=-1, keepdims=True))
    inverse = lax.rsqrt(variance + EPSILON)
    return (centered * inverse, inverse)

def normalize_backward(adjoint, normed, inverse):
    grad_mean = lax.optimization_barrier(jnp.mean(adjoint, axis=-1, keepdims=True))
    grad_cross = lax.optimization_barrier(jnp.mean(adjoint * normed, axis=-1, keepdims=True))
    return inverse * (adjoint - grad_mean - normed * grad_cross)

def rotate(inputs, blocks):
    shaped = inputs.reshape(inputs.shape[0], blocks.shape[0], blocks.shape[1])
    turned = jnp.einsum('tnb,nbc->tnc', shaped, blocks, precision=lax.Precision.HIGHEST)
    return turned.reshape(inputs.shape)

def rotate_transposed(adjoint, blocks):
    shaped = adjoint.reshape(adjoint.shape[0], blocks.shape[0], blocks.shape[1])
    turned = jnp.einsum('tnc,nbc->tnb', shaped, blocks, precision=lax.Precision.HIGHEST)
    return turned.reshape(adjoint.shape)

def rotation_gradient(inputs, adjoint, blocks):
    left_rows = inputs.reshape(inputs.shape[0], blocks.shape[0], blocks.shape[1])
    right_rows = adjoint.reshape(adjoint.shape[0], blocks.shape[0], blocks.shape[1])
    return jnp.einsum('tnb,tnc->nbc', left_rows, right_rows, precision=lax.Precision.HIGHEST)

def attention_weights(queries, key_rows, score_bias):
    scaling = 1.0 / math.sqrt(queries.shape[-1])
    scores = jnp.einsum('nld,nmd->nlm', queries.astype(jnp.float32), key_rows.astype(jnp.float32)) * scaling + score_bias
    return jax.nn.softmax(scores, axis=-1)

def attention_forward(stacked, score_bias):
    probability = attention_weights(stacked[:, :, 0], stacked[:, :, 1], score_bias)
    rounded = lax.optimization_barrier(probability.astype(jnp.bfloat16)).astype(jnp.float32)
    result = jnp.einsum('nlm,nmd->nld', rounded, stacked[:, :, 2].astype(jnp.float32))
    return result.astype(jnp.bfloat16)

def attention_backward(stacked, adjoint, score_bias):
    queries = stacked[:, :, 0]
    key_rows = stacked[:, :, 1]
    values = stacked[:, :, 2]
    scaling = 1.0 / math.sqrt(queries.shape[-1])
    probability = attention_weights(queries, key_rows, score_bias)
    rounded = lax.optimization_barrier(probability.astype(jnp.bfloat16)).astype(jnp.float32)
    upstream = adjoint.astype(jnp.float32)
    grad_values = jnp.einsum('nlm,nld->nmd', rounded, upstream).astype(jnp.bfloat16)
    grad_weights = jnp.einsum('nld,nmd->nlm', upstream, values.astype(jnp.float32))
    delta_sum = lax.optimization_barrier(jnp.sum(probability * grad_weights, axis=-1, keepdims=True))
    grad_scores = (probability * (grad_weights - delta_sum)).astype(jnp.bfloat16)
    grad_scores = lax.optimization_barrier(grad_scores).astype(jnp.float32)
    grad_queries = (scaling * jnp.einsum('nlm,nmd->nld', grad_scores, key_rows.astype(jnp.float32))).astype(jnp.bfloat16)
    grad_keys = (scaling * jnp.einsum('nlm,nld->nmd', grad_scores, queries.astype(jnp.float32))).astype(jnp.bfloat16)
    return jnp.stack([grad_queries, grad_keys, grad_values], axis=2)

def reference(video, cotangent, frame_mask, spatial_project, spatial_output, temporal_project, temporal_output, spatial_inward, spatial_outward, temporal_inward, temporal_outward):
    token_count = FRAMES * PATCHES
    inputs = video.astype(jnp.float32).reshape(token_count, D)
    normed_one, inverse_one = normalize(inputs)
    rotated_one = rotate(normed_one, spatial_inward).astype(jnp.bfloat16)
    projected_one = jnp.dot(rotated_one, spatial_project, preferred_element_type=jnp.float32).astype(jnp.bfloat16)
    spatial_stack = projected_one.reshape(FRAMES, PATCHES, 3, HEADS, HEAD_DIM).transpose(0, 3, 1, 2, 4)
    zero_bias = jnp.zeros((1, 1), jnp.float32)

    def spatial_frame(stacked):
        return attention_forward(stacked, zero_bias)
    attended_one = lax.map(spatial_frame, spatial_stack)
    attended_one = attended_one.transpose(0, 2, 1, 3).reshape(token_count, D)
    attended_wide = lax.optimization_barrier(attended_one).astype(jnp.float32)
    outrot_one = rotate(attended_wide, spatial_outward).astype(jnp.bfloat16)
    hidden = (inputs + jnp.dot(outrot_one, spatial_output, preferred_element_type=jnp.float32)).astype(jnp.bfloat16)
    middle = lax.optimization_barrier(hidden).astype(jnp.float32)
    normed_two, inverse_two = normalize(middle)
    rotated_two = rotate(normed_two, temporal_inward).astype(jnp.bfloat16)
    projected_two = jnp.dot(rotated_two, temporal_project, preferred_element_type=jnp.float32).astype(jnp.bfloat16)
    temporal_stack = projected_two.reshape(FRAMES, PATCHES, 3, HEADS, HEAD_DIM).transpose(1, 3, 0, 2, 4)
    temporal_stack = temporal_stack.reshape(PATCHES * HEADS, FRAMES, 3, HEAD_DIM)
    positions = jnp.arange(FRAMES)
    allowed = (frame_mask[None, :] == 1) | (positions[:, None] == positions[None, :])
    score_bias = jnp.where(allowed, 0.0, NEGATIVE).astype(jnp.float32)
    attended_two = attention_forward(temporal_stack, score_bias)
    attended_two = attended_two.reshape(PATCHES, HEADS, FRAMES, HEAD_DIM).transpose(2, 0, 1, 3).reshape(token_count, D)
    validity = frame_mask.astype(jnp.float32)
    adjoint_top = (cotangent.astype(jnp.float32) * validity[:, None, None]).reshape(token_count, D)
    adjoint_outrot = jnp.dot(adjoint_top.astype(jnp.bfloat16), temporal_output.T, preferred_element_type=jnp.float32)
    term_tout = rotation_gradient(attended_two.astype(jnp.float32), adjoint_outrot, temporal_outward)
    adjoint_attended = rotate_transposed(adjoint_outrot, temporal_outward).astype(jnp.bfloat16)
    adjoint_items = adjoint_attended.reshape(FRAMES, PATCHES, HEADS, HEAD_DIM).transpose(1, 2, 0, 3)
    adjoint_items = adjoint_items.reshape(PATCHES * HEADS, FRAMES, HEAD_DIM)
    adjoint_stack = attention_backward(temporal_stack, adjoint_items, score_bias)
    adjoint_projected = adjoint_stack.reshape(PATCHES, HEADS, FRAMES, 3, HEAD_DIM).transpose(2, 0, 3, 1, 4)
    adjoint_projected = adjoint_projected.reshape(token_count, 3 * D)
    adjoint_rotated = jnp.dot(adjoint_projected, temporal_project.T, preferred_element_type=jnp.float32)
    term_tin = rotation_gradient(normed_two, adjoint_rotated, temporal_inward)
    adjoint_normed = rotate_transposed(adjoint_rotated, temporal_inward)
    adjoint_hidden = adjoint_top + normalize_backward(adjoint_normed, normed_two, inverse_two)
    adjoint_outrot = jnp.dot(adjoint_hidden.astype(jnp.bfloat16), spatial_output.T, preferred_element_type=jnp.float32)
    term_sout = rotation_gradient(attended_wide, adjoint_outrot, spatial_outward)
    adjoint_attended = rotate_transposed(adjoint_outrot, spatial_outward).astype(jnp.bfloat16)
    adjoint_items = adjoint_attended.reshape(FRAMES, PATCHES, HEADS, HEAD_DIM).transpose(0, 2, 1, 3)

    def spatial_back(paired):
        return attention_backward(paired[0], paired[1], zero_bias)
    adjoint_stack = lax.map(spatial_back, (spatial_stack, adjoint_items))
    adjoint_projected = adjoint_stack.transpose(0, 2, 3, 1, 4).reshape(token_count, 3 * D)
    adjoint_rotated = jnp.dot(adjoint_projected, spatial_project.T, preferred_element_type=jnp.float32)
    term_sin = rotation_gradient(normed_one, adjoint_rotated, spatial_inward)
    adjoint_normed = rotate_transposed(adjoint_rotated, spatial_inward)
    video_gradient = (adjoint_hidden + normalize_backward(adjoint_normed, normed_one, inverse_one)).astype(jnp.bfloat16)
    video_gradient = video_gradient.reshape(FRAMES, PATCHES, D)
    scaling = 1.0 / math.sqrt(token_count)
    return (video_gradient, term_sin * scaling, term_sout * scaling, term_tin * scaling, term_tout * scaling)
```

```python
import functools
import math

import jax
import jax.numpy as jnp
from jax import lax
from jax.experimental import pallas as pl
from jax.experimental.pallas import tpu as pltpu
from jax.sharding import PartitionSpec as P

D = 1152
HEADS = 16
HEAD_DIM = 72
BLOCK = 32
GROUPS = D // 128
FRAMES = 8
PATCHES = 2048
ZWAYS = 4
PWAYS = 32
DEVICES = ZWAYS * PWAYS
TOKENS = 128
ROWS = D // 4

EPSILON = 1e-06
NEGATIVE = -1e30
SCALE = 1.0 / math.sqrt(HEAD_DIM)
LOG2E = math.log2(math.e)
LN2 = math.log(2.0)

F32 = jnp.float32
BF16 = jnp.bfloat16
MESH = pl.DeviceIdType.MESH


def dot(a, b):
    return lax.dot_general(a, b, (((1,), (0,)), ((), ())), preferred_element_type=F32)


def dot_nt(a, b):
    return lax.dot_general(a, b, (((1,), (1,)), ((), ())), preferred_element_type=F32)


def dot_tn(a, b):
    return lax.dot_general(a, b, (((0,), (0,)), ((), ())), preferred_element_type=F32)


def lanes(shape):
    return lax.broadcasted_iota(jnp.int32, shape, len(shape) - 1)


def rows(shape):
    return lax.broadcasted_iota(jnp.int32, shape, 0)


def roll(x, amount):
    amount = amount % 128
    return x if amount == 0 else pltpu.roll(x, amount, 1)


def normalize(x):
    centered = x - jnp.mean(x, axis=-1, keepdims=True)
    inverse = lax.rsqrt(jnp.mean(centered * centered, axis=-1, keepdims=True) + EPSILON)
    return centered * inverse, inverse


def normalize_backward(adjoint, normed, inverse):
    grad_mean = jnp.mean(adjoint, axis=-1, keepdims=True)
    grad_cross = jnp.mean(adjoint * normed, axis=-1, keepdims=True)
    return inverse * (adjoint - grad_mean - normed * grad_cross)


def group(x, g):
    return x[:, g * 128 : (g + 1) * 128]


def rotate(x, blocks):
    return jnp.concatenate(
        [dot(group(x, g), blocks[g * 128 : (g + 1) * 128, :]) for g in range(GROUPS)], axis=1
    )


def rotate_transposed(x, blocks):
    return jnp.concatenate(
        [dot_nt(group(x, g), blocks[g * 128 : (g + 1) * 128, :]) for g in range(GROUPS)], axis=1
    )


def block_mask(shape):
    return (rows(shape) // BLOCK) % 4 == lanes(shape) // BLOCK


def rotation_gradient(left, right):
    mask = block_mask((128, 128))
    packed = []
    for g in range(GROUPS):
        full = jnp.where(mask, dot_tn(group(left, g), group(right, g)), 0.0)
        packed.append(full[0:32] + full[32:64] + full[64:96] + full[96:128])
    return packed


def kernel(
    mask_ref, video, cotangent, wsp_h, wso_h, wtp_h, wto_h, rsi_h, rso_h, rti_h, rto_h,
    vg_ref, red_ref,
    wsp, wso, wtp, wto, r4, bd,
    vid, cot, vid_mid, ct_mid,
    normed1, inverse1, proj,
    qkv_snd, qkv_rcv, kx, qx,
    att_snd, att_rcv, att1, top, aot, daz,
    hidp, normed2, proj2, dproj, att2, dproj_b,
    ah_snd, ah_rcv, do_snd, do_rcv, vx, dox, dosh, qsh, kt, dqt, dkv,
    dq_snd, dq_rcv,
    r1_snd, r1_rcv, r1_z, r1_chunk, r1_out,
    r2_snd, r2_rcv, r2_z, r2_chunk, r2_out,
    wsem, vsem, send_sems, recv_sems,
):
    z = lax.axis_index("frame")
    j = lax.axis_index("patch")
    me = z * PWAYS + j

    loads = [
        pltpu.make_async_copy(video, vid, wsem.at[0]),
        pltpu.make_async_copy(rsi_h, r4.at[0], wsem.at[1]),
        pltpu.make_async_copy(wsp_h, wsp, wsem.at[2]),
        pltpu.make_async_copy(cotangent, cot, wsem.at[3]),
        pltpu.make_async_copy(rso_h, r4.at[1], wsem.at[4]),
        pltpu.make_async_copy(rti_h, r4.at[2], wsem.at[5]),
        pltpu.make_async_copy(rto_h, r4.at[3], wsem.at[6]),
        pltpu.make_async_copy(wto_h, wto, wsem.at[7]),
        pltpu.make_async_copy(wso_h, wso, wsem.at[8]),
        pltpu.make_async_copy(wtp_h, wtp, wsem.at[9]),
    ]
    for load in loads:
        load.start()

    barrier = pltpu.get_barrier_semaphore()

    def greet(i, carry):
        there = lax.rem(me + i, DEVICES)
        pl.semaphore_signal(
            barrier, inc=1, device_id=(there // PWAYS, lax.rem(there, PWAYS)), device_id_type=MESH
        )
        return carry

    lax.fori_loop(1, DEVICES, greet, 0)

    def push(src, dst, phase, zz, jj):
        self_ = jnp.logical_and(zz == z, jj == j)

        @pl.when(self_)
        def _():
            pltpu.make_async_copy(src, dst, recv_sems.at[phase]).start()

        @pl.when(jnp.logical_not(self_))
        def _():
            pltpu.make_async_remote_copy(
                src_ref=src, dst_ref=dst, send_sem=send_sems.at[phase],
                recv_sem=recv_sems.at[phase], device_id=(zz, jj), device_id_type=MESH,
            ).start()

    def wait_all(sem, buffer):
        pltpu.make_async_copy(buffer, buffer, sem).wait()

    def make_blocks(index):
        tile = jnp.where(
            lax.rem(lanes((BLOCK, 128)), BLOCK) == rows((BLOCK, 128)), 1.0, 0.0
        ).astype(BF16)
        wide = dot(r4[index].astype(BF16), tile)
        bd[index] = jnp.where(block_mask((D, 128)), wide, 0.0).astype(BF16)

    loads[0].wait()
    normed, inverse = normalize(vid[...].reshape(TOKENS, D).astype(F32))
    normed1[...] = normed
    inverse1[...] = inverse
    loads[1].wait()
    make_blocks(0)
    rotated = rotate(normed1[...].astype(BF16), bd.at[0]).astype(BF16)
    dproj_b[:, 0:D] = rotated

    pl.semaphore_wait(barrier, DEVICES - 1)

    def spread(i, carry):
        zz = lax.rem(z + i, ZWAYS)
        for f in range(2):
            push(vid.at[f, pl.ds(pl.multiple_of(zz * 16, 16), 16)], vid_mid.at[2 * z + f], 0, zz, j)
        return carry

    lax.fori_loop(0, ZWAYS, spread, 0)
    loads[3].wait()

    def spread_ct(i, carry):
        zz = lax.rem(z + i, ZWAYS)
        for f in range(2):
            push(cot.at[f, pl.ds(pl.multiple_of(zz * 16, 16), 16)], ct_mid.at[2 * z + f], 1, zz, j)
        return carry

    lax.fori_loop(0, ZWAYS, spread_ct, 0)

    loads[2].wait()

    def project1(c, carry):
        at = pl.ds(pl.multiple_of(c * D, 128), D)
        proj[:, at] = dot(dproj_b[:, 0:D], wsp[:, at])
        return carry

    lax.fori_loop(0, 3, project1, 0)

    lane = lanes((TOKENS, 128))
    qscale = jnp.where(lane < HEAD_DIM, SCALE * LOG2E, 1.0)
    for h in range(HEADS):
        t, off = (HEAD_DIM * h) // 128, (HEAD_DIM * h) % 128

        def pick(section, to):
            first = proj[:, section * D + t * 128 : section * D + (t + 1) * 128]
            if off + HEAD_DIM > 128:
                second = proj[:, section * D + (t + 1) * 128 : section * D + (t + 2) * 128]
                first = jnp.where(lane >= off, first, second)
            return roll(first, to - off)

        q, k, v = pick(0, 0), pick(1, 72), pick(2, 16)
        low = (jnp.where(lane < 72, q, k) * qscale).astype(BF16)
        high = jnp.where(
            lane < 16, k, jnp.where(lane < 88, v, jnp.where(lane < 92, 1.0, 0.0))
        ).astype(BF16)
        for f in range(2):
            qkv_snd[f * HEADS + h, :, 0:128] = low[64 * f : 64 * (f + 1)]
            qkv_snd[f * HEADS + h, :, 128:256] = high[64 * f : 64 * (f + 1)]

    def send_qkv(i, carry):
        jj = lax.rem(j + i, PWAYS)
        push(qkv_snd.at[jj], qkv_rcv.at[pl.ds(pl.multiple_of(j * 64, 64), 64)], 2, z, jj)
        return carry

    lax.fori_loop(0, PWAYS, send_qkv, 0)

    for i in (4, 5, 6):
        loads[i].wait()
    make_blocks(1)
    make_blocks(2)
    make_blocks(3)
    wait_all(recv_sems.at[1], ct_mid)
    frame_row = rows((TOKENS, 1)) // 16
    valid = jnp.zeros((TOKENS, 1), F32)
    for f in range(FRAMES):
        valid = jnp.where(frame_row == f, mask_ref[f].astype(F32), valid)
    top[...] = ct_mid[...].reshape(TOKENS, D).astype(F32) * valid
    loads[7].wait()
    aot[...] = dot_nt(top[...].astype(BF16), wto[...]).astype(BF16)
    daz[:, 0:D] = rotate_transposed(aot[...], bd.at[3]).astype(BF16)
    daz[:, D:] = jnp.zeros((TOKENS, 128), BF16)

    wait_all(recv_sems.at[2], qkv_rcv)

    def prepare(i, carry):
        at = pl.ds(pl.multiple_of(i * 256, 256), 256)
        block = qkv_rcv[at, :].astype(F32)
        lane2 = lanes((256, 128))
        t0, t1 = block[:, 0:128], block[:, 128:256]
        k = roll(jnp.where(lane2 >= 72, t0, t1), -72)
        ones = jnp.where(jnp.logical_and(lane2 >= 72, lane2 < 76), 1.0, 0.0)
        kk = jnp.where(lane2 < 72, k, ones)
        kx[at, :] = kk.astype(BF16)
        v = roll(t1, -16)
        vx[at, :] = jnp.where(lane2 < 72, v, ones).astype(BF16)
        kt[:, at] = kk.T.astype(BF16)
        q = jnp.where(lane2 < 72, t0, 0.0)
        qx[at, :] = q.astype(BF16)
        q = roll(q, 72)
        qsh[at, 0:128] = jnp.where(lane2 >= 72, q, 0.0).astype(BF16)
        qsh[at, 128:256] = jnp.where(lane2 < 16, q, 0.0).astype(BF16)
        return carry

    lax.fori_loop(0, 8, prepare, 0)

    def attend(i, carry):
        at = pl.ds(pl.multiple_of(i * 256, 256), 256)
        scores = dot_nt(qx[at, :], kx[...])
        top_score = jnp.max(scores, axis=-1, keepdims=True)
        p = jnp.exp2(scores - top_score).astype(BF16)
        out = dot(p, vx[...])
        total = out[:, 72:73]
        lane2 = lanes((256, 128))
        att_snd[at, :] = jnp.where(lane2 < 72, out / total, 0.0).astype(BF16)
        neg = -(top_score + jnp.log(total) * LOG2E)
        hi = neg.astype(BF16).astype(F32)
        mid = (neg - hi).astype(BF16).astype(F32)
        lo = neg - hi - mid
        old = qx[at, :].astype(F32)
        new = jnp.where(lane2 == 72, hi, jnp.where(lane2 == 73, mid, jnp.where(lane2 == 74, lo, old)))
        qx[at, :] = new.astype(BF16)

        def send(s, c):
            there = i * 16 + s
            push(
                att_snd.at[pl.ds(pl.multiple_of(there * 16, 16), 16)],
                att_rcv.at[2 * z + j // HEADS, lax.rem(j, HEADS)],
                3, lax.rem(there, ZWAYS), there // ZWAYS,
            )
            return c

        lax.fori_loop(0, 16, send, 0)
        return carry

    lax.fori_loop(0, 8, attend, 0)

    wait_all(recv_sems.at[0], vid_mid)
    wait_all(recv_sems.at[3], att_rcv)
    tiles = [None] * (GROUPS + 1)
    for h in range(HEADS):
        t, off = (HEAD_DIM * h) // 128, (HEAD_DIM * h) % 128
        r = roll(att_rcv[:, h].reshape(TOKENS, 128).astype(F32), off)
        if off + HEAD_DIM > 128:
            pieces = [(t, jnp.where(lane >= off, r, 0.0)), (t + 1, jnp.where(lane < off, r, 0.0))]
        else:
            pieces = [(t, r)]
        for at, piece in pieces:
            tiles[at] = piece if tiles[at] is None else tiles[at] + piece
    for t in range(GROUPS):
        att1[:, t * 128 : (t + 1) * 128] = tiles[t].astype(BF16)

    loads[8].wait()
    outrot = rotate(att1[...], bd.at[1]).astype(BF16)
    hidden = vid_mid[...].reshape(TOKENS, D).astype(F32) + dot(outrot, wso[...])
    hidden = hidden.astype(BF16).astype(F32)
    normed, inverse2 = normalize(hidden)
    normed2[...] = normed
    dproj_b[:, 0:D] = rotate(normed.astype(BF16), bd.at[2]).astype(BF16)
    loads[9].wait()

    def project2(c, carry):
        at = pl.ds(pl.multiple_of(c * D, 128), D)
        proj2[:, at] = dot(dproj_b[:, 0:D], wtp[:, at]).astype(BF16)
        return carry

    lax.fori_loop(0, 3, project2, 0)
    proj2[:, 3 * D :] = jnp.zeros((TOKENS, 128), BF16)

    square = (TOKENS, TOKENS)
    same_patch = lax.rem(rows(square), 16) == lax.rem(lanes(square), 16)
    same_frame = rows(square) // 16 == lanes(square) // 16
    key_valid = jnp.zeros(square, F32)
    for f in range(FRAMES):
        key_valid = jnp.where(lanes(square) // 16 == f, mask_ref[f].astype(F32), key_valid)
    allowed = jnp.logical_and(same_patch, jnp.logical_or(key_valid == 1.0, same_frame))
    bias = jnp.where(allowed, 0.0, NEGATIVE)

    dproj[...] = jnp.zeros_like(dproj)
    att2[...] = jnp.zeros_like(att2)
    lane4 = lanes((1, 256))
    for h in range(HEADS):
        t, off = (HEAD_DIM * h) // 128, (HEAD_DIM * h) % 128
        win = slice(t * 128, t * 128 + 256)
        kwin = slice(D + t * 128, D + t * 128 + 256)
        vwin = slice(2 * D + t * 128, 2 * D + t * 128 + 256)
        own = jnp.logical_and(lane4 >= off, lane4 < off + HEAD_DIM)
        own_f = jnp.where(own, 1.0, 0.0)
        own_b = own_f.astype(BF16)
        q = proj2[:, win] * own_b
        k = proj2[:, kwin]
        v = proj2[:, vwin]
        g = daz[:, win] * own_b
        scores = dot_nt(q, k) * SCALE + bias
        e = jnp.exp(scores - jnp.max(scores, axis=-1, keepdims=True))
        p = e / jnp.sum(e, axis=-1, keepdims=True)
        pb = p.astype(BF16)
        att2[:, win] += dot(pb, v) * own_f
        dproj[:, vwin] += dot_tn(pb, g)
        dp = dot_nt(g, v)
        ds = (p * (dp - jnp.sum(p * dp, axis=-1, keepdims=True))).astype(BF16)
        dproj[:, win] += dot(ds, k) * (own_f * SCALE)
        dproj[:, kwin] += dot_tn(ds, q) * SCALE

    dproj_b[...] = dproj[:, 0 : 3 * D].astype(BF16)
    hidp[...] = jnp.zeros_like(hidp)

    def back2(c, carry):
        at = pl.ds(pl.multiple_of(c * D, 128), D)
        hidp[...] += dot_nt(dproj_b[:, at], wtp[:, at])
        return carry

    lax.fori_loop(0, 3, back2, 0)
    adj_rot2 = hidp[...].astype(BF16)
    adj_normed = rotate_transposed(adj_rot2, bd.at[2])
    adj_hidden = top[...] + normalize_backward(adj_normed, normed2[...], inverse2)
    adj_hidden_b = adj_hidden.astype(BF16)
    ah_snd[...] = adj_hidden_b.reshape(FRAMES, 16, D)
    aho = dot_nt(adj_hidden_b, wso[...]).astype(BF16)
    adj_att1 = rotate_transposed(aho, bd.at[1])
    for h in range(HEADS):
        t, off = (HEAD_DIM * h) // 128, (HEAD_DIM * h) % 128
        first = group(adj_att1, t)
        if off + HEAD_DIM > 128:
            first = jnp.where(lane >= off, first, group(adj_att1, t + 1))
        piece = jnp.where(lane < 72, roll(first, -off), 0.0).astype(BF16)
        do_snd[:, h] = piece.reshape(FRAMES, 16, 128)

    def send_do(i, carry):
        there = lax.rem(me + i, DEVICES)
        zz, jj = there // PWAYS, lax.rem(there, PWAYS)
        push(
            do_snd.at[2 * zz + jj // HEADS, lax.rem(jj, HEADS)],
            do_rcv.at[pl.ds(pl.multiple_of((4 * j + z) * 16, 16), 16)],
            4, zz, jj,
        )
        return carry

    lax.fori_loop(0, DEVICES, send_do, 0)

    def send_ah(i, carry):
        zz = lax.rem(z + i, ZWAYS)
        for f in range(2):
            push(
                ah_snd.at[2 * zz + f],
                ah_rcv.at[f, pl.ds(pl.multiple_of(z * 16, 16), 16)],
                5, zz, j,
            )
        return carry

    lax.fori_loop(0, ZWAYS, send_ah, 0)

    for n, packed in enumerate((
        rotation_gradient(att1[...], aho),
        rotation_gradient(normed2[...].astype(BF16), adj_rot2),
        rotation_gradient(att2[:, 0:D].astype(BF16), aot[...]),
    )):
        for g in range(GROUPS):
            r1_snd[n * GROUPS + g] = packed[g].astype(BF16)

    def reduce_first(snd, rcv, owners, phase):
        def send(i, carry):
            jj = lax.rem(j + i, PWAYS)

            @pl.when(jj < owners)
            def _():
                push(snd.at[jj], rcv.at[j], phase, z, jj)

            return carry

        lax.fori_loop(0, PWAYS, send, 0)

    def reduce_second(snd, rcv, zbuf, owners, phase):
        @pl.when(j < owners)
        def _():
            wait_all(recv_sems.at[phase], rcv)
            zbuf[z] = jnp.sum(rcv[...].astype(F32), axis=0)

            def send(i, carry):
                zz = lax.rem(z + i, ZWAYS)
                pltpu.make_async_remote_copy(
                    src_ref=zbuf.at[z], dst_ref=zbuf.at[z], send_sem=send_sems.at[phase + 1],
                    recv_sem=recv_sems.at[phase + 1], device_id=(zz, j), device_id_type=MESH,
                ).start()
                return carry

            lax.fori_loop(1, ZWAYS, send, 0)

    def reduce_third(zbuf, chunk, out, owners, phase):
        @pl.when(j < owners)
        def _():
            wait_all(recv_sems.at[phase + 1], zbuf.at[pl.ds(0, ZWAYS - 1)])
            chunk[...] = (((zbuf[0] + zbuf[1]) + (zbuf[2] + zbuf[3])) / 128.0).astype(BF16)

            def send(i, carry):
                push(chunk, out.at[j], phase + 2, z, lax.rem(j + i, PWAYS))
                return carry

            lax.fori_loop(0, PWAYS, send, 0)

    def reduce_sent(snd, zbuf, out, owners, phase):
        @pl.when(j < owners)
        def _():
            wait_all(send_sems.at[phase], snd.at[pl.ds(0, owners - 1)])
            wait_all(send_sems.at[phase + 1], zbuf.at[pl.ds(0, ZWAYS - 1)])

            def one(i, carry):
                wait_all(send_sems.at[phase + 2], out.at[0])
                return carry

            lax.fori_loop(0, PWAYS - 1, one, 0)

        @pl.when(j >= owners)
        def _():
            wait_all(send_sems.at[phase], snd)

    reduce_first(r1_snd, r1_rcv, 27, 7)

    wait_all(recv_sems.at[4], do_rcv)

    def prepare_back(i, carry):
        at = pl.ds(pl.multiple_of(i * 256, 256), 256)
        lane2 = lanes((256, 128))
        g = do_rcv[at, :].astype(F32)
        delta = -jnp.sum(g * att_snd[at, :].astype(F32), axis=-1, keepdims=True)
        hi = delta.astype(BF16).astype(F32)
        lo = delta - hi
        dox[at, :] = jnp.where(lane2 == 72, hi, jnp.where(lane2 == 73, lo, g)).astype(BF16)
        dosh[at, 0:128] = jnp.zeros((256, 128), BF16)
        dosh[at, 128:256] = roll(g, 16).astype(BF16)
        return carry

    lax.fori_loop(0, 8, prepare_back, 0)
    dqt[...] = jnp.zeros_like(dqt)

    def attend_back(i, carry):
        at = pl.ds(pl.multiple_of(i * 256, 256), 256)
        p = jnp.exp2(dot_nt(kx[at, :], qx[...]))
        pb = p.astype(BF16)
        ds = (p * dot_nt(vx[at, :], dox[...])).astype(BF16)
        dkv[at, :] = dot(pb, dosh[...]) + dot(ds, qsh[...])
        dqt[...] += dot(kt[:, at], ds)
        return carry

    lax.fori_loop(0, 8, attend_back, 0)
    reduce_second(r1_snd, r1_rcv, r1_z, 27, 7)

    def finish_back(i, carry):
        at = pl.ds(pl.multiple_of(i * 256, 256), 256)
        lane2 = lanes((256, 128))
        dq = dqt[:, at].T * SCALE
        low = jnp.where(lane2 < 72, dq, dkv[at, 0:128] * LN2)
        high = jnp.where(lane2 < 16, dkv[at, 128:256] * LN2, dkv[at, 128:256])
        dq_snd[at, 0:128] = low.astype(BF16)
        dq_snd[at, 128:256] = high.astype(BF16)

        def send(s, c):
            jj = i * 4 + s
            push(
                dq_snd.at[pl.ds(pl.multiple_of(jj * 64, 64), 64)], dq_rcv.at[j], 6, z, jj
            )
            return c

        lax.fori_loop(0, 4, send, 0)
        return carry

    lax.fori_loop(0, 8, finish_back, 0)
    reduce_third(r1_z, r1_chunk, r1_out, 27, 7)

    wait_all(recv_sems.at[6], dq_rcv)
    tiles = [[None] * (GROUPS + 1) for _ in range(3)]
    for h in range(HEADS):
        t, off = (HEAD_DIM * h) // 128, (HEAD_DIM * h) % 128
        low = jnp.concatenate(
            [dq_rcv[h, :, 0:128], dq_rcv[HEADS + h, :, 0:128]], axis=0
        ).astype(F32)
        high = jnp.concatenate(
            [dq_rcv[h, :, 128:256], dq_rcv[HEADS + h, :, 128:256]], axis=0
        ).astype(F32)
        q = roll(jnp.where(lane < 72, low, 0.0), off)
        k = roll(jnp.where(lane >= 72, low, jnp.where(lane < 16, high, 0.0)), off - 72)
        v = roll(jnp.where(jnp.logical_and(lane >= 16, lane < 88), high, 0.0), off - 16)
        for section, r in enumerate((q, k, v)):
            if off + HEAD_DIM > 128:
                pieces = [
                    (t, jnp.where(lane >= off, r, 0.0)), (t + 1, jnp.where(lane < off, r, 0.0))
                ]
            else:
                pieces = [(t, r)]
            for at, piece in pieces:
                old = tiles[section][at]
                tiles[section][at] = piece if old is None else old + piece
    for section in range(3):
        for t in range(GROUPS):
            at = section * D + t * 128
            dproj_b[:, at : at + 128] = tiles[section][t].astype(BF16)

    hidp[...] = jnp.zeros_like(hidp)

    def back1(c, carry):
        at = pl.ds(pl.multiple_of(c * D, 128), D)
        hidp[...] += dot_nt(dproj_b[:, at], wsp[:, at])
        return carry

    lax.fori_loop(0, 3, back1, 0)
    adj_rot1 = hidp[...].astype(BF16)
    packed = rotation_gradient(normed1[...].astype(BF16), adj_rot1)
    for g in range(GROUPS):
        for s in range(2):
            r2_snd[2 * g + s] = packed[g][16 * s : 16 * (s + 1)].astype(BF16)
    reduce_first(r2_snd, r2_rcv, 18, 10)
    adj_normed = rotate_transposed(adj_rot1, bd.at[0])
    wait_all(recv_sems.at[5], ah_rcv)
    grad = ah_rcv[...].reshape(TOKENS, D).astype(F32) + normalize_backward(
        adj_normed, normed1[...], inverse1[...]
    )
    vg_ref[...] = grad.astype(BF16).reshape(2, 64, D)
    reduce_second(r2_snd, r2_rcv, r2_z, 18, 10)
    reduce_third(r2_z, r2_chunk, r2_out, 18, 10)

    wait_all(send_sems.at[0], vid_mid.at[pl.ds(0, 6)])
    wait_all(send_sems.at[1], ct_mid.at[pl.ds(0, 6)])
    wait_all(send_sems.at[2], qkv_snd.at[pl.ds(0, PWAYS - 1)])
    wait_all(send_sems.at[3], att_snd.at[pl.ds(0, PATCHES - 16)])
    wait_all(send_sems.at[4], do_rcv.at[pl.ds(0, PATCHES - 16)])
    wait_all(send_sems.at[5], ah_snd.at[pl.ds(0, 6)])
    wait_all(send_sems.at[6], dq_snd.at[pl.ds(0, PATCHES - 64)])
    reduce_sent(r1_snd, r1_z, r1_out, 27, 7)
    wait_all(recv_sems.at[9], r1_out)
    red_ref[0 : 3 * ROWS] = r1_out[...].reshape(3 * ROWS, 128).astype(F32)
    reduce_sent(r2_snd, r2_z, r2_out, 18, 10)
    wait_all(recv_sems.at[12], r2_out)
    red_ref[3 * ROWS :] = r2_out[...].reshape(ROWS, 128).astype(F32)


def per_device(
    video,
    cotangent,
    frame_mask,
    spatial_project,
    spatial_output,
    temporal_project,
    temporal_output,
    spatial_inward,
    spatial_outward,
    temporal_inward,
    temporal_outward,
):
    vm = pltpu.VMEM
    scratch = [
        vm((D, 3 * D), BF16), vm((D, D), BF16), vm((D, 3 * D), BF16), vm((D, D), BF16),
        vm((4, D, BLOCK), F32), vm((4, D, 128), BF16),
        vm((2, 64, D), BF16), vm((2, 64, D), BF16), vm((FRAMES, 16, D), BF16), vm((FRAMES, 16, D), BF16),
        vm((TOKENS, D), F32), vm((TOKENS, 1), F32), vm((TOKENS, 3 * D + 128), F32),
        vm((PWAYS, 64, 256), BF16), vm((PATCHES, 256), BF16), vm((PATCHES, 128), BF16), vm((PATCHES, 128), BF16),
        vm((PATCHES, 128), BF16), vm((FRAMES, HEADS, 16, 128), BF16), vm((TOKENS, D), BF16),
        vm((TOKENS, D), F32), vm((TOKENS, D), BF16), vm((TOKENS, D + 128), BF16),
        vm((TOKENS, D), F32), vm((TOKENS, D), F32), vm((TOKENS, 3 * D + 128), BF16),
        vm((TOKENS, 3 * D + 128), F32), vm((TOKENS, D + 128), F32), vm((TOKENS, 3 * D), BF16),
        vm((FRAMES, 16, D), BF16), vm((2, 64, D), BF16),
        vm((FRAMES, HEADS, 16, 128), BF16), vm((PATCHES, 128), BF16),
        vm((PATCHES, 128), BF16), vm((PATCHES, 128), BF16),
        vm((PATCHES, 256), BF16), vm((PATCHES, 256), BF16),
        vm((128, PATCHES), BF16), vm((128, PATCHES), F32), vm((PATCHES, 256), F32),
        vm((PATCHES, 256), BF16), vm((PWAYS, 64, 256), BF16),
        vm((27, 32, 128), BF16), vm((PWAYS, 32, 128), BF16), vm((ZWAYS, 32, 128), F32),
        vm((32, 128), BF16), vm((27, 32, 128), BF16),
        vm((18, 16, 128), BF16), vm((PWAYS, 16, 128), BF16), vm((ZWAYS, 16, 128), F32),
        vm((16, 128), BF16), vm((18, 16, 128), BF16),
        pltpu.SemaphoreType.DMA((10,)), pltpu.SemaphoreType.DMA((1,)),
        pltpu.SemaphoreType.DMA((13,)), pltpu.SemaphoreType.DMA((13,)),
    ]
    anyspec = pl.BlockSpec(memory_space=pl.ANY)
    grad, red = pl.pallas_call(
        kernel,
        out_shape=(
            jax.ShapeDtypeStruct((2, 64, D), BF16),
            jax.ShapeDtypeStruct((4 * ROWS, 128), F32),
        ),
        in_specs=[pl.BlockSpec(memory_space=pltpu.SMEM)] + [anyspec] * 10,
        out_specs=(pl.BlockSpec(memory_space=pltpu.VMEM), pl.BlockSpec(memory_space=pltpu.VMEM)),
        scratch_shapes=scratch,
        compiler_params=pltpu.CompilerParams(
            collective_id=0, has_side_effects=True, vmem_limit_bytes=60 * 1024 * 1024
        ),
        name="block_backward",
    )(
        frame_mask, video, cotangent, spatial_project, spatial_output, temporal_project, temporal_output,
        *(r.reshape(D, BLOCK) for r in (spatial_inward, spatial_outward, temporal_inward, temporal_outward)),
    )
    red = red.reshape(4, GROUPS, BLOCK, 4, BLOCK).transpose(0, 1, 3, 2, 4).reshape(4, 36, BLOCK, BLOCK)
    sout, tin, tout, sin = red[0], red[1], red[2], red[3]
    return grad, sin, sout, tin, tout


def solution(mesh):
    split = P("frame", "patch", None)
    in_specs = (split, split) + (P(),) * 9
    out_specs = (split,) + (P(),) * 4
    return jax.shard_map(
        per_device, mesh=mesh, in_specs=in_specs, out_specs=out_specs, check_vma=False
    )
```

```python
import itertools
import math

import jax
import jax.numpy as jnp
from jax import lax
from jax.experimental import pallas as pl
from jax.experimental.pallas import tpu as pltpu
from jax.sharding import PartitionSpec as P

D = 1152
HEADS = 16
HEAD_DIM = 72
BLOCK = 32
GROUPS = D // 128
FRAMES = 8
PATCHES = 2048
ZWAYS = 4
PWAYS = 32
DEVICES = ZWAYS * PWAYS
TOKENS = 128
ROWS = D // 4
NBLOCK = D // 32

EPSILON = 1e-06
NEGATIVE = -1e30
SCALE = 1.0 / math.sqrt(HEAD_DIM)
LOG2E = math.log2(math.e)
LN2 = math.log(2.0)

F32 = jnp.float32
BF16 = jnp.bfloat16
MESH = pl.DeviceIdType.MESH


def hops(step):
    return min(step[0], 4 - step[0]) + min(step[1], 4 - step[1]) + min(step[3], 4 - step[3])


PLANE = sorted(
    [s for s in itertools.product(range(4), range(4), range(2), [0]) if any(s)], key=lambda s: -hops(s)
)
SPACE = sorted(
    [s for s in itertools.product(range(4), range(4), range(2), range(4)) if any(s)],
    key=lambda s: -hops(s),
)
SLOTS = PLANE + [(0, 0, 0, 0)]
SLOT_OF = {s[:3]: n for n, s in enumerate(SLOTS)}


def dot(a, b):
    return lax.dot_general(a, b, (((1,), (0,)), ((), ())), preferred_element_type=F32)


def dot_nt(a, b):
    return lax.dot_general(a, b, (((1,), (1,)), ((), ())), preferred_element_type=F32)


def dot_tn(a, b):
    return lax.dot_general(a, b, (((0,), (0,)), ((), ())), preferred_element_type=F32)


def lanes(shape):
    return lax.broadcasted_iota(jnp.int32, shape, len(shape) - 1)


def rows(shape):
    return lax.broadcasted_iota(jnp.int32, shape, 0)


def roll(x, amount):
    amount = amount % 128
    return x if amount == 0 else pltpu.roll(x, amount, 1)


def normalize(x):
    centered = x - jnp.mean(x, axis=-1, keepdims=True)
    inverse = lax.rsqrt(jnp.mean(centered * centered, axis=-1, keepdims=True) + EPSILON)
    return centered * inverse, inverse


def normalize_backward(adjoint, normed, inverse):
    grad_mean = jnp.mean(adjoint, axis=-1, keepdims=True)
    grad_cross = jnp.mean(adjoint * normed, axis=-1, keepdims=True)
    return inverse * (adjoint - grad_mean - normed * grad_cross)


def group(x, g):
    return x[:, g * 128 : (g + 1) * 128]


def rotate(x, blocks):
    return jnp.concatenate(
        [dot(group(x, g), blocks[g * 128 : (g + 1) * 128, :]) for g in range(GROUPS)], axis=1
    )


def rotate_transposed(x, blocks):
    return jnp.concatenate(
        [dot_nt(group(x, g), blocks[g * 128 : (g + 1) * 128, :]) for g in range(GROUPS)], axis=1
    )


def block_mask(shape):
    return (rows(shape) // BLOCK) % 4 == lanes(shape) // BLOCK


def rotation_gradient(left, right):
    mask = block_mask((128, 128))
    packed = []
    for g in range(GROUPS):
        full = jnp.where(mask, dot_tn(group(left, g), group(right, g)), 0.0)
        packed.append(full[0:32] + full[32:64] + full[64:96] + full[96:128])
    return packed


def kernel(
    mask_ref, video, cotangent, wsp_h, wso_h, wtp_h, wto_h, rsi_h, rso_h, rti_h, rto_h,
    vg_ref, red_ref,
    wsp, wso, wtp, wto, r4, bd32, bd,
    vid, cot, vid_mid, ct_mid,
    normed1, inverse1, rot_b, proj,
    qkv_snd, qkv_rcv, kx, qx, vx,
    att_snd, att_rcv, att1, top, aot, daz,
    hidp, normed2, proj2, att2_b, dproj_b,
    t_s, t_dp, t_p, t_ds,
    ah_snd, ah_rcv, do_snd, do_rcv, dox, dosh, qsh, kt, dqt, pt,
    dkv_snd, dkv_rcv, dq_snd, dq_rcv, vg,
    r1_snd, r1_rcv, r1_z, r1_chunk, r1_out,
    r2_snd, r2_rcv, r2_z, r2_chunk, r2_out,
    load_sems, out_sems, send_sems, recv_sems, qkv_sems,
):
    z = lax.axis_index("frame")
    j = lax.axis_index("patch")
    px, py, pc = j >> 3, (j >> 1) & 3, j & 1
    xs = [((px + d) & 3) * 8 for d in range(4)]
    ys = [((py + d) & 3) * 2 for d in range(4)]
    cs = [(pc + d) & 1 for d in range(2)]
    zs = [(z + d) & 3 for d in range(4)]
    xys = [[a + b for b in ys] for a in xs]

    def ahead(step):
        return zs[step[3]], xys[step[0]][step[1]] + cs[step[2]]

    def behind(step):
        return zs[-step[3] & 3], xys[-step[0] & 3][-step[1] & 3] + cs[step[2]]

    def load(src, dst, n):
        return pltpu.make_async_copy(src, dst, load_sems.at[n])

    early = [load(video, vid, 0), load(rsi_h, r4.at[0], 1), load(wsp_h, wsp, 2)]
    late = [
        load(cotangent, cot, 3), load(rso_h, r4.at[1], 4), load(rti_h, r4.at[2], 5),
        load(rto_h, r4.at[3], 6), load(wto_h, wto, 7), load(wso_h, wso, 8), load(wtp_h, wtp, 9),
    ]
    for copy in early:
        copy.start()

    barrier = pltpu.get_barrier_semaphore()
    for step in SPACE:
        pl.semaphore_signal(barrier, inc=1, device_id=ahead(step), device_id_type=MESH)

    def local(src, dst, sem):
        pltpu.make_async_copy(src, dst, sem).start()

    def remote(src, dst, phase, there, recv_sem=None):
        pltpu.make_async_remote_copy(
            src_ref=src, dst_ref=dst, send_sem=send_sems.at[phase],
            recv_sem=recv_sems.at[phase] if recv_sem is None else recv_sem,
            device_id=there, device_id_type=MESH,
        ).start()

    def wait_all(sem, buffer):
        pltpu.make_async_copy(buffer, buffer, sem).wait()

    def make_blocks(index):
        shape = (128, 512)
        spread = jnp.where(
            jnp.logical_and(
                rows(shape) // BLOCK == lanes(shape) // 128, rows(shape) % BLOCK == lanes(shape) % BLOCK
            ),
            1.0, 0.0,
        ).astype(BF16)
        shape = (NBLOCK, 128)
        own = rows(shape) % 4 == lanes(shape) // BLOCK
        for m in range(8):
            four = r4[index, 4 * m : 4 * m + 4].reshape(128, NBLOCK).astype(BF16)
            wide = dot_tn(four, spread)
            for s in range(4):
                bd32[pl.ds(4 * m + s, NBLOCK, stride=BLOCK), :] = jnp.where(own, group(wide, s), 0.0)
        bd[index] = bd32[...].astype(BF16)

    early[0].wait()
    normed, inverse = normalize(vid[...].reshape(TOKENS, D).astype(F32))
    normed1[...] = normed
    inverse1[...] = inverse
    early[1].wait()
    make_blocks(0)
    rot_b[...] = rotate(normed1[...].astype(BF16), bd.at[0]).astype(BF16)

    early[2].wait()
    for copy in late:
        copy.start()

    def project1(c, carry):
        at = pl.ds(pl.multiple_of(c * D, 128), D)
        proj[:, at] = dot(rot_b[...], wsp[:, at])
        return carry

    lax.fori_loop(0, 3, project1, 0)

    lane = lanes((TOKENS, 128))
    qscale = jnp.where(lane < HEAD_DIM, SCALE * LOG2E, 1.0)
    for h in range(HEADS):
        t, off = (HEAD_DIM * h) // 128, (HEAD_DIM * h) % 128

        def pick(section, to):
            first = proj[:, section * D + t * 128 : section * D + (t + 1) * 128]
            if off + HEAD_DIM > 128:
                second = proj[:, section * D + (t + 1) * 128 : section * D + (t + 2) * 128]
                first = jnp.where(lane >= off, first, second)
            return roll(first, to - off)

        q, k, v = pick(0, 0), pick(1, 72), pick(2, 16)
        low = (jnp.where(lane < 72, q, k) * qscale).astype(BF16)
        high = jnp.where(lane < 16, k, jnp.where(lane < 88, v, 0.0)).astype(BF16)
        for f in range(2):
            qkv_snd[f * HEADS + h, :, 0:128] = low[64 * f : 64 * (f + 1)]
            qkv_snd[f * HEADS + h, :, 128:256] = high[64 * f : 64 * (f + 1)]

    pl.semaphore_wait(barrier, DEVICES - 1)

    for n, step in enumerate(SLOTS):
        dst = qkv_rcv.at[pl.ds(64 * n, 64)]
        if any(step):
            zz, jj = ahead(step)
            remote(qkv_snd.at[jj], dst, 2, (zz, jj), qkv_sems.at[n // 8])
        else:
            local(qkv_snd.at[j], dst, qkv_sems.at[n // 8])

    late[0].wait()
    for phase, src, dst in ((1, cot, ct_mid), (0, vid, vid_mid)):
        for d in (2, 1, 3, 0):
            for f in range(2):
                piece = src.at[f, pl.ds(pl.multiple_of(zs[d] * 16, 16), 16)]
                if d:
                    remote(piece, dst.at[2 * z + f], phase, (zs[d], j))
                else:
                    local(piece, dst.at[2 * z + f], recv_sems.at[phase])

    for n in (1, 2, 3):
        late[n].wait()
        make_blocks(n)

    wait_all(recv_sems.at[1], ct_mid)
    frame_row = rows((TOKENS, 1)) // 16
    valid = jnp.zeros((TOKENS, 1), F32)
    for f in range(FRAMES):
        valid = jnp.where(frame_row == f, mask_ref[f].astype(F32), valid)
    top[...] = ct_mid[...].reshape(TOKENS, D).astype(F32) * valid
    late[4].wait()
    aot[...] = dot_nt(top[...].astype(BF16), wto[...]).astype(BF16)
    daz[:, 0:D] = rotate_transposed(aot[...], bd.at[3]).astype(BF16)
    daz[:, D:] = jnp.zeros((TOKENS, 128), BF16)

    lane2 = lanes((256, 128))
    ones = jnp.where(jnp.logical_and(lane2 >= 72, lane2 < 76), 1.0, 0.0)

    def prepare(i, carry):
        at = pl.ds(pl.multiple_of(i * 256, 256), 256)
        t0, t1 = qkv_rcv[at, 0:128].astype(F32), qkv_rcv[at, 128:256].astype(F32)
        k = roll(jnp.where(lane2 >= 72, t0, t1), -72)
        kx[at, :] = jnp.where(lane2 < 72, k, ones).astype(BF16)
        vx[at, :] = jnp.where(lane2 < 72, roll(t1, -16), ones).astype(BF16)
        qx[at, :] = jnp.where(lane2 < 72, t0, 0.0).astype(BF16)
        return carry

    for g in range(4):
        wait_all(qkv_sems.at[g], qkv_rcv.at[pl.ds(512 * g, 512)])
        lax.fori_loop(2 * g, 2 * g + 2, prepare, 0)

    def attend(i, carry):
        spans = [pl.ds(pl.multiple_of(i * 512 + s * 256, 256), 256) for s in range(2)]
        outs = []
        for at in spans:
            scores = dot_nt(qx[at, :], kx[...])
            high_score = jnp.max(scores, axis=-1, keepdims=True)
            outs.append((high_score, dot(jnp.exp2(scores - high_score).astype(BF16), vx[...])))
        for at, (high_score, out) in zip(spans, outs):
            total = out[:, 72:73]
            att_snd[at, :] = jnp.where(lane2 < 72, out / total, 0.0).astype(BF16)
            neg = -(high_score + jnp.log(total) * LOG2E)
            hi = neg.astype(BF16).astype(F32)
            mid = (neg - hi).astype(BF16).astype(F32)
            lo = neg - hi - mid
            old = qx[at, :].astype(F32)
            new = jnp.where(
                lane2 == 72, hi, jnp.where(lane2 == 73, mid, jnp.where(lane2 == 74, lo, old))
            )
            qx[at, :] = new.astype(BF16)

        for ii in range(4):

            @pl.when(i == ii)
            def _():
                for n in range(8 * ii, 8 * ii + 8):
                    for d in (2, 1, 3, 0):
                        zz, jj = zs[d], behind(SLOTS[n])[1]
                        src = att_snd.at[pl.ds(pl.multiple_of(64 * n + 16 * zz, 16), 16)]
                        dst = att_rcv.at[2 * z + (j >> 4), j & 15]
                        if d or any(SLOTS[n]):
                            remote(src, dst, 3, (zz, jj))
                        else:
                            local(src, dst, recv_sems.at[3])

        return carry

    lax.fori_loop(0, 4, attend, 0)

    wait_all(recv_sems.at[0], vid_mid)
    wait_all(recv_sems.at[3], att_rcv)

    def add_piece(tiles, at, piece):
        tiles[at] = piece if tiles[at] is None else tiles[at] + piece

    def place(tiles, h, value):
        t, off = (HEAD_DIM * h) // 128, (HEAD_DIM * h) % 128
        if off + HEAD_DIM > 128:
            add_piece(tiles, t, jnp.where(lane >= off, value, 0.0))
            add_piece(tiles, t + 1, jnp.where(lane < off, value, 0.0))
        else:
            add_piece(tiles, t, value)

    tiles = [None] * GROUPS
    for h in range(HEADS):
        place(tiles, h, roll(att_rcv[:, h].reshape(TOKENS, 128).astype(F32), (HEAD_DIM * h) % 128))
    for t in range(GROUPS):
        att1[:, t * 128 : (t + 1) * 128] = tiles[t].astype(BF16)

    late[5].wait()
    outrot = rotate(att1[...], bd.at[1]).astype(BF16)
    hidden = vid_mid[...].reshape(TOKENS, D).astype(F32) + dot(outrot, wso[...])
    hidden = hidden.astype(BF16).astype(F32)
    normed, inverse2 = normalize(hidden)
    normed2[...] = normed
    rot_b[...] = rotate(normed.astype(BF16), bd.at[2]).astype(BF16)
    late[6].wait()

    def project2(c, carry):
        at = pl.ds(pl.multiple_of(c * D, 128), D)
        proj2[:, at] = dot(rot_b[...], wtp[:, at]).astype(BF16)
        return carry

    lax.fori_loop(0, 3, project2, 0)

    square = (TOKENS, TOKENS)
    same_patch = rows(square) % 16 == lanes(square) % 16
    same_frame = rows(square) // 16 == lanes(square) // 16
    key_valid = jnp.zeros(square, F32)
    for f in range(FRAMES):
        key_valid = jnp.where(rows(square) // 16 == f, mask_ref[f].astype(F32), key_valid)
    allowed = jnp.logical_and(same_patch, jnp.logical_or(key_valid == 1.0, same_frame))
    bias = jnp.where(allowed, 0.0, NEGATIVE)

    def window(h, section):
        t, off = (HEAD_DIM * h) // 128, (HEAD_DIM * h) % 128
        width = 256 if off + HEAD_DIM > 128 else 128
        return slice(section * D + t * 128, section * D + t * 128 + width)

    def own_lanes(h):
        off = (HEAD_DIM * h) % 128
        l = lanes((1, 256 if off + HEAD_DIM > 128 else 128))
        return jnp.where(jnp.logical_and(l >= off, l < off + HEAD_DIM), 1.0, 0.0)

    for h in range(HEADS):
        own = own_lanes(h).astype(BF16)
        t_s[h] = dot_nt(proj2[:, window(h, 1)], proj2[:, window(h, 0)] * own)
        t_dp[h] = dot_nt(proj2[:, window(h, 2)], daz[:, window(h, 0)] * own)

    for h in range(HEADS):
        scores = t_s[h] * SCALE + bias
        e = jnp.exp(scores - jnp.max(scores, axis=0, keepdims=True))
        p = e * (1.0 / jnp.sum(e, axis=0, keepdims=True))
        dp = t_dp[h]
        t_p[h] = p.astype(BF16)
        t_ds[h] = (p * (dp - jnp.sum(p * dp, axis=0, keepdims=True))).astype(BF16)

    def gather(section, dst, base):
        tiles = [None] * (GROUPS + 1)
        for h in range(HEADS):
            own = own_lanes(h)
            own_b = own.astype(BF16)
            if section == 0:
                part = dot_tn(t_ds[h], proj2[:, window(h, 1)]) * (own * SCALE)
            elif section == 1:
                part = dot(t_ds[h], proj2[:, window(h, 0)] * own_b) * SCALE
            elif section == 2:
                part = dot(t_p[h], daz[:, window(h, 0)] * own_b)
            else:
                part = dot_tn(t_p[h], proj2[:, window(h, 2)]) * own
            t = (HEAD_DIM * h) // 128
            for w in range(part.shape[1] // 128):
                add_piece(tiles, t + w, group(part, w))
        for t in range(GROUPS):
            dst[:, base + t * 128 : base + (t + 1) * 128] = tiles[t].astype(BF16)

    for section in range(3):
        gather(section, dproj_b, section * D)

    hidp[...] = jnp.zeros_like(hidp)

    def back2(c, carry):
        at = pl.ds(pl.multiple_of(c * D, 128), D)
        hidp[...] += dot_nt(dproj_b[:, at], wtp[:, at])
        return carry

    lax.fori_loop(0, 3, back2, 0)
    adj_rot2 = hidp[...].astype(BF16)
    adj_normed = rotate_transposed(adj_rot2, bd.at[2])
    adj_hidden = top[...] + normalize_backward(adj_normed, normed2[...], inverse2)
    adj_hidden_b = adj_hidden.astype(BF16)
    ah_snd[...] = adj_hidden_b.reshape(FRAMES, 16, D)
    aho = dot_nt(adj_hidden_b, wso[...]).astype(BF16)
    adj_att1 = rotate_transposed(aho, bd.at[1])
    for h in range(HEADS):
        t, off = (HEAD_DIM * h) // 128, (HEAD_DIM * h) % 128
        first = group(adj_att1, t)
        if off + HEAD_DIM > 128:
            first = jnp.where(lane >= off, first, group(adj_att1, t + 1))
        piece = jnp.where(lane < 72, roll(first, -off), 0.0).astype(BF16)
        do_snd[:, h] = piece.reshape(FRAMES, 16, 128)

    for step in SPACE + [(0, 0, 0, 0)]:
        zz, jj = ahead(step)
        src = do_snd.at[2 * zz + (jj >> 4), jj & 15]
        dst = do_rcv.at[pl.ds(pl.multiple_of(64 * SLOT_OF[step[:3]] + 16 * z, 16), 16)]
        if any(step):
            remote(src, dst, 4, (zz, jj))
        else:
            local(src, dst, recv_sems.at[4])
    for d in (2, 1, 3, 0):
        for f in range(2):
            src = ah_snd.at[2 * zs[d] + f]
            dst = ah_rcv.at[f, pl.ds(pl.multiple_of(z * 16, 16), 16)]
            if d:
                remote(src, dst, 5, (zs[d], j))
            else:
                local(src, dst, recv_sems.at[5])

    gather(3, att2_b, 0)
    for n, packed in enumerate((
        rotation_gradient(att1[...], aho),
        rotation_gradient(normed2[...].astype(BF16), adj_rot2),
        rotation_gradient(att2_b[...], aot[...]),
    )):
        for g in range(GROUPS):
            r1_snd[n * GROUPS + g] = packed[g].astype(BF16)

    def reduce_first(snd, rcv, chunk_of, owns, phase):
        for step in SLOTS:
            zz, jj = ahead(step)

            @pl.when(owns(jj))
            def _():
                if any(step):
                    remote(snd.at[chunk_of(jj)], rcv.at[j], phase, (zz, jj))
                else:
                    local(snd.at[chunk_of(jj)], rcv.at[j], recv_sems.at[phase])

    def reduce_second(rcv, zbuf, owns, phase):
        @pl.when(owns(j))
        def _():
            wait_all(recv_sems.at[phase], rcv)
            zbuf[z] = jnp.sum(rcv[...].astype(F32), axis=0)
            for d in (2, 1, 3):
                remote(zbuf.at[z], zbuf.at[z], phase + 1, (zs[d], j))

    def reduce_third(zbuf, chunk, out, chunk_of, owns, phase):
        size = chunk.shape[0]

        @pl.when(owns(j))
        def _():
            wait_all(recv_sems.at[phase + 1], zbuf.at[pl.ds(0, ZWAYS - 1)])
            chunk[...] = (((zbuf[0] + zbuf[1]) + (zbuf[2] + zbuf[3])) / 128.0).astype(BF16)
            dst = out.at[pl.ds(pl.multiple_of(chunk_of(j) * size, size), size)]
            for step in SLOTS:
                if any(step):
                    remote(chunk, dst, phase + 2, ahead(step))
                else:
                    local(chunk, dst, recv_sems.at[phase + 2])

    def reduce_sent(snd, rcv, zbuf, owners, owns, phase):
        @pl.when(owns(j))
        def _():
            wait_all(send_sems.at[phase], snd.at[pl.ds(0, owners - 1)])
            wait_all(send_sems.at[phase + 1], zbuf.at[pl.ds(0, ZWAYS - 1)])
            wait_all(send_sems.at[phase + 2], rcv.at[pl.ds(0, PWAYS - 1)])

        @pl.when(jnp.logical_not(owns(j)))
        def _():
            wait_all(send_sems.at[phase], snd)

    def chunk1(jj):
        return jj

    def owns1(jj):
        return jj < 27

    def chunk2(jj):
        return jnp.where((jj & 1) == 0, jj >> 1, 16 + (jj >> 4))

    def owns2(jj):
        return jnp.logical_or((jj & 1) == 0, (jj & 15) == 1)

    reduce_first(r1_snd, r1_rcv, chunk1, owns1, 7)

    def probabilities(i, carry):
        for s in range(2):
            at = pl.ds(pl.multiple_of(i * 512 + s * 256, 256), 256)
            pt[at, :] = jnp.exp2(dot_nt(kx[at, :], qx[...])).astype(BF16)
        return carry

    lax.fori_loop(0, 4, probabilities, 0)

    def prepare_keys(i, carry):
        at = pl.ds(pl.multiple_of(i * 256, 256), 256)
        kt[:, at] = kx[at, :].astype(F32).T.astype(BF16)
        qsh[at, :] = jnp.where(lane2 < 72, qx[at, :].astype(F32), 0.0).astype(BF16)
        return carry

    lax.fori_loop(0, 8, prepare_keys, 0)
    wait_all(recv_sems.at[4], do_rcv)

    def prepare_back(i, carry):
        at = pl.ds(pl.multiple_of(i * 256, 256), 256)
        g = do_rcv[at, :].astype(F32)
        delta = -jnp.sum(g * att_snd[at, :].astype(F32), axis=-1, keepdims=True)
        hi = delta.astype(BF16).astype(F32)
        lo = delta - hi
        dox[at, :] = jnp.where(lane2 == 72, hi, jnp.where(lane2 == 73, lo, g)).astype(BF16)
        g = roll(g, 72)
        dosh[at, 0:128] = jnp.where(lane2 >= 72, g, 0.0).astype(BF16)
        dosh[at, 128:256] = jnp.where(lane2 < 16, g, 0.0).astype(BF16)
        return carry

    lax.fori_loop(0, 8, prepare_back, 0)
    dqt[...] = jnp.zeros_like(dqt)

    def attend_back(i, carry):
        update = None
        for s in range(2):
            at = pl.ds(pl.multiple_of(i * 512 + s * 256, 256), 256)
            p = pt[at, :]
            ds = (p.astype(F32) * dot_nt(vx[at, :], dox[...])).astype(BF16)
            part = dot(kt[:, at], ds)
            update = part if update is None else update + part
            dv = dot(p, dosh[...])
            dk = dot(ds, qsh[...]) * LN2
            low = (dv[:, 0:128] + dk).astype(BF16)
            for m in range(4):
                tail = dv[64 * m : 64 * m + 8, 128:256]
                for e in range(1, 8):
                    tail = tail + roll(dv[64 * m + 8 * e : 64 * m + 8 * e + 8, 128:256], 16 * e)
                slot = i * 8 + s * 4 + m
                dkv_snd[slot, 0:64] = low[64 * m : 64 * m + 64]
                dkv_snd[slot, 64:80] = jnp.concatenate([tail, jnp.zeros_like(tail)], axis=0).astype(BF16)
        dqt[...] += update

        for ii in range(4):

            @pl.when(i == ii)
            def _():
                for n in range(8 * ii, 8 * ii + 8):
                    there = behind(SLOTS[n])
                    if any(SLOTS[n]):
                        remote(dkv_snd.at[n], dkv_rcv.at[j], 6, there)
                    else:
                        local(dkv_snd.at[n], dkv_rcv.at[j], recv_sems.at[6])

        return carry

    lax.fori_loop(0, 4, attend_back, 0)

    def finish_back(i, carry):
        at = pl.ds(pl.multiple_of(i * 512, 512), 512)
        dq_snd[at, :] = (dqt[:, at].T * SCALE).astype(BF16)
        for ii in range(4):

            @pl.when(i == ii)
            def _():
                for n in range(8 * ii, 8 * ii + 8):
                    there = behind(SLOTS[n])
                    src = dq_snd.at[pl.ds(64 * n, 64)]
                    if any(SLOTS[n]):
                        remote(src, dq_rcv.at[j], 13, there)
                    else:
                        local(src, dq_rcv.at[j], recv_sems.at[13])

        return carry

    lax.fori_loop(0, 4, finish_back, 0)
    reduce_second(r1_rcv, r1_z, owns1, 7)
    wait_all(recv_sems.at[6], dkv_rcv)

    def both(buffer, h, part):
        return jnp.concatenate([buffer[h, part], buffer[HEADS + h, part]], axis=0).astype(F32)

    tiles_k, tiles_v = [None] * GROUPS, [None] * GROUPS
    for h in range(HEADS):
        off = (HEAD_DIM * h) % 128
        low = both(dkv_rcv, h, slice(0, 64))
        tails = []
        for f in range(2):
            tail = dkv_rcv[f * HEADS + h, 64:80].astype(F32)[0:8]
            tails += [roll(tail, -16 * e) for e in range(8)]
        tail = jnp.concatenate(tails, axis=0)
        place(tiles_k, h, roll(jnp.where(lane < 72, low, 0.0), off))
        v = jnp.where(lane >= 72, low, jnp.where(lane < 16, tail, 0.0))
        place(tiles_v, h, roll(v, off - 72))
    for t in range(GROUPS):
        dproj_b[:, D + t * 128 : D + (t + 1) * 128] = tiles_k[t].astype(BF16)
        dproj_b[:, 2 * D + t * 128 : 2 * D + (t + 1) * 128] = tiles_v[t].astype(BF16)
    hidp[...] = jnp.zeros_like(hidp)

    def back1(c, carry):
        at = pl.ds(pl.multiple_of(c * D, 128), D)
        hidp[...] += dot_nt(dproj_b[:, at], wsp[:, at])
        return carry

    lax.fori_loop(1, 3, back1, 0)
    reduce_third(r1_z, r1_chunk, r1_out, chunk1, owns1, 7)
    wait_all(recv_sems.at[13], dq_rcv)
    tiles = [None] * GROUPS
    for h in range(HEADS):
        low = jnp.where(lane < 72, both(dq_rcv, h, slice(0, 64)), 0.0)
        place(tiles, h, roll(low, (HEAD_DIM * h) % 128))
    for t in range(GROUPS):
        dproj_b[:, t * 128 : (t + 1) * 128] = tiles[t].astype(BF16)
    lax.fori_loop(0, 1, back1, 0)
    adj_rot1 = hidp[...].astype(BF16)
    packed = rotation_gradient(normed1[...].astype(BF16), adj_rot1)
    for g in range(GROUPS):
        for s in range(2):
            r2_snd[2 * g + s] = packed[g][16 * s : 16 * (s + 1)].astype(BF16)
    reduce_first(r2_snd, r2_rcv, chunk2, owns2, 10)
    adj_normed = rotate_transposed(adj_rot1, bd.at[0])
    wait_all(recv_sems.at[5], ah_rcv)
    grad = ah_rcv[...].reshape(TOKENS, D).astype(F32) + normalize_backward(
        adj_normed, normed1[...], inverse1[...]
    )
    vg[...] = grad.astype(BF16).reshape(2, 64, D)
    vg_out = pltpu.make_async_copy(vg, vg_ref, out_sems.at[0])
    vg_out.start()
    reduce_second(r2_rcv, r2_z, owns2, 10)
    wait_all(send_sems.at[0], vid_mid.at[pl.ds(0, 6)])
    wait_all(send_sems.at[1], ct_mid.at[pl.ds(0, 6)])
    wait_all(send_sems.at[2], qkv_snd.at[pl.ds(0, PWAYS - 1)])
    wait_all(send_sems.at[3], att_snd.at[pl.ds(0, PATCHES - 16)])
    wait_all(send_sems.at[4], do_rcv.at[pl.ds(0, PATCHES - 16)])
    wait_all(send_sems.at[5], ah_snd.at[pl.ds(0, 6)])
    wait_all(send_sems.at[6], dkv_snd.at[pl.ds(0, PWAYS - 1)])
    wait_all(send_sems.at[13], dq_snd.at[pl.ds(0, PATCHES - 64)])
    wait_all(recv_sems.at[9], r1_out)
    red1 = pltpu.make_async_copy(r1_out, red_ref.at[pl.ds(0, 3 * ROWS)], out_sems.at[1])
    red1.start()
    reduce_third(r2_z, r2_chunk, r2_out, chunk2, owns2, 10)
    reduce_sent(r1_snd, r1_rcv, r1_z, 27, owns1, 7)
    reduce_sent(r2_snd, r2_rcv, r2_z, 18, owns2, 10)
    wait_all(recv_sems.at[12], r2_out)
    red2 = pltpu.make_async_copy(r2_out, red_ref.at[pl.ds(3 * ROWS, ROWS)], out_sems.at[2])
    red2.start()
    red1.wait()
    vg_out.wait()
    red2.wait()


def unpack_kernel(red, vg_in, vg_out, sout, tin, tout, sin, sem):
    copy = pltpu.make_async_copy(vg_in, vg_out, sem)
    copy.start()
    shape = (BLOCK, 40, ROWS)
    b = lax.broadcasted_iota(jnp.int32, shape, 0)
    n = lax.broadcasted_iota(jnp.int32, shape, 1)
    from_row = lax.broadcasted_iota(jnp.int32, shape, 2)
    pick = jnp.where(from_row == (n >> 2) * BLOCK + b, 1.0, 0.0).reshape(BLOCK * 40, ROWS).astype(BF16)
    shape = (BLOCK, 40, 128)
    n = lax.broadcasted_iota(jnp.int32, shape, 1)
    own = ((n & 3) == (lax.broadcasted_iota(jnp.int32, shape, 2) >> 5)).reshape(BLOCK * 40, 128)
    repeat = jnp.where(lanes((128, 128)) % BLOCK == rows((128, 128)) % BLOCK, 1.0, 0.0).astype(BF16)
    lane = lanes((40, 128)) >> 5
    for term, out in enumerate((sout, tin, tout, sin)):
        wide = dot(pick, red[term * ROWS : (term + 1) * ROWS, :])
        wide = dot(jnp.where(own, wide, 0.0).astype(BF16), repeat)
        for m in range(8):
            four = jnp.zeros((40, 128), F32)
            for s in range(4):
                at = (4 * m + s) * 40
                four = jnp.where(lane == s, wide[at : at + 40], four)
            out[4 * m : 4 * m + 4] = four.T[:, 0:NBLOCK].reshape(4, BLOCK, NBLOCK)
    copy.wait()


def per_device(
    video,
    cotangent,
    frame_mask,
    spatial_project,
    spatial_output,
    temporal_project,
    temporal_output,
    spatial_inward,
    spatial_outward,
    temporal_inward,
    temporal_outward,
):
    vm = pltpu.VMEM
    dma = pltpu.SemaphoreType.DMA
    scratch = [
        vm((D, 3 * D), BF16), vm((D, D), BF16), vm((D, 3 * D), BF16), vm((D, D), BF16),
        vm((4, BLOCK, BLOCK, NBLOCK), F32), vm((D, 128), F32), vm((4, D, 128), BF16),
        vm((2, 64, D), BF16), vm((2, 64, D), BF16), vm((FRAMES, 16, D), BF16), vm((FRAMES, 16, D), BF16),
        vm((TOKENS, D), F32), vm((TOKENS, 1), F32), vm((TOKENS, D), BF16), vm((TOKENS, 3 * D), F32),
        vm((PWAYS, 64, 256), BF16), vm((PATCHES, 256), BF16),
        vm((PATCHES, 128), BF16), vm((PATCHES, 128), BF16), vm((PATCHES, 128), BF16),
        vm((PATCHES, 128), BF16), vm((FRAMES, HEADS, 16, 128), BF16), vm((TOKENS, D), BF16),
        vm((TOKENS, D), F32), vm((TOKENS, D), BF16), vm((TOKENS, D + 128), BF16),
        vm((TOKENS, D), F32), vm((TOKENS, D), F32), vm((TOKENS, 3 * D), BF16),
        vm((TOKENS, D), BF16), vm((TOKENS, 3 * D), BF16),
        vm((HEADS, TOKENS, TOKENS), F32), vm((HEADS, TOKENS, TOKENS), F32),
        vm((HEADS, TOKENS, TOKENS), BF16), vm((HEADS, TOKENS, TOKENS), BF16),
        vm((FRAMES, 16, D), BF16), vm((2, 64, D), BF16),
        vm((FRAMES, HEADS, 16, 128), BF16), vm((PATCHES, 128), BF16),
        vm((PATCHES, 128), BF16), vm((PATCHES, 256), BF16), vm((PATCHES, 128), BF16),
        vm((128, PATCHES), BF16), vm((128, PATCHES), F32), vm((PATCHES, PATCHES), BF16),
        vm((PWAYS, 80, 128), BF16), vm((PWAYS, 80, 128), BF16),
        vm((PATCHES, 128), BF16), vm((PWAYS, 64, 128), BF16), vm((2, 64, D), BF16),
        vm((27, 32, 128), BF16), vm((PWAYS, 32, 128), BF16), vm((ZWAYS, 32, 128), F32),
        vm((32, 128), BF16), vm((3 * ROWS, 128), BF16),
        vm((18, 16, 128), BF16), vm((PWAYS, 16, 128), BF16), vm((ZWAYS, 16, 128), F32),
        vm((16, 128), BF16), vm((ROWS, 128), BF16),
        dma((10,)), dma((3,)), dma((14,)), dma((14,)), dma((4,)),
    ]
    anyspec = pl.BlockSpec(memory_space=pl.ANY)
    vspec = pl.BlockSpec(memory_space=pltpu.VMEM)
    blocks = [r.transpose(1, 2, 0) for r in (spatial_inward, spatial_outward, temporal_inward, temporal_outward)]
    grad, red = pl.pallas_call(
        kernel,
        out_shape=(
            jax.ShapeDtypeStruct((2, 64, D), BF16),
            jax.ShapeDtypeStruct((4 * ROWS, 128), BF16),
        ),
        in_specs=[pl.BlockSpec(memory_space=pltpu.SMEM)] + [anyspec] * 10,
        out_specs=(anyspec, anyspec),
        scratch_shapes=scratch,
        compiler_params=pltpu.CompilerParams(
            collective_id=0, has_side_effects=True, vmem_limit_bytes=62 * 1024 * 1024
        ),
        name="block_backward",
    )(
        frame_mask, video, cotangent, spatial_project, spatial_output, temporal_project, temporal_output,
        *blocks,
    )
    term = jax.ShapeDtypeStruct((BLOCK, BLOCK, NBLOCK), F32)
    grad, sout, tin, tout, sin = pl.pallas_call(
        unpack_kernel,
        out_shape=(jax.ShapeDtypeStruct((2, 64, D), BF16), term, term, term, term),
        in_specs=[vspec, anyspec],
        out_specs=(anyspec, vspec, vspec, vspec, vspec),
        scratch_shapes=[dma],
        compiler_params=pltpu.CompilerParams(vmem_limit_bytes=32 * 1024 * 1024),
        name="unpack_terms",
    )(red, grad)
    sin, sout, tin, tout = (r.transpose(2, 0, 1) for r in (sin, sout, tin, tout))
    return grad, sin, sout, tin, tout


def solution(mesh):
    split = P("frame", "patch", None)
    in_specs = (split, split) + (P(),) * 9
    out_specs = (split,) + (P(),) * 4
    return jax.shard_map(
        per_device, mesh=mesh, in_specs=in_specs, out_specs=out_specs, check_vma=False
    )
```

```python
import itertools
import math

import jax
import jax.numpy as jnp
from jax import lax
from jax.experimental import pallas as pl
from jax.experimental.pallas import tpu as pltpu
from jax.sharding import PartitionSpec as P

D = 1152
HEADS = 16
HEAD_DIM = 72
BLOCK = 32
GROUPS = D // 128
FRAMES = 8
PATCHES = 2048
ZWAYS = 4
PWAYS = 32
DEVICES = ZWAYS * PWAYS
TOKENS = 128
ROWS = D // 4
NBLOCK = D // 32

EPSILON = 1e-06
NEGATIVE = -1e30
SCALE = 1.0 / math.sqrt(HEAD_DIM)
LOG2E = math.log2(math.e)
LN2 = math.log(2.0)

F32 = jnp.float32
BF16 = jnp.bfloat16
MESH = pl.DeviceIdType.MESH


def hops(step):
    return min(step[0], 4 - step[0]) + min(step[1], 4 - step[1]) + min(step[3], 4 - step[3])


PLANE = sorted(
    [s for s in itertools.product(range(4), range(4), range(2), [0]) if any(s)], key=lambda s: -hops(s)
)
SPACE = sorted(
    [s for s in itertools.product(range(4), range(4), range(2), range(4)) if any(s)],
    key=lambda s: -hops(s),
)
SLOTS = PLANE + [(0, 0, 0, 0)]
SLOT_OF = {s[:3]: n for n, s in enumerate(SLOTS)}


def dot(a, b):
    return lax.dot_general(a, b, (((1,), (0,)), ((), ())), preferred_element_type=F32)


def dot_nt(a, b):
    return lax.dot_general(a, b, (((1,), (1,)), ((), ())), preferred_element_type=F32)


def dot_tn(a, b):
    return lax.dot_general(a, b, (((0,), (0,)), ((), ())), preferred_element_type=F32)


def lanes(shape):
    return lax.broadcasted_iota(jnp.int32, shape, len(shape) - 1)


def rows(shape):
    return lax.broadcasted_iota(jnp.int32, shape, 0)


def roll(x, amount):
    amount = amount % 128
    return x if amount == 0 else pltpu.roll(x, amount, 1)


def normalize(x):
    centered = x - jnp.mean(x, axis=-1, keepdims=True)
    inverse = lax.rsqrt(jnp.mean(centered * centered, axis=-1, keepdims=True) + EPSILON)
    return centered * inverse, inverse


def normalize_backward(adjoint, normed, inverse):
    grad_mean = jnp.mean(adjoint, axis=-1, keepdims=True)
    grad_cross = jnp.mean(adjoint * normed, axis=-1, keepdims=True)
    return inverse * (adjoint - grad_mean - normed * grad_cross)


def group(x, g):
    return x[:, g * 128 : (g + 1) * 128]


def rotate(x, blocks):
    return jnp.concatenate(
        [dot(group(x, g), blocks[g * 128 : (g + 1) * 128, :]) for g in range(GROUPS)], axis=1
    )


def rotate_transposed(x, blocks):
    return jnp.concatenate(
        [dot_nt(group(x, g), blocks[g * 128 : (g + 1) * 128, :]) for g in range(GROUPS)], axis=1
    )


def block_mask(shape):
    return (rows(shape) // BLOCK) % 4 == lanes(shape) // BLOCK


def rotation_gradient(left, right):
    mask = block_mask((128, 128))
    packed = []
    for g in range(GROUPS):
        full = jnp.where(mask, dot_tn(group(left, g), group(right, g)), 0.0)
        packed.append(full[0:32] + full[32:64] + full[64:96] + full[96:128])
    return packed


def kernel(
    mask_ref, video, cotangent, wsp_h, wso_h, wtp_h, wto_h, rsi_h, rso_h, rti_h, rto_h,
    vg_ref, red_ref,
    wsp, wso, wtp, wto, r4, bd32, bd,
    vid, cot, vid_mid, ct_mid,
    normed1, inverse1, rot_b, proj,
    qkv_snd, qkv_rcv, kx, qx, vx,
    att_snd, att_rcv, att1, top, aot, daz,
    hidp, normed2, proj2, att2_b, dproj_b,
    t_s, t_dp, t_p, t_ds,
    ah_snd, ah_rcv, do_snd, do_rcv, qt, dkt, dvt, pq,
    dkv_snd, dkv_rcv, dq_snd, dq_rcv, vg,
    r1_snd, r1_rcv, r1_z, r1_chunk, r1_out,
    r2_snd, r2_rcv, r2_z, r2_chunk,
    load_sems, out_sems, send_sems, recv_sems, qkv_sems, do_sems,
):
    z = lax.axis_index("frame")
    j = lax.axis_index("patch")
    px, py, pc = j >> 3, (j >> 1) & 3, j & 1
    xs = [((px + d) & 3) * 8 for d in range(4)]
    ys = [((py + d) & 3) * 2 for d in range(4)]
    cs = [(pc + d) & 1 for d in range(2)]
    zs = [(z + d) & 3 for d in range(4)]
    xys = [[a + b for b in ys] for a in xs]

    def ahead(step):
        return zs[step[3]], xys[step[0]][step[1]] + cs[step[2]]

    def behind(step):
        return zs[-step[3] & 3], xys[-step[0] & 3][-step[1] & 3] + cs[step[2]]

    def load(src, dst, n):
        return pltpu.make_async_copy(src, dst, load_sems.at[n])

    early = [load(video, vid, 0), load(rsi_h, r4.at[0], 1)]
    early += [
        load(wsp_h.at[:, pl.ds(c * D, D)], wsp.at[:, pl.ds(c * D, D)], n) for c, n in enumerate((2, 10, 11))
    ]
    late = [
        load(cotangent, cot, 3), load(rso_h, r4.at[1], 4), load(rti_h, r4.at[2], 5),
        load(rto_h, r4.at[3], 6), load(wto_h, wto, 7), load(wso_h, wso, 8), load(wtp_h, wtp, 9),
    ]
    for copy in early:
        copy.start()

    barrier = pltpu.get_barrier_semaphore()
    near = PLANE + [(0, 0, 0, d) for d in (2, 1, 3)]
    for step in near:
        pl.semaphore_signal(barrier, inc=1, device_id=ahead(step), device_id_type=MESH)

    def local(src, dst, sem):
        pltpu.make_async_copy(src, dst, sem).start()

    def remote(src, dst, phase, there, recv_sem=None):
        pltpu.make_async_remote_copy(
            src_ref=src, dst_ref=dst, send_sem=send_sems.at[phase],
            recv_sem=recv_sems.at[phase] if recv_sem is None else recv_sem,
            device_id=there, device_id_type=MESH,
        ).start()

    def wait_all(sem, buffer):
        pltpu.make_async_copy(buffer, buffer, sem).wait()

    def make_blocks(index):
        shape = (128, 512)
        spread = jnp.where(
            jnp.logical_and(
                rows(shape) // BLOCK == lanes(shape) // 128, rows(shape) % BLOCK == lanes(shape) % BLOCK
            ),
            1.0, 0.0,
        ).astype(BF16)
        shape = (NBLOCK, 128)
        own = rows(shape) % 4 == lanes(shape) // BLOCK
        for m in range(8):
            four = r4[index, 4 * m : 4 * m + 4].reshape(128, NBLOCK).astype(BF16)
            wide = dot_tn(four, spread)
            for s in range(4):
                bd32[pl.ds(4 * m + s, NBLOCK, stride=BLOCK), :] = jnp.where(own, group(wide, s), 0.0)
        bd[index] = bd32[...].astype(BF16)

    early[0].wait()
    normed, inverse = normalize(vid[...].reshape(TOKENS, D).astype(F32))
    normed1[...] = normed
    inverse1[...] = inverse
    early[1].wait()
    make_blocks(0)
    rot_b[...] = rotate(normed1[...].astype(BF16), bd.at[0]).astype(BF16)

    for c in range(3):
        at = slice(c * D, (c + 1) * D)
        early[2 + c].wait()
        proj[:, at] = dot(rot_b[...], wsp[:, at])
    for copy in late:
        copy.start()

    lane = lanes((TOKENS, 128))
    qscale = jnp.where(lane < HEAD_DIM, SCALE * LOG2E, 1.0)
    for h in range(HEADS):
        t, off = (HEAD_DIM * h) // 128, (HEAD_DIM * h) % 128

        def pick(section, to):
            first = proj[:, section * D + t * 128 : section * D + (t + 1) * 128]
            if off + HEAD_DIM > 128:
                second = proj[:, section * D + (t + 1) * 128 : section * D + (t + 2) * 128]
                first = jnp.where(lane >= off, first, second)
            return roll(first, to - off)

        q, k, v = pick(0, 0), pick(1, 72), pick(2, 16)
        low = (jnp.where(lane < 72, q, k) * qscale).astype(BF16)
        high = jnp.where(lane < 16, k, jnp.where(lane < 88, v, 0.0)).astype(BF16)
        for f in range(2):
            qkv_snd[f * HEADS + h, :, 0:128] = low[64 * f : 64 * (f + 1)]
            qkv_snd[f * HEADS + h, :, 128:256] = high[64 * f : 64 * (f + 1)]

    pl.semaphore_wait(barrier, len(near))

    for n, step in enumerate(SLOTS):
        dst = qkv_rcv.at[pl.ds(64 * n, 64)]
        if any(step):
            zz, jj = ahead(step)
            remote(qkv_snd.at[jj], dst, 2, (zz, jj), qkv_sems.at[n // 8])
        else:
            local(qkv_snd.at[j], dst, qkv_sems.at[n // 8])

    late[0].wait()
    for phase, src, dst in ((1, cot, ct_mid), (0, vid, vid_mid)):
        for d in (2, 1, 3, 0):
            for f in range(2):
                piece = src.at[f, pl.ds(pl.multiple_of(zs[d] * 16, 16), 16)]
                if d:
                    remote(piece, dst.at[2 * z + f], phase, (zs[d], j))
                else:
                    local(piece, dst.at[2 * z + f], recv_sems.at[phase])

    for n in (1, 2, 3):
        late[n].wait()
        make_blocks(n)

    wait_all(recv_sems.at[1], ct_mid)
    frame_row = rows((TOKENS, 1)) // 16
    valid = jnp.zeros((TOKENS, 1), F32)
    for f in range(FRAMES):
        valid = jnp.where(frame_row == f, mask_ref[f].astype(F32), valid)
    top[...] = ct_mid[...].reshape(TOKENS, D).astype(F32) * valid
    late[4].wait()
    aot[...] = dot_nt(top[...].astype(BF16), wto[...]).astype(BF16)
    daz[:, 0:D] = rotate_transposed(aot[...], bd.at[3]).astype(BF16)
    daz[:, D:] = jnp.zeros((TOKENS, 128), BF16)

    lane2 = lanes((256, 128))
    ones = jnp.where(jnp.logical_and(lane2 >= 72, lane2 < 76), 1.0, 0.0)

    def prepare(i, carry):
        at = pl.ds(pl.multiple_of(i * 256, 256), 256)
        t0, t1 = qkv_rcv[at, 0:128].astype(F32), qkv_rcv[at, 128:256].astype(F32)
        k = roll(jnp.where(lane2 >= 72, t0, t1), -72)
        kx[at, :] = jnp.where(lane2 < 72, k, ones).astype(BF16)
        vx[at, :] = jnp.where(lane2 < 72, roll(t1, -16), ones).astype(BF16)
        qx[at, :] = jnp.where(lane2 < 72, t0, 0.0).astype(BF16)
        return carry

    for g in range(4):
        wait_all(qkv_sems.at[g], qkv_rcv.at[pl.ds(512 * g, 512)])
        lax.fori_loop(2 * g, 2 * g + 2, prepare, 0)

    def attend(i, carry):
        spans = [pl.ds(pl.multiple_of(i * 512 + s * 256, 256), 256) for s in range(2)]
        highs = []
        for s, at in enumerate(spans):
            scores = dot_nt(qx[at, :], kx[...])
            highs.append(jnp.max(scores, axis=-1, keepdims=True))
            pq[256 * s : 256 * s + 256, :] = jnp.exp2(scores - highs[-1]).astype(BF16)
        both_out = dot(pq[0:512, :], vx[...])
        for s, (at, high_score) in enumerate(zip(spans, highs)):
            out = both_out[256 * s : 256 * s + 256]
            total = out[:, 72:73]
            att_snd[at, :] = jnp.where(lane2 < 72, out / total, 0.0).astype(BF16)
            neg = -(high_score + jnp.log(total) * LOG2E)
            hi = neg.astype(BF16).astype(F32)
            mid = (neg - hi).astype(BF16).astype(F32)
            lo = neg - hi - mid
            old = qx[at, :].astype(F32)
            new = jnp.where(
                lane2 == 72, hi, jnp.where(lane2 == 73, mid, jnp.where(lane2 == 74, lo, old))
            )
            qx[at, :] = new.astype(BF16)

        for ii in range(4):

            @pl.when(i == ii)
            def _():
                for n in range(8 * ii, 8 * ii + 8):
                    for d in (2, 1, 3, 0):
                        zz, jj = zs[d], behind(SLOTS[n])[1]
                        src = att_snd.at[pl.ds(pl.multiple_of(64 * n + 16 * zz, 16), 16)]
                        dst = att_rcv.at[2 * z + (j >> 4), j & 15]
                        if d or any(SLOTS[n]):
                            remote(src, dst, 3, (zz, jj))
                        else:
                            local(src, dst, recv_sems.at[3])

        return carry

    lax.fori_loop(0, 4, attend, 0)

    wait_all(recv_sems.at[0], vid_mid)
    wait_all(recv_sems.at[3], att_rcv)

    def add_piece(tiles, at, piece):
        tiles[at] = piece if tiles[at] is None else tiles[at] + piece

    def place(tiles, h, value):
        t, off = (HEAD_DIM * h) // 128, (HEAD_DIM * h) % 128
        if off + HEAD_DIM > 128:
            add_piece(tiles, t, jnp.where(lane >= off, value, 0.0))
            add_piece(tiles, t + 1, jnp.where(lane < off, value, 0.0))
        else:
            add_piece(tiles, t, value)

    tiles = [None] * GROUPS
    for h in range(HEADS):
        place(tiles, h, roll(att_rcv[:, h].reshape(TOKENS, 128).astype(F32), (HEAD_DIM * h) % 128))
    for t in range(GROUPS):
        att1[:, t * 128 : (t + 1) * 128] = tiles[t].astype(BF16)

    late[5].wait()
    outrot = rotate(att1[...], bd.at[1]).astype(BF16)
    hidden = vid_mid[...].reshape(TOKENS, D).astype(F32) + dot(outrot, wso[...])
    hidden = hidden.astype(BF16).astype(F32)
    normed, inverse2 = normalize(hidden)
    normed2[...] = normed
    rot_b[...] = rotate(normed.astype(BF16), bd.at[2]).astype(BF16)
    late[6].wait()

    def project2(c, carry):
        at = pl.ds(pl.multiple_of(c * D, 128), D)
        proj2[:, at] = dot(rot_b[...], wtp[:, at]).astype(BF16)
        return carry

    lax.fori_loop(0, 3, project2, 0)

    square = (TOKENS, TOKENS)
    same_patch = rows(square) % 16 == lanes(square) % 16
    same_frame = rows(square) // 16 == lanes(square) // 16
    key_valid = jnp.zeros(square, F32)
    for f in range(FRAMES):
        key_valid = jnp.where(rows(square) // 16 == f, mask_ref[f].astype(F32), key_valid)
    allowed = jnp.logical_and(same_patch, jnp.logical_or(key_valid == 1.0, same_frame))
    bias = jnp.where(allowed, 0.0, NEGATIVE)

    def window(h, section):
        t, off = (HEAD_DIM * h) // 128, (HEAD_DIM * h) % 128
        width = 256 if off + HEAD_DIM > 128 else 128
        return slice(section * D + t * 128, section * D + t * 128 + width)

    def own_lanes(h):
        off = (HEAD_DIM * h) % 128
        l = lanes((1, 256 if off + HEAD_DIM > 128 else 128))
        return jnp.where(jnp.logical_and(l >= off, l < off + HEAD_DIM), 1.0, 0.0)

    for h in range(HEADS):
        own = own_lanes(h).astype(BF16)
        t_s[h] = dot_nt(proj2[:, window(h, 1)], proj2[:, window(h, 0)] * own)
        t_dp[h] = dot_nt(proj2[:, window(h, 2)], daz[:, window(h, 0)] * own)

    for h in range(HEADS):
        scores = t_s[h] * SCALE + bias
        e = jnp.exp(scores - jnp.max(scores, axis=0, keepdims=True))
        p = e * (1.0 / jnp.sum(e, axis=0, keepdims=True))
        dp = t_dp[h]
        t_p[h] = p.astype(BF16)
        t_ds[h] = (p * (dp - jnp.sum(p * dp, axis=0, keepdims=True))).astype(BF16)

    def gather(section, dst, base):
        tiles = [None] * (GROUPS + 1)
        for h in range(HEADS):
            own = own_lanes(h)
            own_b = own.astype(BF16)
            if section == 0:
                part = dot_tn(t_ds[h], proj2[:, window(h, 1)]) * (own * SCALE)
            elif section == 1:
                part = dot(t_ds[h], proj2[:, window(h, 0)] * own_b) * SCALE
            elif section == 2:
                part = dot(t_p[h], daz[:, window(h, 0)] * own_b)
            else:
                part = dot_tn(t_p[h], proj2[:, window(h, 2)]) * own
            t = (HEAD_DIM * h) // 128
            for w in range(part.shape[1] // 128):
                add_piece(tiles, t + w, group(part, w))
        for t in range(GROUPS):
            dst[:, base + t * 128 : base + (t + 1) * 128] = tiles[t].astype(BF16)

    for section in range(3):
        gather(section, dproj_b, section * D)

    for c in range(3):
        at = slice(c * 384, (c + 1) * 384)
        hidp[:, at] = dot_nt(dproj_b[...], wtp[at, :])
    adj_rot2 = hidp[...].astype(BF16)
    adj_normed = rotate_transposed(adj_rot2, bd.at[2])
    adj_hidden = top[...] + normalize_backward(adj_normed, normed2[...], inverse2)
    adj_hidden_b = adj_hidden.astype(BF16)
    ah_snd[...] = adj_hidden_b.reshape(FRAMES, 16, D)
    aho = dot_nt(adj_hidden_b, wso[...]).astype(BF16)
    adj_att1 = rotate_transposed(aho, bd.at[1])
    for h in range(HEADS):
        t, off = (HEAD_DIM * h) // 128, (HEAD_DIM * h) % 128
        first = group(adj_att1, t)
        if off + HEAD_DIM > 128:
            first = jnp.where(lane >= off, first, group(adj_att1, t + 1))
        piece = jnp.where(lane < 72, roll(first, -off), 0.0).astype(BF16)
        do_snd[:, h] = piece.reshape(FRAMES, 16, 128)

    for step in SPACE + [(0, 0, 0, 0)]:
        zz, jj = ahead(step)
        src = do_snd.at[2 * zz + (jj >> 4), jj & 15]
        n = SLOT_OF[step[:3]]
        dst = do_rcv.at[pl.ds(pl.multiple_of(64 * n + 16 * z, 16), 16)]
        if any(step):
            remote(src, dst, 4, (zz, jj), do_sems.at[n // 8])
        else:
            local(src, dst, do_sems.at[n // 8])
    for d in (2, 1, 3, 0):
        for f in range(2):
            src = ah_snd.at[2 * zs[d] + f]
            dst = ah_rcv.at[f, pl.ds(pl.multiple_of(z * 16, 16), 16)]
            if d:
                remote(src, dst, 5, (zs[d], j))
            else:
                local(src, dst, recv_sems.at[5])

    gather(3, att2_b, 0)
    for n, packed in enumerate((
        rotation_gradient(att1[...], aho),
        rotation_gradient(normed2[...].astype(BF16), adj_rot2),
        rotation_gradient(att2_b[...], aot[...]),
    )):
        for g in range(GROUPS):
            r1_snd[n * GROUPS + g] = packed[g].astype(BF16)

    def reduce_first(snd, rcv, chunk_of, owns, phase):
        for step in SLOTS:
            zz, jj = ahead(step)

            @pl.when(owns(jj))
            def _():
                if any(step):
                    remote(snd.at[chunk_of(jj)], rcv.at[j], phase, (zz, jj))
                else:
                    local(snd.at[chunk_of(jj)], rcv.at[j], recv_sems.at[phase])

    def reduce_second(rcv, zbuf, owns, phase):
        @pl.when(owns(j))
        def _():
            wait_all(recv_sems.at[phase], rcv)
            zbuf[z] = jnp.sum(rcv[...].astype(F32), axis=0)
            for d in (2, 1, 3):
                remote(zbuf.at[z], zbuf.at[z], phase + 1, (zs[d], j))

    def reduce_third(zbuf, chunk, out, chunk_of, owns, phase):
        size = chunk.shape[0]

        @pl.when(owns(j))
        def _():
            wait_all(recv_sems.at[phase + 1], zbuf.at[pl.ds(0, ZWAYS - 1)])
            chunk[...] = (((zbuf[0] + zbuf[1]) + (zbuf[2] + zbuf[3])) / 128.0).astype(BF16)
            dst = out.at[pl.ds(pl.multiple_of(chunk_of(j) * size, size), size)]
            for step in SLOTS:
                if any(step):
                    remote(chunk, dst, phase + 2, ahead(step))
                else:
                    local(chunk, dst, recv_sems.at[phase + 2])

    def reduce_sent(snd, rcv, zbuf, owners, owns, phase):
        @pl.when(owns(j))
        def _():
            wait_all(send_sems.at[phase], snd.at[pl.ds(0, owners - 1)])
            wait_all(send_sems.at[phase + 1], zbuf.at[pl.ds(0, ZWAYS - 1)])
            wait_all(send_sems.at[phase + 2], rcv.at[pl.ds(0, PWAYS - 1)])

        @pl.when(jnp.logical_not(owns(j)))
        def _():
            wait_all(send_sems.at[phase], snd)

    def chunk1(jj):
        return jj

    def owns1(jj):
        return jj < 27

    reduce_first(r1_snd, r1_rcv, chunk1, owns1, 7)

    def probabilities(i, carry):
        for s in range(2):
            at = pl.ds(pl.multiple_of(i * 512 + s * 256, 256), 256)
            pq[at, :] = jnp.exp2(dot_nt(qx[at, :], kx[...])).astype(BF16)
        return carry

    lax.fori_loop(0, 4, probabilities, 0)

    def prepare_queries(i, carry):
        at = pl.ds(pl.multiple_of(i * 256, 256), 256)
        qt[:, at] = qx[at, :].astype(F32).T[0:80].astype(BF16)
        return carry

    lax.fori_loop(0, 8, prepare_queries, 0)

    def attend_back(group_, first):
        at = pl.ds(group_ * 512, 512)
        lane5 = lanes((512, 128))
        g = do_rcv[at, :].astype(F32)
        delta = -jnp.sum(g * att_snd[at, :].astype(F32), axis=-1, keepdims=True)
        hi = delta.astype(BF16).astype(F32)
        lo = delta - hi
        dox = jnp.where(lane5 == 72, hi, jnp.where(lane5 == 73, lo, g)).astype(BF16)
        p = pq[at, :]
        dv = dot(g.T[0:80].astype(BF16), p)
        ds = (p.astype(F32) * dot_nt(dox, vx[...])).astype(BF16)
        dq = dot(ds, kx[...]) * SCALE
        dq_snd[at, :] = jnp.where(lane5 < 72, dq, 0.0).astype(BF16)
        dk = dot(qt[:, at], ds)
        if first:
            dkt[...] = dk
            dvt[...] = dv
        else:
            dkt[...] += dk
            dvt[...] += dv
        for n in range(8 * group_, 8 * group_ + 8):
            src = dq_snd.at[pl.ds(64 * n, 64)]
            if any(SLOTS[n]):
                remote(src, dq_rcv.at[j], 13, behind(SLOTS[n]))
            else:
                local(src, dq_rcv.at[j], recv_sems.at[13])

    for group_ in range(4):
        wait_all(do_sems.at[group_], do_rcv.at[pl.ds(512 * group_, 512)])
        attend_back(group_, group_ == 0)

    for group_ in range(4):
        at = slice(group_ * 512, group_ * 512 + 512)
        low = jnp.concatenate([dkt[0:72, at] * LN2, dvt[0:56, at]], axis=0).T.astype(BF16)
        for m in range(8):
            n = 8 * group_ + m
            dkv_snd[n, 0:64] = low[64 * m : 64 * m + 64]
            tail = dvt[56:72, 128 * (n // 2) : 128 * (n // 2) + 128]
            dkv_snd[n, 64:80] = roll(tail, 64 * (n % 2)).astype(BF16)
            if any(SLOTS[n]):
                remote(dkv_snd.at[n], dkv_rcv.at[j], 6, behind(SLOTS[n]))
            else:
                local(dkv_snd.at[n], dkv_rcv.at[j], recv_sems.at[6])

    reduce_second(r1_rcv, r1_z, owns1, 7)

    wait_all(recv_sems.at[13], dq_rcv)

    def both(buffer, h):
        return jnp.concatenate([buffer[h, 0:64], buffer[HEADS + h, 0:64]], axis=0).astype(F32)

    tiles = [None] * GROUPS
    for h in range(HEADS):
        place(tiles, h, roll(both(dq_rcv, h), (HEAD_DIM * h) % 128))
    for t in range(GROUPS):
        dproj_b[:, t * 128 : (t + 1) * 128] = tiles[t].astype(BF16)
    for c in range(3):
        at = slice(c * 384, (c + 1) * 384)
        hidp[:, at] = dot_nt(dproj_b[:, 0:D], wsp[at, 0:D])
    reduce_third(r1_z, r1_chunk, r1_out, chunk1, owns1, 7)
    wait_all(recv_sems.at[6], dkv_rcv)

    tails = []
    for eight in range(2):
        stack = []
        for h in range(8 * eight, 8 * eight + 8):
            first = dkv_rcv[h, 64:80].astype(F32)
            second = dkv_rcv[HEADS + h, 64:80].astype(F32)
            stack.append(jnp.where(lanes((16, 128)) < 64, first, roll(second, 64)))
        tails.append(jnp.concatenate(stack, axis=0).T)
    tiles_k, tiles_v = [None] * GROUPS, [None] * GROUPS
    for h in range(HEADS):
        off = (HEAD_DIM * h) % 128
        low = both(dkv_rcv, h)
        tail = roll(tails[h // 8], -16 * (h % 8))
        place(tiles_k, h, roll(jnp.where(lane < 72, low, 0.0), off))
        v = jnp.where(lane >= 72, low, jnp.where(lane < 16, tail, 0.0))
        place(tiles_v, h, roll(v, off - 72))
    for t in range(GROUPS):
        dproj_b[:, D + t * 128 : D + (t + 1) * 128] = tiles_k[t].astype(BF16)
        dproj_b[:, 2 * D + t * 128 : 2 * D + (t + 1) * 128] = tiles_v[t].astype(BF16)

    for c in range(3):
        at = slice(c * 384, (c + 1) * 384)
        hidp[:, at] += dot_nt(dproj_b[:, D:], wsp[at, D:])
    adj_rot1 = hidp[...].astype(BF16)
    packed = rotation_gradient(normed1[...].astype(BF16), adj_rot1)
    flat = jnp.concatenate(packed, axis=0).astype(BF16)
    for o in range(6):
        r2_snd[o] = flat[48 * o : 48 * o + 48]
    owner = 2 * px + pc
    owns2 = owner < 6
    row = [s for s in SLOTS if s[1] == 0]
    sheet = [s for s in SPACE if s[0] == 0 and s[2] == 0]
    for step in row:
        zz, jj = ahead(step)
        there = 2 * (jj >> 3) + (jj & 1)

        @pl.when(there < 6)
        def _():
            if any(step):
                remote(r2_snd.at[there], r2_rcv.at[owner], 10, (zz, jj))
            else:
                local(r2_snd.at[there], r2_rcv.at[owner], recv_sems.at[10])

    adj_normed = rotate_transposed(adj_rot1, bd.at[0])
    wait_all(recv_sems.at[5], ah_rcv)
    grad = ah_rcv[...].reshape(TOKENS, D).astype(F32) + normalize_backward(
        adj_normed, normed1[...], inverse1[...]
    )
    vg[...] = grad.astype(BF16).reshape(2, 64, D)
    vg_out = pltpu.make_async_copy(vg, vg_ref, out_sems.at[0])
    vg_out.start()
    @pl.when(owns2)
    def _():
        wait_all(recv_sems.at[10], r2_rcv)
        own = 4 * z + py
        r2_z[own] = jnp.sum(r2_rcv[...].astype(F32), axis=0).astype(BF16)
        for step in sheet:
            remote(r2_z.at[own], r2_z.at[own], 11, ahead(step))

    wait_all(send_sems.at[0], vid_mid.at[pl.ds(0, 6)])
    wait_all(send_sems.at[1], ct_mid.at[pl.ds(0, 6)])
    wait_all(send_sems.at[2], qkv_snd.at[pl.ds(0, PWAYS - 1)])
    wait_all(send_sems.at[3], att_snd.at[pl.ds(0, PATCHES - 16)])
    wait_all(send_sems.at[4], do_rcv.at[pl.ds(0, PATCHES - 16)])
    wait_all(send_sems.at[5], ah_snd.at[pl.ds(0, 6)])
    wait_all(send_sems.at[6], dkv_snd.at[pl.ds(0, PWAYS - 1)])
    wait_all(send_sems.at[13], dq_snd.at[pl.ds(0, PATCHES - 64)])
    wait_all(recv_sems.at[9], r1_out)
    red1 = pltpu.make_async_copy(r1_out, red_ref.at[pl.ds(0, 3 * ROWS)], out_sems.at[1])
    red1.start()
    @pl.when(owns2)
    def _():
        wait_all(recv_sems.at[11], r2_z.at[pl.ds(0, 15)])
        r2_chunk[...] = (jnp.sum(r2_z[...].astype(F32), axis=0) / 128.0).astype(BF16)
        dst = red_ref.at[pl.ds(pl.multiple_of(3 * ROWS + 48 * owner, 16), 48)]
        for step in row:
            if any(step):
                remote(r2_chunk, dst, 12, ahead(step))
            else:
                local(r2_chunk, dst, recv_sems.at[12])

    reduce_sent(r1_snd, r1_rcv, r1_z, 27, owns1, 7)
    @pl.when(owns2)
    def _():
        wait_all(send_sems.at[10], r2_snd.at[pl.ds(0, 5)])
        wait_all(send_sems.at[11], r2_z.at[pl.ds(0, 15)])
        wait_all(send_sems.at[12], r2_rcv.at[pl.ds(0, 7)])

    @pl.when(jnp.logical_not(owns2))
    def _():
        wait_all(send_sems.at[10], r2_snd)

    wait_all(recv_sems.at[12], red_ref.at[pl.ds(3 * ROWS, ROWS)])
    red1.wait()
    vg_out.wait()


def unpack_kernel(red_h, vg_in, vg_out, sout, tin, tout, sin, red, vg, terms, sems):
    load = pltpu.make_async_copy(red_h, red, sems.at[0])
    load.start()
    copy = pltpu.make_async_copy(vg_in, vg, sems.at[1])
    copy.start()
    shape = (BLOCK, 40, ROWS)
    b = lax.broadcasted_iota(jnp.int32, shape, 0)
    n = lax.broadcasted_iota(jnp.int32, shape, 1)
    from_row = lax.broadcasted_iota(jnp.int32, shape, 2)
    pick = jnp.where(from_row == (n >> 2) * BLOCK + b, 1.0, 0.0).reshape(BLOCK * 40, ROWS).astype(BF16)
    shape = (BLOCK, 40, 128)
    n = lax.broadcasted_iota(jnp.int32, shape, 1)
    own = ((n & 3) == (lax.broadcasted_iota(jnp.int32, shape, 2) >> 5)).reshape(BLOCK * 40, 128)
    repeat = jnp.where(lanes((128, 128)) % BLOCK == rows((128, 128)) % BLOCK, 1.0, 0.0).astype(BF16)
    lane = lanes((40, 128)) >> 5
    copy.wait()
    stores = [pltpu.make_async_copy(vg, vg_out, sems.at[1])]
    stores[0].start()
    load.wait()
    for term, out in enumerate((sout, tin, tout, sin)):
        wide = dot(pick, red[term * ROWS : (term + 1) * ROWS, :])
        wide = dot(jnp.where(own, wide, 0.0).astype(BF16), repeat)
        for m in range(8):
            four = jnp.zeros((40, 128), F32)
            for s in range(4):
                at = (4 * m + s) * 40
                four = jnp.where(lane == s, wide[at : at + 40], four)
            terms[term, 4 * m : 4 * m + 4] = four.T[:, 0:NBLOCK].reshape(4, BLOCK, NBLOCK)
        stores.append(pltpu.make_async_copy(terms.at[term], out, sems.at[2 + term]))
        stores[-1].start()
    for store in stores:
        store.wait()


def per_device(
    video,
    cotangent,
    frame_mask,
    spatial_project,
    spatial_output,
    temporal_project,
    temporal_output,
    spatial_inward,
    spatial_outward,
    temporal_inward,
    temporal_outward,
):
    vm = pltpu.VMEM
    dma = pltpu.SemaphoreType.DMA
    scratch = [
        vm((D, 3 * D), BF16), vm((D, D), BF16), vm((D, 3 * D), BF16), vm((D, D), BF16),
        vm((4, BLOCK, BLOCK, NBLOCK), F32), vm((D, 128), F32), vm((4, D, 128), BF16),
        vm((2, 64, D), BF16), vm((2, 64, D), BF16), vm((FRAMES, 16, D), BF16), vm((FRAMES, 16, D), BF16),
        vm((TOKENS, D), F32), vm((TOKENS, 1), F32), vm((TOKENS, D), BF16), vm((TOKENS, 3 * D), F32),
        vm((PWAYS, 64, 256), BF16), vm((PATCHES, 256), BF16),
        vm((PATCHES, 128), BF16), vm((PATCHES, 128), BF16), vm((PATCHES, 128), BF16),
        vm((PATCHES, 128), BF16), vm((FRAMES, HEADS, 16, 128), BF16), vm((TOKENS, D), BF16),
        vm((TOKENS, D), F32), vm((TOKENS, D), BF16), vm((TOKENS, D + 128), BF16),
        vm((TOKENS, D), F32), vm((TOKENS, D), F32), vm((TOKENS, 3 * D), BF16),
        vm((TOKENS, D), BF16), vm((TOKENS, 3 * D), BF16),
        vm((HEADS, TOKENS, TOKENS), F32), vm((HEADS, TOKENS, TOKENS), F32),
        vm((HEADS, TOKENS, TOKENS), BF16), vm((HEADS, TOKENS, TOKENS), BF16),
        vm((FRAMES, 16, D), BF16), vm((2, 64, D), BF16),
        vm((FRAMES, HEADS, 16, 128), BF16), vm((PATCHES, 128), BF16),
        vm((80, PATCHES), BF16), vm((80, PATCHES), F32), vm((80, PATCHES), F32), vm((PATCHES, PATCHES), BF16),
        vm((PWAYS, 80, 128), BF16), vm((PWAYS, 80, 128), BF16),
        vm((PATCHES, 128), BF16), vm((PWAYS, 64, 128), BF16), vm((2, 64, D), BF16),
        vm((27, 32, 128), BF16), vm((PWAYS, 32, 128), BF16), vm((ZWAYS, 32, 128), F32),
        vm((32, 128), BF16), vm((3 * ROWS, 128), BF16),
        vm((6, 48, 128), BF16), vm((8, 48, 128), BF16), vm((16, 48, 128), BF16),
        vm((48, 128), BF16),
        dma((12,)), dma((3,)), dma((14,)), dma((14,)), dma((4,)), dma((4,)),
    ]
    anyspec = pl.BlockSpec(memory_space=pl.ANY)
    blocks = [r.transpose(1, 2, 0) for r in (spatial_inward, spatial_outward, temporal_inward, temporal_outward)]
    grad, red = pl.pallas_call(
        kernel,
        out_shape=(
            jax.ShapeDtypeStruct((2, 64, D), BF16),
            jax.ShapeDtypeStruct((4 * ROWS, 128), BF16),
        ),
        in_specs=[pl.BlockSpec(memory_space=pltpu.SMEM)] + [anyspec] * 10,
        out_specs=(anyspec, anyspec),
        scratch_shapes=scratch,
        compiler_params=pltpu.CompilerParams(
            collective_id=0, has_side_effects=True, vmem_limit_bytes=62 * 1024 * 1024
        ),
        name="block_backward",
    )(
        frame_mask, video, cotangent, spatial_project, spatial_output, temporal_project, temporal_output,
        *blocks,
    )
    term = jax.ShapeDtypeStruct((BLOCK, BLOCK, NBLOCK), F32)
    grad, sout, tin, tout, sin = pl.pallas_call(
        unpack_kernel,
        out_shape=(jax.ShapeDtypeStruct((2, 64, D), BF16), term, term, term, term),
        in_specs=[anyspec] * 2,
        out_specs=(anyspec,) * 5,
        scratch_shapes=[
            vm((4 * ROWS, 128), BF16), vm((2, 64, D), BF16), vm((4, BLOCK, BLOCK, NBLOCK), F32), dma((6,)),
        ],
        compiler_params=pltpu.CompilerParams(vmem_limit_bytes=62 * 1024 * 1024),
        name="unpack_terms",
    )(red, grad)
    sin, sout, tin, tout = (r.transpose(2, 0, 1) for r in (sin, sout, tin, tout))
    return grad, sin, sout, tin, tout


def solution(mesh):
    split = P("frame", "patch", None)
    in_specs = (split, split) + (P(),) * 9
    out_specs = (split,) + (P(),) * 4
    return jax.shard_map(
        per_device, mesh=mesh, in_specs=in_specs, out_specs=out_specs, check_vma=False
    )
```

```python
import itertools
import math

import jax
import jax.numpy as jnp
from jax import lax
from jax.experimental import pallas as pl
from jax.experimental.pallas import tpu as pltpu
from jax.sharding import PartitionSpec as P

D = 1152
HEADS = 16
HEAD_DIM = 72
BLOCK = 32
GROUPS = D // 128
FRAMES = 8
PATCHES = 2048
ZWAYS = 4
PWAYS = 32
DEVICES = ZWAYS * PWAYS
TOKENS = 128
ROWS = D // 4
NBLOCK = D // 32

EPSILON = 1e-06
NEGATIVE = -1e30
SCALE = 1.0 / math.sqrt(HEAD_DIM)
LOG2E = math.log2(math.e)
LN2 = math.log(2.0)

F32 = jnp.float32
BF16 = jnp.bfloat16
MESH = pl.DeviceIdType.MESH


def hops(step):
    return min(step[0], 4 - step[0]) + min(step[1], 4 - step[1]) + min(step[3], 4 - step[3])


PLANE = sorted(
    [s for s in itertools.product(range(4), range(4), range(2), [0]) if any(s)], key=lambda s: -hops(s)
)
SPACE = sorted(
    [s for s in itertools.product(range(4), range(4), range(2), range(4)) if any(s)],
    key=lambda s: -hops(s),
)
SLOTS = PLANE + [(0, 0, 0, 0)]
SLOT_OF = {s[:3]: n for n, s in enumerate(SLOTS)}


def dot(a, b):
    return lax.dot_general(a, b, (((1,), (0,)), ((), ())), preferred_element_type=F32)


def dot_nt(a, b):
    return lax.dot_general(a, b, (((1,), (1,)), ((), ())), preferred_element_type=F32)


def dot_tn(a, b):
    return lax.dot_general(a, b, (((0,), (0,)), ((), ())), preferred_element_type=F32)


def lanes(shape):
    return lax.broadcasted_iota(jnp.int32, shape, len(shape) - 1)


def rows(shape):
    return lax.broadcasted_iota(jnp.int32, shape, 0)


def roll(x, amount):
    amount = amount % 128
    return x if amount == 0 else pltpu.roll(x, amount, 1)


def normalize(x):
    centered = x - jnp.mean(x, axis=-1, keepdims=True)
    inverse = lax.rsqrt(jnp.mean(centered * centered, axis=-1, keepdims=True) + EPSILON)
    return centered * inverse, inverse


def normalize_backward(adjoint, normed, inverse):
    grad_mean = jnp.mean(adjoint, axis=-1, keepdims=True)
    grad_cross = jnp.mean(adjoint * normed, axis=-1, keepdims=True)
    return inverse * (adjoint - grad_mean - normed * grad_cross)


def group(x, g):
    return x[:, g * 128 : (g + 1) * 128]


def rotate(x, blocks):
    return jnp.concatenate(
        [dot(group(x, g), blocks[g * 128 : (g + 1) * 128, :]) for g in range(GROUPS)], axis=1
    )


def rotate_transposed(x, blocks):
    return jnp.concatenate(
        [dot_nt(group(x, g), blocks[g * 128 : (g + 1) * 128, :]) for g in range(GROUPS)], axis=1
    )


def block_mask(shape):
    return (rows(shape) // BLOCK) % 4 == lanes(shape) // BLOCK


def rotation_gradient(left, right):
    mask = block_mask((128, 128))
    packed = []
    for g in range(GROUPS):
        full = jnp.where(mask, dot_tn(group(left, g), group(right, g)), 0.0)
        packed.append(full[0:32] + full[32:64] + full[64:96] + full[96:128])
    return packed


def layout_tools():
    shape = (BLOCK, 40, ROWS)
    b = lax.broadcasted_iota(jnp.int32, shape, 0)
    n = lax.broadcasted_iota(jnp.int32, shape, 1)
    from_row = lax.broadcasted_iota(jnp.int32, shape, 2)
    pick = jnp.where(from_row == (n >> 2) * BLOCK + b, 1.0, 0.0).reshape(BLOCK * 40, ROWS).astype(BF16)
    shape = (BLOCK, 40, 128)
    n = lax.broadcasted_iota(jnp.int32, shape, 1)
    own = ((n & 3) == (lax.broadcasted_iota(jnp.int32, shape, 2) >> 5)).reshape(BLOCK * 40, 128)
    repeat = jnp.where(lanes((128, 128)) % BLOCK == rows((128, 128)) % BLOCK, 1.0, 0.0).astype(BF16)
    return pick, own, repeat


def lay_out(tools, term, out):
    pick, own, repeat = tools
    lane = lanes((40, 128)) >> 5
    wide = dot(pick, term)
    wide = dot(jnp.where(own, wide, 0.0).astype(BF16), repeat)
    for m in range(8):
        four = jnp.zeros((40, 128), F32)
        for s in range(4):
            at = (4 * m + s) * 40
            four = jnp.where(lane == s, wide[at : at + 40], four)
        out[4 * m : 4 * m + 4] = four.T[:, 0:NBLOCK].reshape(4, BLOCK, NBLOCK)


def kernel(
    mask_ref, video, cotangent, wsp_h, wso_h, wtp_h, wto_h, rsi_h, rso_h, rti_h, rto_h,
    vg_ref, terms_ref, red_ref,
    wsp, wso, wtp, wto, r4, bd32, bd,
    vid, cot, vid_mid, ct_mid,
    normed1, inverse1, rot_b, proj,
    qkv_snd, qkv_rcv, kx, qx, vx,
    att_snd, att_rcv, att1, top, aot, daz,
    hidp, normed2, proj2, att2_b, dproj_b,
    t_s, t_dp, t_p, t_ds,
    ah_snd, ah_rcv, do_snd, do_rcv, qt, dkt, dvt, pq,
    dk_snd, dk_rcv, dv_snd, dv_rcv, dq_snd, dq_rcv, dq_last, w_last, vg, dpt, adjt,
    r1_snd, r1_rcv, r1_z, r1_chunk, r1_out,
    r2_snd, r2_rcv, r2_z, r2_chunk, terms,
    load_sems, out_sems, send_sems, recv_sems, qkv_sems, do_sems,
):
    z = lax.axis_index("frame")
    j = lax.axis_index("patch")
    px, py, pc = j >> 3, (j >> 1) & 3, j & 1
    xs = [((px + d) & 3) * 8 for d in range(4)]
    ys = [((py + d) & 3) * 2 for d in range(4)]
    cs = [(pc + d) & 1 for d in range(2)]
    zs = [(z + d) & 3 for d in range(4)]
    xys = [[a + b for b in ys] for a in xs]

    def ahead(step):
        return zs[step[3]], xys[step[0]][step[1]] + cs[step[2]]

    def behind(step):
        return zs[-step[3] & 3], xys[-step[0] & 3][-step[1] & 3] + cs[step[2]]

    def load(src, dst, n):
        return pltpu.make_async_copy(src, dst, load_sems.at[n])

    early = [load(video, vid, 0), load(rsi_h, r4.at[0], 1)]
    early += [
        load(wsp_h.at[:, pl.ds(c * D, D)], wsp.at[:, pl.ds(c * D, D)], n) for c, n in enumerate((2, 10, 11))
    ]
    late = [
        load(cotangent, cot, 3), load(rso_h, r4.at[1], 4), load(rti_h, r4.at[2], 5),
        load(rto_h, r4.at[3], 6), load(wto_h, wto, 7), load(wso_h, wso, 8), load(wtp_h, wtp, 9),
    ]
    for copy in early:
        copy.start()

    barrier = pltpu.get_barrier_semaphore()
    near = PLANE + [(0, 0, 0, d) for d in (2, 1, 3)]
    for step in near:
        pl.semaphore_signal(barrier, inc=1, device_id=ahead(step), device_id_type=MESH)

    def local(src, dst, sem):
        pltpu.make_async_copy(src, dst, sem).start()

    def remote(src, dst, phase, there, recv_sem=None):
        pltpu.make_async_remote_copy(
            src_ref=src, dst_ref=dst, send_sem=send_sems.at[phase],
            recv_sem=recv_sems.at[phase] if recv_sem is None else recv_sem,
            device_id=there, device_id_type=MESH,
        ).start()

    def wait_all(sem, buffer):
        pltpu.make_async_copy(buffer, buffer, sem).wait()

    def make_blocks(index):
        shape = (128, 512)
        spread = jnp.where(
            jnp.logical_and(
                rows(shape) // BLOCK == lanes(shape) // 128, rows(shape) % BLOCK == lanes(shape) % BLOCK
            ),
            1.0, 0.0,
        ).astype(BF16)
        shape = (NBLOCK, 128)
        own = rows(shape) % 4 == lanes(shape) // BLOCK
        for m in range(8):
            four = r4[index, 4 * m : 4 * m + 4].reshape(128, NBLOCK).astype(BF16)
            wide = dot_tn(four, spread)
            for s in range(4):
                bd32[pl.ds(4 * m + s, NBLOCK, stride=BLOCK), :] = jnp.where(own, group(wide, s), 0.0)
        bd[index] = bd32[...].astype(BF16)

    early[0].wait()
    normed, _ = normalize(vid[...].reshape(TOKENS, D).astype(F32))
    early[1].wait()
    make_blocks(0)
    rot_b[...] = rotate(normed.astype(BF16), bd.at[0]).astype(BF16)

    for c in range(3):
        at = slice(c * D, (c + 1) * D)
        early[2 + c].wait()
        proj[:, at] = dot(rot_b[...], wsp[:, at])
    for copy in late:
        copy.start()

    lane = lanes((TOKENS, 128))
    qscale = jnp.where(lane < HEAD_DIM, SCALE * LOG2E, 1.0)
    for h in range(HEADS):
        t, off = (HEAD_DIM * h) // 128, (HEAD_DIM * h) % 128

        def pick(section, to):
            first = proj[:, section * D + t * 128 : section * D + (t + 1) * 128]
            if off + HEAD_DIM > 128:
                second = proj[:, section * D + (t + 1) * 128 : section * D + (t + 2) * 128]
                first = jnp.where(lane >= off, first, second)
            return roll(first, to - off)

        q, k, v = pick(0, 0), pick(1, 72), pick(2, 16)
        low = (jnp.where(lane < 72, q, k) * qscale).astype(BF16)
        high = jnp.where(lane < 16, k, jnp.where(lane < 88, v, 0.0)).astype(BF16)
        for f in range(2):
            qkv_snd[f * HEADS + h, :, 0:128] = low[64 * f : 64 * (f + 1)]
            qkv_snd[f * HEADS + h, :, 128:256] = high[64 * f : 64 * (f + 1)]

    pl.semaphore_wait(barrier, len(near))

    for n, step in enumerate(SLOTS):
        dst = qkv_rcv.at[pl.ds(64 * n, 64)]
        if any(step):
            zz, jj = ahead(step)
            remote(qkv_snd.at[jj], dst, 2, (zz, jj), qkv_sems.at[n // 8])
        else:
            local(qkv_snd.at[j], dst, qkv_sems.at[n // 8])

    late[0].wait()
    for phase, src, dst in ((1, cot, ct_mid), (0, vid, vid_mid)):
        for d in (2, 1, 3, 0):
            for f in range(2):
                piece = src.at[f, pl.ds(pl.multiple_of(zs[d] * 16, 16), 16)]
                if d:
                    remote(piece, dst.at[2 * z + f], phase, (zs[d], j))
                else:
                    local(piece, dst.at[2 * z + f], recv_sems.at[phase])

    for n in (1, 2, 3):
        late[n].wait()
        make_blocks(n)

    columns = vid[...].reshape(TOKENS, D).astype(F32).T
    columns = columns - jnp.mean(columns, axis=0, keepdims=True)
    inverse = lax.rsqrt(jnp.mean(columns * columns, axis=0, keepdims=True) + EPSILON)
    normed1[...] = columns * inverse
    inverse1[...] = jnp.broadcast_to(inverse, (8, 128))

    shape = (D, 128)
    column = HEAD_DIM * (lanes(shape) >> 3) + 64 + (lanes(shape) & 7)
    select = jnp.where(rows(shape) == column, 1.0, 0.0).astype(BF16)
    for n, section in enumerate((0, 2)):
        w_last[n] = dot(wsp[:, section * D : (section + 1) * D], select).astype(BF16)

    wait_all(recv_sems.at[1], ct_mid)
    frame_row = rows((TOKENS, 1)) // 16
    valid = jnp.zeros((TOKENS, 1), F32)
    for f in range(FRAMES):
        valid = jnp.where(frame_row == f, mask_ref[f].astype(F32), valid)
    top[...] = ct_mid[...].reshape(TOKENS, D).astype(F32) * valid
    late[4].wait()
    aot[...] = dot_nt(top[...].astype(BF16), wto[...]).astype(BF16)
    daz[:, 0:D] = rotate_transposed(aot[...], bd.at[3]).astype(BF16)
    daz[:, D:] = jnp.zeros((TOKENS, 128), BF16)

    lane2 = lanes((256, 128))
    ones = jnp.where(jnp.logical_and(lane2 >= 72, lane2 < 76), 1.0, 0.0)

    def prepare(i, carry):
        at = pl.ds(pl.multiple_of(i * 256, 256), 256)
        t0, t1 = qkv_rcv[at, 0:128].astype(F32), qkv_rcv[at, 128:256].astype(F32)
        k = roll(jnp.where(lane2 >= 72, t0, t1), -72)
        kx[at, :] = jnp.where(lane2 < 72, k, ones).astype(BF16)
        vx[at, :] = jnp.where(lane2 < 72, roll(t1, -16), ones).astype(BF16)
        qx[at, :] = jnp.where(lane2 < 72, t0, 0.0).astype(BF16)
        return carry

    for g in range(4):
        wait_all(qkv_sems.at[g], qkv_rcv.at[pl.ds(512 * g, 512)])
        lax.fori_loop(2 * g, 2 * g + 2, prepare, 0)

    def attend(i, carry):
        spans = [pl.ds(pl.multiple_of(i * 512 + s * 256, 256), 256) for s in range(2)]
        highs = []
        for s, at in enumerate(spans):
            scores = dot_nt(qx[at, :], kx[...])
            highs.append(jnp.max(scores, axis=-1, keepdims=True))
            pq[256 * s : 256 * s + 256, :] = jnp.exp2(scores - highs[-1]).astype(BF16)
        both_out = dot(pq[0:512, :], vx[...])
        for s, (at, high_score) in enumerate(zip(spans, highs)):
            out = both_out[256 * s : 256 * s + 256]
            total = out[:, 72:73]
            att_snd[at, :] = jnp.where(lane2 < 72, out / total, 0.0).astype(BF16)
            neg = -(high_score + jnp.log(total) * LOG2E)
            hi = neg.astype(BF16).astype(F32)
            mid = (neg - hi).astype(BF16).astype(F32)
            lo = neg - hi - mid
            old = qx[at, :].astype(F32)
            new = jnp.where(
                lane2 == 72, hi, jnp.where(lane2 == 73, mid, jnp.where(lane2 == 74, lo, old))
            )
            qx[at, :] = new.astype(BF16)

        for ii in range(4):

            @pl.when(i == ii)
            def _():
                for n in range(8 * ii, 8 * ii + 8):
                    for d in (2, 1, 3, 0):
                        zz, jj = zs[d], behind(SLOTS[n])[1]
                        src = att_snd.at[pl.ds(pl.multiple_of(64 * n + 16 * zz, 16), 16)]
                        dst = att_rcv.at[2 * z + (j >> 4), j & 15]
                        if d or any(SLOTS[n]):
                            remote(src, dst, 3, (zz, jj))
                        else:
                            local(src, dst, recv_sems.at[3])

        return carry

    lax.fori_loop(0, 4, attend, 0)

    wait_all(recv_sems.at[0], vid_mid)
    wait_all(recv_sems.at[3], att_rcv)

    def add_piece(tiles, at, piece):
        tiles[at] = piece if tiles[at] is None else tiles[at] + piece

    def place(tiles, h, value):
        t, off = (HEAD_DIM * h) // 128, (HEAD_DIM * h) % 128
        if off + HEAD_DIM > 128:
            add_piece(tiles, t, jnp.where(lane >= off, value, 0.0))
            add_piece(tiles, t + 1, jnp.where(lane < off, value, 0.0))
        else:
            add_piece(tiles, t, value)

    tiles = [None] * GROUPS
    for h in range(HEADS):
        place(tiles, h, roll(att_rcv[:, h].reshape(TOKENS, 128).astype(F32), (HEAD_DIM * h) % 128))
    for t in range(GROUPS):
        att1[:, t * 128 : (t + 1) * 128] = tiles[t].astype(BF16)

    late[5].wait()
    outrot = rotate(att1[...], bd.at[1]).astype(BF16)
    hidden = vid_mid[...].reshape(TOKENS, D).astype(F32) + dot(outrot, wso[...])
    hidden = hidden.astype(BF16).astype(F32)
    normed, inverse2 = normalize(hidden)
    normed2[...] = normed
    rot_b[...] = rotate(normed.astype(BF16), bd.at[2]).astype(BF16)
    late[6].wait()

    def project2(c, carry):
        at = pl.ds(pl.multiple_of(c * D, 128), D)
        proj2[:, at] = dot(rot_b[...], wtp[:, at]).astype(BF16)
        return carry

    lax.fori_loop(0, 3, project2, 0)

    square = (TOKENS, TOKENS)
    same_patch = rows(square) % 16 == lanes(square) % 16
    same_frame = rows(square) // 16 == lanes(square) // 16
    key_valid = jnp.zeros(square, F32)
    for f in range(FRAMES):
        key_valid = jnp.where(rows(square) // 16 == f, mask_ref[f].astype(F32), key_valid)
    allowed = jnp.logical_and(same_patch, jnp.logical_or(key_valid == 1.0, same_frame))
    bias = jnp.where(allowed, 0.0, NEGATIVE)

    def window(h, section):
        t, off = (HEAD_DIM * h) // 128, (HEAD_DIM * h) % 128
        width = 256 if off + HEAD_DIM > 128 else 128
        return slice(section * D + t * 128, section * D + t * 128 + width)

    def own_lanes(h):
        off = (HEAD_DIM * h) % 128
        l = lanes((1, 256 if off + HEAD_DIM > 128 else 128))
        return jnp.where(jnp.logical_and(l >= off, l < off + HEAD_DIM), 1.0, 0.0)

    for h in range(HEADS):
        own = own_lanes(h).astype(BF16)
        t_s[h] = dot_nt(proj2[:, window(h, 1)], proj2[:, window(h, 0)] * own)
        t_dp[h] = dot_nt(proj2[:, window(h, 2)], daz[:, window(h, 0)] * own)

    for h in range(HEADS):
        scores = t_s[h] * SCALE + bias
        e = jnp.exp(scores - jnp.max(scores, axis=0, keepdims=True))
        p = e * (1.0 / jnp.sum(e, axis=0, keepdims=True))
        dp = t_dp[h]
        t_p[h] = p.astype(BF16)
        t_ds[h] = (p * (dp - jnp.sum(p * dp, axis=0, keepdims=True))).astype(BF16)

    def gather(section, dst, base):
        tiles = [None] * (GROUPS + 1)
        for h in range(HEADS):
            own = own_lanes(h)
            own_b = own.astype(BF16)
            if section == 0:
                part = dot_tn(t_ds[h], proj2[:, window(h, 1)]) * (own * SCALE)
            elif section == 1:
                part = dot(t_ds[h], proj2[:, window(h, 0)] * own_b) * SCALE
            elif section == 2:
                part = dot(t_p[h], daz[:, window(h, 0)] * own_b)
            else:
                part = dot_tn(t_p[h], proj2[:, window(h, 2)]) * own
            t = (HEAD_DIM * h) // 128
            for w in range(part.shape[1] // 128):
                add_piece(tiles, t + w, group(part, w))
        for t in range(GROUPS):
            dst[:, base + t * 128 : base + (t + 1) * 128] = tiles[t].astype(BF16)

    for section in range(3):
        gather(section, dproj_b, section * D)

    for c in range(3):
        at = slice(c * 384, (c + 1) * 384)
        hidp[:, at] = dot_nt(dproj_b[...], wtp[at, :])
    adj_rot2 = hidp[...].astype(BF16)
    adj_normed = rotate_transposed(adj_rot2, bd.at[2])
    adj_hidden = top[...] + normalize_backward(adj_normed, normed2[...], inverse2)
    adj_hidden_b = adj_hidden.astype(BF16)
    ah_snd[...] = adj_hidden_b.reshape(FRAMES, 16, D)
    aho = dot_nt(adj_hidden_b, wso[...]).astype(BF16)
    adj_att1 = rotate_transposed(aho, bd.at[1])
    for h in range(HEADS):
        t, off = (HEAD_DIM * h) // 128, (HEAD_DIM * h) % 128
        first = group(adj_att1, t)
        if off + HEAD_DIM > 128:
            first = jnp.where(lane >= off, first, group(adj_att1, t + 1))
        piece = jnp.where(lane < 72, roll(first, -off), 0.0).astype(BF16)
        do_snd[:, h] = piece.reshape(FRAMES, 16, 128)

    for step in [slot[:3] + (d,) for slot in SLOTS for d in (2, 1, 3, 0)]:
        zz, jj = ahead(step)
        src = do_snd.at[2 * zz + (jj >> 4), jj & 15]
        n = SLOT_OF[step[:3]]
        dst = do_rcv.at[pl.ds(pl.multiple_of(64 * n + 16 * z, 16), 16)]
        if any(step):
            remote(src, dst, 4, (zz, jj), do_sems.at[n // 8])
        else:
            local(src, dst, do_sems.at[n // 8])
    for d in (2, 1, 3, 0):
        for f in range(2):
            src = ah_snd.at[2 * zs[d] + f]
            dst = ah_rcv.at[f, pl.ds(pl.multiple_of(z * 16, 16), 16)]
            if d:
                remote(src, dst, 5, (zs[d], j))
            else:
                local(src, dst, recv_sems.at[5])

    gather(3, att2_b, 0)
    for n, packed in enumerate((
        rotation_gradient(att1[...], aho),
        rotation_gradient(normed2[...].astype(BF16), adj_rot2),
        rotation_gradient(att2_b[...], aot[...]),
    )):
        for g in range(GROUPS):
            r1_snd[n * GROUPS + g] = packed[g].astype(BF16)

    def reduce_first(snd, rcv, chunk_of, owns, phase):
        for step in SLOTS:
            zz, jj = ahead(step)

            @pl.when(owns(jj))
            def _():
                if any(step):
                    remote(snd.at[chunk_of(jj)], rcv.at[j], phase, (zz, jj))
                else:
                    local(snd.at[chunk_of(jj)], rcv.at[j], recv_sems.at[phase])

    def reduce_second(rcv, zbuf, owns, phase):
        @pl.when(owns(j))
        def _():
            wait_all(recv_sems.at[phase], rcv)
            zbuf[z] = jnp.sum(rcv[...].astype(F32), axis=0)
            for d in (2, 1, 3):
                remote(zbuf.at[z], zbuf.at[z], phase + 1, (zs[d], j))

    def reduce_third(zbuf, chunk, out, chunk_of, owns, phase):
        size = chunk.shape[0]

        @pl.when(owns(j))
        def _():
            wait_all(recv_sems.at[phase + 1], zbuf.at[pl.ds(0, ZWAYS - 1)])
            chunk[...] = (((zbuf[0] + zbuf[1]) + (zbuf[2] + zbuf[3])) / 128.0).astype(BF16)
            dst = out.at[pl.ds(pl.multiple_of(chunk_of(j) * size, size), size)]
            for step in SLOTS:
                if any(step):
                    remote(chunk, dst, phase + 2, ahead(step))
                else:
                    local(chunk, dst, recv_sems.at[phase + 2])

    def reduce_sent(snd, rcv, zbuf, owners, owns, phase):
        @pl.when(owns(j))
        def _():
            wait_all(send_sems.at[phase], snd.at[pl.ds(0, owners - 1)])
            wait_all(send_sems.at[phase + 1], zbuf.at[pl.ds(0, ZWAYS - 1)])
            wait_all(send_sems.at[phase + 2], rcv.at[pl.ds(0, PWAYS - 1)])

        @pl.when(jnp.logical_not(owns(j)))
        def _():
            wait_all(send_sems.at[phase], snd)

    def chunk1(jj):
        return jj

    def owns1(jj):
        return jj < 27

    reduce_first(r1_snd, r1_rcv, chunk1, owns1, 7)

    def probabilities(i, carry):
        for s in range(2):
            at = pl.ds(pl.multiple_of(i * 512 + s * 256, 256), 256)
            pq[at, :] = jnp.exp2(dot_nt(qx[at, :], kx[...])).astype(BF16)
        return carry

    lax.fori_loop(0, 4, probabilities, 0)

    def prepare_queries(i, carry):
        at = pl.ds(pl.multiple_of(i * 256, 256), 256)
        qt[:, at] = qx[at, :].astype(F32).T[0:80].astype(BF16)
        return carry

    lax.fori_loop(0, 8, prepare_queries, 0)

    def beside(left, right, odd):
        left, right = (roll(left, 64), right) if odd else (left, roll(right, 64))
        return jnp.where(lanes(left.shape) < 64, left, right)

    def value_gradient(group_):
        at = pl.ds(group_ * 512, 512)
        dv = dot(do_rcv[at, :].astype(F32).T[0:80].astype(BF16), pq[at, :])
        if group_ == 0:
            dvt[...] = dv
        else:
            dvt[...] += dv

    def attend_back(group_):
        at = pl.ds(group_ * 512, 512)
        lane5 = lanes((512, 128))
        g = do_rcv[at, :].astype(F32)
        delta = -jnp.sum(g * att_snd[at, :].astype(F32), axis=-1, keepdims=True)
        hi = delta.astype(BF16).astype(F32)
        lo = delta - hi
        dox = jnp.where(lane5 == 72, hi, jnp.where(lane5 == 73, lo, g)).astype(BF16)
        ds = (pq[at, :].astype(F32) * dot_nt(dox, vx[...])).astype(BF16)
        dq = dot(ds, kx[...]).T * SCALE
        for m in range(8):
            tile = dq[:, 128 * (m // 2) : 128 * (m // 2) + 128]
            dq_snd[8 * group_ + m] = beside(tile[0:32], tile[32:64], m % 2).astype(BF16)
        dq_last[:, group_ * 512 : group_ * 512 + 512] = dq[64:72]
        dk = dot(qt[:, at], ds)
        if group_ == 0:
            dkt[...] = dk
        else:
            dkt[...] += dk
        send_back(dq_snd, dq_rcv, 13, range(8 * group_, 8 * group_ + 8))

    def send_back(snd, rcv, phase, slots):
        for n in slots:
            if any(SLOTS[n]):
                remote(snd.at[n], rcv.at[j], phase, behind(SLOTS[n]))
            else:
                local(snd.at[n], rcv.at[j], recv_sems.at[phase])

    for group_ in range(4):
        wait_all(do_sems.at[group_], do_rcv.at[pl.ds(512 * group_, 512)])
        value_gradient(group_)
        if group_ == 0:
            attend_back(0)
    for n in range(PWAYS):
        at = slice(128 * (n // 2), 128 * (n // 2) + 128)
        dv_snd[n] = beside(dvt[0:32, at], dvt[32:64, at], n % 2).astype(BF16)
    send_back(dv_snd, dv_rcv, 15, range(PWAYS))
    for group_ in (1, 2, 3):
        attend_back(group_)

    for n in range(PWAYS):
        at = slice(128 * (n // 2), 128 * (n // 2) + 128)
        rest = [dkt[48:72, at] * LN2, dq_last[:, at], dvt[64:72, at], jnp.zeros((8, 128), F32)]
        dk_snd[n] = beside(dkt[0:48, at] * LN2, jnp.concatenate(rest, axis=0), n % 2).astype(BF16)
    send_back(dk_snd, dk_rcv, 6, range(PWAYS))

    reduce_second(r1_rcv, r1_z, owns1, 7)

    def halves(buffer, h):
        one, two = buffer[h].astype(F32), buffer[HEADS + h].astype(F32)
        first = lanes(one.shape) < 64
        return jnp.where(first, one, roll(two, 64)), jnp.where(first, roll(one, 64), two)

    def unpack_first(buffer, base):
        for pair in range(HEADS // 2):
            parts = []
            for h in (2 * pair, 2 * pair + 1):
                parts += [*halves(buffer, h), jnp.zeros((8, 128), F32)]
            at = base + 144 * pair
            dpt[at : at + 144] = jnp.concatenate(parts, axis=0).astype(BF16)

    wait_all(recv_sems.at[15], dv_rcv)
    unpack_first(dv_rcv, 2 * D)
    for c in range(3):
        at = slice(c * 384, (c + 1) * 384)
        adjt[at] = dot(wsp[at, 2 * D :], dpt[2 * D :])
    wait_all(recv_sems.at[13], dq_rcv)
    unpack_first(dq_rcv, 0)
    for c in range(3):
        at = slice(c * 384, (c + 1) * 384)
        adjt[at] += dot(wsp[at, 0:D], dpt[0:D])
    reduce_third(r1_z, r1_chunk, r1_out, chunk1, owns1, 7)
    wait_all(recv_sems.at[6], dk_rcv)

    last = [[], []]
    for pair in range(HEADS // 2):
        parts = []
        for h in (2 * pair, 2 * pair + 1):
            left, right = halves(dk_rcv, h)
            parts += [left, right[0:24]]
            last[0].append(right[24:32])
            last[1].append(right[32:40])
        at = D + 144 * pair
        dpt[at : at + 144] = jnp.concatenate(parts, axis=0).astype(BF16)
    last = [jnp.concatenate(parts, axis=0).astype(BF16) for parts in last]

    for c in range(3):
        at = slice(c * 384, (c + 1) * 384)
        adjt[at] += (
            dot(wsp[at, D : 2 * D], dpt[D : 2 * D]) + dot(w_last[0, at], last[0]) + dot(w_last[1, at], last[1])
        )
    packed = []
    mask = block_mask((128, 128))
    for g in range(GROUPS):
        at = slice(g * 128, (g + 1) * 128)
        full = jnp.where(mask, dot_nt(normed1[at].astype(BF16), adjt[at].astype(BF16)), 0.0)
        packed.append(full[0:32] + full[32:64] + full[64:96] + full[96:128])
    flat = jnp.concatenate(packed, axis=0).astype(BF16)
    for o in range(6):
        r2_snd[o] = flat[48 * o : 48 * o + 48]
    owner = 2 * px + pc
    owns2 = owner < 6
    row = [s for s in SLOTS if s[1] == 0]
    sheet = [s for s in SPACE if s[0] == 0 and s[2] == 0]
    for step in row:
        zz, jj = ahead(step)
        there = 2 * (jj >> 3) + (jj & 1)

        @pl.when(there < 6)
        def _():
            if any(step):
                remote(r2_snd.at[there], r2_rcv.at[owner], 10, (zz, jj))
            else:
                local(r2_snd.at[there], r2_rcv.at[owner], recv_sems.at[10])

    adj_normed = jnp.concatenate(
        [
            dot(bd[0, g * 128 : (g + 1) * 128, :], adjt[g * 128 : (g + 1) * 128].astype(BF16))
            for g in range(GROUPS)
        ],
        axis=0,
    )
    grad_mean = jnp.mean(adj_normed, axis=0, keepdims=True)
    grad_cross = jnp.mean(adj_normed * normed1[...], axis=0, keepdims=True)
    grad = (inverse1[0:1] * (adj_normed - grad_mean - normed1[...] * grad_cross)).T
    wait_all(recv_sems.at[5], ah_rcv)
    grad = ah_rcv[...].reshape(TOKENS, D).astype(F32) + grad
    vg[...] = grad.astype(BF16).reshape(2, 64, D)
    vg_out = pltpu.make_async_copy(vg, vg_ref, out_sems.at[0])
    vg_out.start()
    @pl.when(owns2)
    def _():
        wait_all(recv_sems.at[10], r2_rcv)
        own = 4 * z + py
        r2_z[own] = jnp.sum(r2_rcv[...].astype(F32), axis=0).astype(BF16)
        for step in sheet:
            remote(r2_z.at[own], r2_z.at[own], 11, ahead(step))

    wait_all(send_sems.at[0], vid_mid.at[pl.ds(0, 6)])
    wait_all(send_sems.at[1], ct_mid.at[pl.ds(0, 6)])
    wait_all(send_sems.at[2], qkv_snd.at[pl.ds(0, PWAYS - 1)])
    wait_all(send_sems.at[3], att_snd.at[pl.ds(0, PATCHES - 16)])
    wait_all(send_sems.at[4], do_rcv.at[pl.ds(0, PATCHES - 16)])
    wait_all(send_sems.at[5], ah_snd.at[pl.ds(0, 6)])
    wait_all(send_sems.at[6], dk_snd.at[pl.ds(0, PWAYS - 1)])
    wait_all(send_sems.at[15], dv_snd.at[pl.ds(0, PWAYS - 1)])
    wait_all(send_sems.at[13], dq_snd.at[pl.ds(0, PWAYS - 1)])
    wait_all(recv_sems.at[9], r1_out)
    @pl.when(owns2)
    def _():
        wait_all(recv_sems.at[11], r2_z.at[pl.ds(0, 15)])
        r2_chunk[...] = (jnp.sum(r2_z[...].astype(F32), axis=0) / 128.0).astype(BF16)
        dst = red_ref.at[pl.ds(pl.multiple_of(48 * owner, 16), 48)]
        for step in row:
            if any(step):
                remote(r2_chunk, dst, 12, ahead(step))
            else:
                local(r2_chunk, dst, recv_sems.at[12])

    tools = layout_tools()
    for n in range(3):
        lay_out(tools, r1_out[n * ROWS : (n + 1) * ROWS], terms.at[n])
    red1 = pltpu.make_async_copy(terms, terms_ref, out_sems.at[1])
    red1.start()
    reduce_sent(r1_snd, r1_rcv, r1_z, 27, owns1, 7)
    @pl.when(owns2)
    def _():
        wait_all(send_sems.at[10], r2_snd.at[pl.ds(0, 5)])
        wait_all(send_sems.at[11], r2_z.at[pl.ds(0, 15)])
        wait_all(send_sems.at[12], r2_rcv.at[pl.ds(0, 7)])

    @pl.when(jnp.logical_not(owns2))
    def _():
        wait_all(send_sems.at[10], r2_snd)

    wait_all(recv_sems.at[12], red_ref)
    red1.wait()
    vg_out.wait()


def unpack_kernel(sin_h, terms_h, vg_in, vg_out, sout, tin, tout, sin, packed, terms, vg, in_sems, out_sems):
    loads = [pltpu.make_async_copy(sin_h, packed, in_sems.at[0])]
    loads += [pltpu.make_async_copy(terms_h.at[n], terms.at[n], in_sems.at[n + 1]) for n in range(3)]
    loads.append(pltpu.make_async_copy(vg_in, vg, in_sems.at[4]))
    for copy in loads:
        copy.start()
    stores = [pltpu.make_async_copy(terms.at[n], out, out_sems.at[n]) for n, out in enumerate((sout, tin, tout, sin))]
    stores.append(pltpu.make_async_copy(vg, vg_out, out_sems.at[4]))
    tools = layout_tools()
    loads[0].wait()
    lay_out(tools, packed[...], terms.at[3])
    stores[3].start()
    for n, at in ((1, 0), (2, 1), (3, 2), (4, 4)):
        loads[n].wait()
        stores[at].start()
    for store in stores:
        store.wait()


def per_device(
    video,
    cotangent,
    frame_mask,
    spatial_project,
    spatial_output,
    temporal_project,
    temporal_output,
    spatial_inward,
    spatial_outward,
    temporal_inward,
    temporal_outward,
):
    vm = pltpu.VMEM
    dma = pltpu.SemaphoreType.DMA
    scratch = [
        vm((D, 3 * D), BF16), vm((D, D), BF16), vm((D, 3 * D), BF16), vm((D, D), BF16),
        vm((4, BLOCK, BLOCK, NBLOCK), F32), vm((D, 128), F32), vm((4, D, 128), BF16),
        vm((2, 64, D), BF16), vm((2, 64, D), BF16), vm((FRAMES, 16, D), BF16), vm((FRAMES, 16, D), BF16),
        vm((D, TOKENS), F32), vm((8, TOKENS), F32), vm((TOKENS, D), BF16), vm((TOKENS, 3 * D), F32),
        vm((PWAYS, 64, 256), BF16), vm((PATCHES, 256), BF16),
        vm((PATCHES, 128), BF16), vm((PATCHES, 128), BF16), vm((PATCHES, 128), BF16),
        vm((PATCHES, 128), BF16), vm((FRAMES, HEADS, 16, 128), BF16), vm((TOKENS, D), BF16),
        vm((TOKENS, D), F32), vm((TOKENS, D), BF16), vm((TOKENS, D + 128), BF16),
        vm((TOKENS, D), F32), vm((TOKENS, D), F32), vm((TOKENS, 3 * D), BF16),
        vm((TOKENS, D), BF16), vm((TOKENS, 3 * D), BF16),
        vm((HEADS, TOKENS, TOKENS), F32), vm((HEADS, TOKENS, TOKENS), F32),
        vm((HEADS, TOKENS, TOKENS), BF16), vm((HEADS, TOKENS, TOKENS), BF16),
        vm((FRAMES, 16, D), BF16), vm((2, 64, D), BF16),
        vm((FRAMES, HEADS, 16, 128), BF16), vm((PATCHES, 128), BF16),
        vm((80, PATCHES), BF16), vm((80, PATCHES), F32), vm((80, PATCHES), F32), vm((PATCHES, PATCHES), BF16),
        vm((PWAYS, 48, 128), BF16), vm((PWAYS, 48, 128), BF16), vm((PWAYS, 32, 128), BF16), vm((PWAYS, 32, 128), BF16),
        vm((PWAYS, 32, 128), BF16), vm((PWAYS, 32, 128), BF16), vm((8, PATCHES), F32), vm((2, D, 128), BF16),
        vm((2, 64, D), BF16),
        vm((3 * D, TOKENS), BF16), vm((D, TOKENS), F32),
        vm((27, 32, 128), BF16), vm((PWAYS, 32, 128), BF16), vm((ZWAYS, 32, 128), F32),
        vm((32, 128), BF16), vm((3 * ROWS, 128), BF16),
        vm((6, 48, 128), BF16), vm((8, 48, 128), BF16), vm((16, 48, 128), BF16),
        vm((48, 128), BF16), vm((3, BLOCK, BLOCK, NBLOCK), F32),
        dma((12,)), dma((3,)), dma((16,)), dma((16,)), dma((4,)), dma((4,)),
    ]
    anyspec = pl.BlockSpec(memory_space=pl.ANY)
    blocks = [r.transpose(1, 2, 0) for r in (spatial_inward, spatial_outward, temporal_inward, temporal_outward)]
    grad, terms, red = pl.pallas_call(
        kernel,
        out_shape=(
            jax.ShapeDtypeStruct((2, 64, D), BF16),
            jax.ShapeDtypeStruct((3, BLOCK, BLOCK, NBLOCK), F32),
            jax.ShapeDtypeStruct((ROWS, 128), BF16),
        ),
        in_specs=[pl.BlockSpec(memory_space=pltpu.SMEM)] + [anyspec] * 10,
        out_specs=(anyspec,) * 3,
        scratch_shapes=scratch,
        compiler_params=pltpu.CompilerParams(
            collective_id=0, has_side_effects=True, vmem_limit_bytes=62 * 1024 * 1024
        ),
        name="block_backward",
    )(
        frame_mask, video, cotangent, spatial_project, spatial_output, temporal_project, temporal_output,
        *blocks,
    )
    term = jax.ShapeDtypeStruct((BLOCK, BLOCK, NBLOCK), F32)
    grad, sout, tin, tout, sin = pl.pallas_call(
        unpack_kernel,
        out_shape=(jax.ShapeDtypeStruct((2, 64, D), BF16), term, term, term, term),
        in_specs=[anyspec] * 3,
        out_specs=(anyspec,) * 5,
        scratch_shapes=[
            vm((ROWS, 128), BF16), vm((4, BLOCK, BLOCK, NBLOCK), F32), vm((2, 64, D), BF16), dma((5,)), dma((5,)),
        ],
        compiler_params=pltpu.CompilerParams(vmem_limit_bytes=62 * 1024 * 1024),
        name="unpack_terms",
    )(red, terms, grad)
    sin, sout, tin, tout = (r.transpose(2, 0, 1) for r in (sin, sout, tin, tout))
    return grad, sin, sout, tin, tout


def solution(mesh):
    split = P("frame", "patch", None)
    in_specs = (split, split) + (P(),) * 9
    out_specs = (split,) + (P(),) * 4
    return jax.shard_map(
        per_device, mesh=mesh, in_specs=in_specs, out_specs=out_specs, check_vma=False
    )
```

```python
import itertools
import math

import jax
import jax.numpy as jnp
from jax import lax
from jax.experimental import pallas as pl
from jax.experimental.pallas import tpu as pltpu
from jax.sharding import PartitionSpec as P

D = 1152
HEADS = 16
HEAD_DIM = 72
BLOCK = 32
GROUPS = D // 128
FRAMES = 8
PATCHES = 2048
ZWAYS = 4
PWAYS = 32
DEVICES = ZWAYS * PWAYS
TOKENS = 128
ROWS = D // 4
NBLOCK = D // 32

EPSILON = 1e-06
NEGATIVE = -1e30
SCALE = 1.0 / math.sqrt(HEAD_DIM)
LOG2E = math.log2(math.e)
LN2 = math.log(2.0)

F32 = jnp.float32
BF16 = jnp.bfloat16
MESH = pl.DeviceIdType.MESH


def hops(step):
    return min(step[0], 4 - step[0]) + min(step[1], 4 - step[1]) + min(step[3], 4 - step[3])


PLANE = sorted(
    [s for s in itertools.product(range(4), range(4), range(2), [0]) if any(s)], key=lambda s: -hops(s)
)
SPACE = sorted(
    [s for s in itertools.product(range(4), range(4), range(2), range(4)) if any(s)],
    key=lambda s: -hops(s),
)
SLOTS = PLANE + [(0, 0, 0, 0)]
SLOT_OF = {s[:3]: n for n, s in enumerate(SLOTS)}


def dot(a, b):
    return lax.dot_general(a, b, (((1,), (0,)), ((), ())), preferred_element_type=F32)


def dot_nt(a, b):
    return lax.dot_general(a, b, (((1,), (1,)), ((), ())), preferred_element_type=F32)


def dot_tn(a, b):
    return lax.dot_general(a, b, (((0,), (0,)), ((), ())), preferred_element_type=F32)


def lanes(shape):
    return lax.broadcasted_iota(jnp.int32, shape, len(shape) - 1)


def rows(shape):
    return lax.broadcasted_iota(jnp.int32, shape, 0)


def roll(x, amount):
    amount = amount % 128
    return x if amount == 0 else pltpu.roll(x, amount, 1)


def normalize(x):
    centered = x - jnp.mean(x, axis=-1, keepdims=True)
    inverse = lax.rsqrt(jnp.mean(centered * centered, axis=-1, keepdims=True) + EPSILON)
    return centered * inverse, inverse


def normalize_backward(adjoint, normed, inverse):
    grad_mean = jnp.mean(adjoint, axis=-1, keepdims=True)
    grad_cross = jnp.mean(adjoint * normed, axis=-1, keepdims=True)
    return inverse * (adjoint - grad_mean - normed * grad_cross)


def group(x, g):
    return x[:, g * 128 : (g + 1) * 128]


def rotate(x, blocks):
    return jnp.concatenate(
        [dot(group(x, g), blocks[g * 128 : (g + 1) * 128, :]) for g in range(GROUPS)], axis=1
    )


def rotate_transposed(x, blocks):
    return jnp.concatenate(
        [dot_nt(group(x, g), blocks[g * 128 : (g + 1) * 128, :]) for g in range(GROUPS)], axis=1
    )


def block_mask(shape):
    return (rows(shape) // BLOCK) % 4 == lanes(shape) // BLOCK


def rotation_gradient(left, right):
    mask = block_mask((128, 128))
    packed = []
    for g in range(GROUPS):
        full = jnp.where(mask, dot_tn(group(left, g), group(right, g)), 0.0)
        packed.append(full[0:32] + full[32:64] + full[64:96] + full[96:128])
    return packed


def layout_tools():
    shape = (BLOCK, 40, ROWS)
    b = lax.broadcasted_iota(jnp.int32, shape, 0)
    n = lax.broadcasted_iota(jnp.int32, shape, 1)
    from_row = lax.broadcasted_iota(jnp.int32, shape, 2)
    pick = jnp.where(from_row == (n >> 2) * BLOCK + b, 1.0, 0.0).reshape(BLOCK * 40, ROWS).astype(BF16)
    shape = (BLOCK, 40, 128)
    n = lax.broadcasted_iota(jnp.int32, shape, 1)
    own = ((n & 3) == (lax.broadcasted_iota(jnp.int32, shape, 2) >> 5)).reshape(BLOCK * 40, 128)
    repeat = jnp.where(lanes((128, 128)) % BLOCK == rows((128, 128)) % BLOCK, 1.0, 0.0).astype(BF16)
    return pick, own, repeat


def lay_out(tools, term, out):
    pick, own, repeat = tools
    lane = lanes((40, 128)) >> 5
    wide = dot(pick, term)
    wide = dot(jnp.where(own, wide, 0.0).astype(BF16), repeat)
    for m in range(8):
        four = jnp.zeros((40, 128), F32)
        for s in range(4):
            at = (4 * m + s) * 40
            four = jnp.where(lane == s, wide[at : at + 40], four)
        out[4 * m : 4 * m + 4] = four.T[:, 0:NBLOCK].reshape(4, BLOCK, NBLOCK)


def kernel(
    mask_ref, video, cotangent, wsp_h, wso_h, wtp_h, wto_h, rsi_h, rso_h, rti_h, rto_h,
    vg_ref, terms_ref, red_ref,
    wsp, wso, wtp, wto, r4, bd32, bd,
    vid, cot, vid_mid, ct_mid,
    normed1, inverse1, rot_b, proj,
    qkv_snd, qkv_rcv, beside_snd, fold, kx, qx, vx,
    att_snd, att_rcv, att1, top, aot, daz,
    hidp, normed2, proj2, att2_b, dproj_b,
    t_s, t_dp, t_p, t_ds,
    ah_snd, ah_rcv, do_snd, do_rcv, qt, dvt, pq,
    dk_snd, dk_rcv, dv_snd, dv_rcv, dq_snd, dq_rcv, dq_last, w_last, vg, dpt, adjt,
    r1_snd, r1_rcv, r1_z, r1_chunk, r1_out,
    r2_snd, r2_rcv, r2_z, r2_chunk, terms,
    load_sems, out_sems, send_sems, recv_sems, qkv_sems, do_sems,
):
    z = lax.axis_index("frame")
    j = lax.axis_index("patch")
    px, py, pc = j >> 3, (j >> 1) & 3, j & 1
    xs = [((px + d) & 3) * 8 for d in range(4)]
    ys = [((py + d) & 3) * 2 for d in range(4)]
    cs = [(pc + d) & 1 for d in range(2)]
    zs = [(z + d) & 3 for d in range(4)]
    xys = [[a + b for b in ys] for a in xs]

    def ahead(step):
        return zs[step[3]], xys[step[0]][step[1]] + cs[step[2]]

    def behind(step):
        return zs[-step[3] & 3], xys[-step[0] & 3][-step[1] & 3] + cs[step[2]]

    def load(src, dst, n):
        return pltpu.make_async_copy(src, dst, load_sems.at[n])

    early = [load(video, vid, 0), load(rsi_h, r4.at[0], 1)]
    early += [
        load(wsp_h.at[:, pl.ds(c * D, D)], wsp.at[:, pl.ds(c * D, D)], n) for c, n in enumerate((2, 10, 11))
    ]
    late = [
        load(cotangent, cot, 3), load(rso_h, r4.at[1], 4), load(rti_h, r4.at[2], 5),
        load(rto_h, r4.at[3], 6), load(wto_h, wto, 7), load(wso_h, wso, 8), load(wtp_h, wtp, 9),
    ]
    for copy in early:
        copy.start()

    barrier = pltpu.get_barrier_semaphore()
    near = PLANE + [(0, 0, 0, d) for d in (2, 1, 3)]
    for step in near:
        pl.semaphore_signal(barrier, inc=1, device_id=ahead(step), device_id_type=MESH)

    def local(src, dst, sem):
        pltpu.make_async_copy(src, dst, sem).start()

    def remote(src, dst, phase, there, recv_sem=None):
        pltpu.make_async_remote_copy(
            src_ref=src, dst_ref=dst, send_sem=send_sems.at[phase],
            recv_sem=recv_sems.at[phase] if recv_sem is None else recv_sem,
            device_id=there, device_id_type=MESH,
        ).start()

    def wait_all(sem, buffer):
        pltpu.make_async_copy(buffer, buffer, sem).wait()

    def make_blocks(index):
        shape = (128, 512)
        spread = jnp.where(
            jnp.logical_and(
                rows(shape) // BLOCK == lanes(shape) // 128, rows(shape) % BLOCK == lanes(shape) % BLOCK
            ),
            1.0, 0.0,
        ).astype(BF16)
        shape = (NBLOCK, 128)
        own = rows(shape) % 4 == lanes(shape) // BLOCK
        for m in range(8):
            four = r4[index, 4 * m : 4 * m + 4].reshape(128, NBLOCK).astype(BF16)
            wide = dot_tn(four, spread)
            for s in range(4):
                bd32[pl.ds(4 * m + s, NBLOCK, stride=BLOCK), :] = jnp.where(own, group(wide, s), 0.0)
        bd[index] = bd32[...].astype(BF16)

    shape = (512, 384)
    source, target = rows(shape), lanes(shape)
    quarter, lane_in = source >> 7, source & 127
    to_pair = jnp.where(lane_in < 64, (quarter & 1) * 128 + (quarter >> 1) * 64 + lane_in, -1)
    to_last = jnp.where(jnp.logical_and(lane_in >= 64, lane_in < 88), 256 + quarter * 32 + lane_in - 64, -1)
    hit = jnp.logical_or(target == to_pair, target == to_last)
    fold[...] = jnp.where(hit, 1.0, 0.0).astype(BF16)

    early[0].wait()
    normed, _ = normalize(vid[...].reshape(TOKENS, D).astype(F32))
    early[1].wait()
    make_blocks(0)
    rot_b[...] = rotate(normed.astype(BF16), bd.at[0]).astype(BF16)

    for c in range(3):
        at = slice(c * D, (c + 1) * D)
        early[2 + c].wait()
        proj[:, at] = dot(rot_b[...], wsp[:, at])
    for copy in late:
        copy.start()

    lane = lanes((TOKENS, 128))
    qscale = jnp.where(lane < HEAD_DIM, SCALE * LOG2E, 1.0)
    for h in range(HEADS):
        t, off = (HEAD_DIM * h) // 128, (HEAD_DIM * h) % 128

        def pick(section, to):
            first = proj[:, section * D + t * 128 : section * D + (t + 1) * 128]
            if off + HEAD_DIM > 128:
                second = proj[:, section * D + (t + 1) * 128 : section * D + (t + 2) * 128]
                first = jnp.where(lane >= off, first, second)
            return roll(first, to - off)

        q, k, v = pick(0, 0), pick(1, 72), pick(2, 16)
        low = (jnp.where(lane < 72, q, k) * qscale).astype(BF16)
        high = jnp.where(lane < 16, k, jnp.where(lane < 88, v, 0.0)).astype(BF16)
        for f in range(2):
            item = f * HEADS + h
            qkv_snd[item, 0:64] = low[64 * f : 64 * (f + 1)]
            for e in range(4):
                at = 64 * f + 16 * e
                beside_snd[16 * item : 16 * item + 16, 128 * e : 128 * e + 128] = high[at : at + 16]
    folded = dot(beside_snd[...], fold[...]).astype(BF16)
    for part in range(3):
        qkv_snd[:, 64 + 16 * part : 80 + 16 * part] = group(folded, part).reshape(PWAYS, 16, 128)

    pl.semaphore_wait(barrier, len(near))

    for n, step in enumerate(SLOTS):
        dst = qkv_rcv.at[n]
        if any(step):
            zz, jj = ahead(step)
            remote(qkv_snd.at[jj], dst, 2, (zz, jj), qkv_sems.at[n // 8])
        else:
            local(qkv_snd.at[j], dst, qkv_sems.at[n // 8])

    late[0].wait()
    for phase, src, dst in ((1, cot, ct_mid), (0, vid, vid_mid)):
        for d in (2, 1, 3, 0):
            for f in range(2):
                piece = src.at[f, pl.ds(pl.multiple_of(zs[d] * 16, 16), 16)]
                if d:
                    remote(piece, dst.at[2 * z + f], phase, (zs[d], j))
                else:
                    local(piece, dst.at[2 * z + f], recv_sems.at[phase])

    for n in (1, 2, 3):
        late[n].wait()
        make_blocks(n)

    columns = vid[...].reshape(TOKENS, D).astype(F32).T
    columns = columns - jnp.mean(columns, axis=0, keepdims=True)
    inverse = lax.rsqrt(jnp.mean(columns * columns, axis=0, keepdims=True) + EPSILON)
    normed1[...] = columns * inverse
    inverse1[...] = jnp.broadcast_to(inverse, (8, 128))

    shape = (D, 128)
    column = HEAD_DIM * (lanes(shape) >> 3) + 64 + (lanes(shape) & 7)
    select = jnp.where(rows(shape) == column, 1.0, 0.0).astype(BF16)
    for n, section in enumerate((0, 2)):
        w_last[n] = dot(wsp[:, section * D : (section + 1) * D], select).astype(BF16)

    wait_all(recv_sems.at[1], ct_mid)
    frame_row = rows((TOKENS, 1)) // 16
    valid = jnp.zeros((TOKENS, 1), F32)
    for f in range(FRAMES):
        valid = jnp.where(frame_row == f, mask_ref[f].astype(F32), valid)
    top[...] = ct_mid[...].reshape(TOKENS, D).astype(F32) * valid
    late[4].wait()
    aot[...] = dot_nt(top[...].astype(BF16), wto[...]).astype(BF16)
    daz[:, 0:D] = rotate_transposed(aot[...], bd.at[3]).astype(BF16)
    daz[:, D:] = jnp.zeros((TOKENS, 128), BF16)

    lane2 = lanes((256, 128))
    ones = jnp.where(jnp.logical_and(lane2 >= 72, lane2 < 76), 1.0, 0.0)

    def prepare(i, carry):
        at = pl.ds(pl.multiple_of(i * 256, 256), 256)
        low, high = [], []
        for m in range(4):
            slot = qkv_rcv[4 * i + m].astype(F32)
            low.append(slot[0:64])
            mid, last = slot[64:96], slot[96:112]
            high.append(
                jnp.where(
                    lanes((64, 128)) < 64,
                    jnp.concatenate([mid, roll(mid, 64)], axis=0),
                    jnp.concatenate([roll(last, 64 - 32 * e) for e in range(4)], axis=0),
                )
            )
        t0, t1 = jnp.concatenate(low, axis=0), jnp.concatenate(high, axis=0)
        k = roll(jnp.where(lane2 >= 72, t0, t1), -72)
        kx[at, :] = jnp.where(lane2 < 72, k, ones).astype(BF16)
        vx[at, :] = jnp.where(lane2 < 72, roll(t1, -16), ones).astype(BF16)
        qx[at, :] = jnp.where(lane2 < 72, t0, 0.0).astype(BF16)
        return carry

    for g in range(4):
        wait_all(qkv_sems.at[g], qkv_rcv.at[pl.ds(8 * g, 8)])
        lax.fori_loop(2 * g, 2 * g + 2, prepare, 0)

    def attend_span(start, count):
        spans = [pl.ds(start + s * 256, 256) for s in range(count)]
        highs = []
        for s, at in enumerate(spans):
            scores = dot_nt(qx[at, :], kx[...])
            highs.append(jnp.max(scores, axis=-1, keepdims=True))
            pq[256 * s : 256 * s + 256, :] = jnp.exp2(scores - highs[-1]).astype(BF16)
        both_out = dot(pq[0 : 256 * count, :], vx[...])
        for s, (at, high_score) in enumerate(zip(spans, highs)):
            out = both_out[256 * s : 256 * s + 256]
            total = out[:, 72:73]
            att_snd[at, :] = jnp.where(lane2 < 72, out / total, 0.0).astype(BF16)
            neg = -(high_score + jnp.log(total) * LOG2E)
            hi = neg.astype(BF16).astype(F32)
            mid = (neg - hi).astype(BF16).astype(F32)
            lo = neg - hi - mid
            old = qx[at, :].astype(F32)
            new = jnp.where(
                lane2 == 72, hi, jnp.where(lane2 == 73, mid, jnp.where(lane2 == 74, lo, old))
            )
            qx[at, :] = new.astype(BF16)

    def send_attended(slots):
        for n in slots:
            for d in (2, 1, 3, 0):
                zz, jj = zs[d], behind(SLOTS[n])[1]
                src = att_snd.at[pl.ds(pl.multiple_of(64 * n + 16 * zz, 16), 16)]
                dst = att_rcv.at[2 * z + (j >> 4), j & 15]
                if d or any(SLOTS[n]):
                    remote(src, dst, 3, (zz, jj))
                else:
                    local(src, dst, recv_sems.at[3])

    def attend(i, carry):
        attend_span(pl.multiple_of(i * 512, 512), 2)
        for ii in range(1, 4):

            @pl.when(i == ii)
            def _():
                send_attended(range(8 * ii, 8 * ii + 8))

        return carry

    for half in range(2):
        attend_span(256 * half, 1)
        send_attended(range(4 * half, 4 * half + 4))
    lax.fori_loop(1, 4, attend, 0)

    wait_all(recv_sems.at[0], vid_mid)
    wait_all(recv_sems.at[3], att_rcv)

    def add_piece(tiles, at, piece):
        tiles[at] = piece if tiles[at] is None else tiles[at] + piece

    def place(tiles, h, value):
        t, off = (HEAD_DIM * h) // 128, (HEAD_DIM * h) % 128
        if off + HEAD_DIM > 128:
            add_piece(tiles, t, jnp.where(lane >= off, value, 0.0))
            add_piece(tiles, t + 1, jnp.where(lane < off, value, 0.0))
        else:
            add_piece(tiles, t, value)

    tiles = [None] * GROUPS
    for h in range(HEADS):
        place(tiles, h, roll(att_rcv[:, h].reshape(TOKENS, 128).astype(F32), (HEAD_DIM * h) % 128))
    for t in range(GROUPS):
        att1[:, t * 128 : (t + 1) * 128] = tiles[t].astype(BF16)

    late[5].wait()
    outrot = rotate(att1[...], bd.at[1]).astype(BF16)
    hidden = vid_mid[...].reshape(TOKENS, D).astype(F32) + dot(outrot, wso[...])
    hidden = hidden.astype(BF16).astype(F32)
    normed, inverse2 = normalize(hidden)
    normed2[...] = normed
    rot_b[...] = rotate(normed.astype(BF16), bd.at[2]).astype(BF16)
    late[6].wait()

    def project2(c, carry):
        at = pl.ds(pl.multiple_of(c * D, 128), D)
        proj2[:, at] = dot(rot_b[...], wtp[:, at]).astype(BF16)
        return carry

    lax.fori_loop(0, 3, project2, 0)

    square = (TOKENS, TOKENS)
    same_patch = rows(square) % 16 == lanes(square) % 16
    same_frame = rows(square) // 16 == lanes(square) // 16
    key_valid = jnp.zeros(square, F32)
    for f in range(FRAMES):
        key_valid = jnp.where(rows(square) // 16 == f, mask_ref[f].astype(F32), key_valid)
    allowed = jnp.logical_and(same_patch, jnp.logical_or(key_valid == 1.0, same_frame))
    bias = jnp.where(allowed, 0.0, NEGATIVE)

    def window(h, section):
        t, off = (HEAD_DIM * h) // 128, (HEAD_DIM * h) % 128
        width = 256 if off + HEAD_DIM > 128 else 128
        return slice(section * D + t * 128, section * D + t * 128 + width)

    def own_lanes(h):
        off = (HEAD_DIM * h) % 128
        l = lanes((1, 256 if off + HEAD_DIM > 128 else 128))
        return jnp.where(jnp.logical_and(l >= off, l < off + HEAD_DIM), 1.0, 0.0)

    for h in range(HEADS):
        own = own_lanes(h).astype(BF16)
        t_s[h] = dot_nt(proj2[:, window(h, 1)], proj2[:, window(h, 0)] * own)
        t_dp[h] = dot_nt(proj2[:, window(h, 2)], daz[:, window(h, 0)] * own)

    for h in range(HEADS):
        scores = t_s[h] * SCALE + bias
        e = jnp.exp(scores - jnp.max(scores, axis=0, keepdims=True))
        p = e * (1.0 / jnp.sum(e, axis=0, keepdims=True))
        dp = t_dp[h]
        t_p[h] = p.astype(BF16)
        t_ds[h] = (p * (dp - jnp.sum(p * dp, axis=0, keepdims=True))).astype(BF16)

    def gather(section, dst, base):
        tiles = [None] * (GROUPS + 1)
        for h in range(HEADS):
            own = own_lanes(h)
            own_b = own.astype(BF16)
            if section == 0:
                part = dot_tn(t_ds[h], proj2[:, window(h, 1)]) * (own * SCALE)
            elif section == 1:
                part = dot(t_ds[h], proj2[:, window(h, 0)] * own_b) * SCALE
            elif section == 2:
                part = dot(t_p[h], daz[:, window(h, 0)] * own_b)
            else:
                part = dot_tn(t_p[h], proj2[:, window(h, 2)]) * own
            t = (HEAD_DIM * h) // 128
            for w in range(part.shape[1] // 128):
                add_piece(tiles, t + w, group(part, w))
        for t in range(GROUPS):
            dst[:, base + t * 128 : base + (t + 1) * 128] = tiles[t].astype(BF16)

    for section in range(3):
        gather(section, dproj_b, section * D)

    for c in range(3):
        at = slice(c * 384, (c + 1) * 384)
        hidp[:, at] = dot_nt(dproj_b[...], wtp[at, :])
    adj_rot2 = hidp[...].astype(BF16)
    adj_normed = rotate_transposed(adj_rot2, bd.at[2])
    adj_hidden = top[...] + normalize_backward(adj_normed, normed2[...], inverse2)
    adj_hidden_b = adj_hidden.astype(BF16)
    ah_snd[...] = adj_hidden_b.reshape(FRAMES, 16, D)
    aho = dot_nt(adj_hidden_b, wso[...]).astype(BF16)
    adj_att1 = rotate_transposed(aho, bd.at[1])
    for h in range(HEADS):
        t, off = (HEAD_DIM * h) // 128, (HEAD_DIM * h) % 128
        first = group(adj_att1, t)
        if off + HEAD_DIM > 128:
            first = jnp.where(lane >= off, first, group(adj_att1, t + 1))
        piece = jnp.where(lane < 72, roll(first, -off), 0.0).astype(BF16)
        do_snd[:, h] = piece.reshape(FRAMES, 16, 128)

    for step in [slot[:3] + (d,) for slot in SLOTS for d in (2, 1, 3, 0)]:
        zz, jj = ahead(step)
        src = do_snd.at[2 * zz + (jj >> 4), jj & 15]
        n = SLOT_OF[step[:3]]
        dst = do_rcv.at[pl.ds(pl.multiple_of(64 * n + 16 * z, 16), 16)]
        if any(step):
            remote(src, dst, 4, (zz, jj), do_sems.at[n // 8])
        else:
            local(src, dst, do_sems.at[n // 8])
    for d in (2, 1, 3, 0):
        for f in range(2):
            src = ah_snd.at[2 * zs[d] + f]
            dst = ah_rcv.at[f, pl.ds(pl.multiple_of(z * 16, 16), 16)]
            if d:
                remote(src, dst, 5, (zs[d], j))
            else:
                local(src, dst, recv_sems.at[5])

    gather(3, att2_b, 0)
    for n, packed in enumerate((
        rotation_gradient(att1[...], aho),
        rotation_gradient(normed2[...].astype(BF16), adj_rot2),
        rotation_gradient(att2_b[...], aot[...]),
    )):
        for g in range(GROUPS):
            r1_snd[n * GROUPS + g] = packed[g].astype(BF16)

    def reduce_first(snd, rcv, chunk_of, owns, phase):
        for step in SLOTS:
            zz, jj = ahead(step)

            @pl.when(owns(jj))
            def _():
                if any(step):
                    remote(snd.at[chunk_of(jj)], rcv.at[j], phase, (zz, jj))
                else:
                    local(snd.at[chunk_of(jj)], rcv.at[j], recv_sems.at[phase])

    def reduce_second(rcv, zbuf, owns, phase):
        @pl.when(owns(j))
        def _():
            wait_all(recv_sems.at[phase], rcv)
            zbuf[z] = jnp.sum(rcv[...].astype(F32), axis=0)
            for d in (2, 1, 3):
                remote(zbuf.at[z], zbuf.at[z], phase + 1, (zs[d], j))

    def reduce_third(zbuf, chunk, out, chunk_of, owns, phase):
        size = chunk.shape[0]

        @pl.when(owns(j))
        def _():
            wait_all(recv_sems.at[phase + 1], zbuf.at[pl.ds(0, ZWAYS - 1)])
            chunk[...] = (((zbuf[0] + zbuf[1]) + (zbuf[2] + zbuf[3])) / 128.0).astype(BF16)
            dst = out.at[pl.ds(pl.multiple_of(chunk_of(j) * size, size), size)]
            for step in SLOTS:
                if any(step):
                    remote(chunk, dst, phase + 2, ahead(step))
                else:
                    local(chunk, dst, recv_sems.at[phase + 2])

    def reduce_sent(snd, rcv, zbuf, owners, owns, phase):
        @pl.when(owns(j))
        def _():
            wait_all(send_sems.at[phase], snd.at[pl.ds(0, owners - 1)])
            wait_all(send_sems.at[phase + 1], zbuf.at[pl.ds(0, ZWAYS - 1)])
            wait_all(send_sems.at[phase + 2], rcv.at[pl.ds(0, PWAYS - 1)])

        @pl.when(jnp.logical_not(owns(j)))
        def _():
            wait_all(send_sems.at[phase], snd)

    def chunk1(jj):
        return jj

    def owns1(jj):
        return jj < 27

    reduce_first(r1_snd, r1_rcv, chunk1, owns1, 7)

    def probabilities(i, carry):
        for s in range(2):
            at = pl.ds(pl.multiple_of(i * 512 + s * 256, 256), 256)
            pq[at, :] = jnp.exp2(dot_nt(qx[at, :], kx[...])).astype(BF16)
        return carry

    lax.fori_loop(0, 4, probabilities, 0)

    def prepare_queries(i, carry):
        at = pl.ds(pl.multiple_of(i * 256, 256), 256)
        qt[:, at] = qx[at, :].astype(F32).T[0:80].astype(BF16)
        return carry

    lax.fori_loop(0, 8, prepare_queries, 0)

    def beside(left, right, odd):
        left, right = (roll(left, 64), right) if odd else (left, roll(right, 64))
        return jnp.where(lanes(left.shape) < 64, left, right)

    def value_gradient(group_):
        at = pl.ds(group_ * 512, 512)
        dv = dot(do_rcv[at, :].astype(F32).T[0:80].astype(BF16), pq[at, :])
        if group_ == 0:
            dvt[...] = dv
        else:
            dvt[...] += dv

    def attend_back(group_):
        at = pl.ds(group_ * 512, 512)
        lane5 = lanes((512, 128))
        g = do_rcv[at, :].astype(F32)
        delta = -jnp.sum(g * att_snd[at, :].astype(F32), axis=-1, keepdims=True)
        hi = delta.astype(BF16).astype(F32)
        lo = delta - hi
        dox = jnp.where(lane5 == 72, hi, jnp.where(lane5 == 73, lo, g)).astype(BF16)
        ds = (pq[at, :].astype(F32) * dot_nt(dox, vx[...])).astype(BF16)
        dq = dot(ds, kx[...]).T * SCALE
        for m in range(8):
            tile = dq[:, 128 * (m // 2) : 128 * (m // 2) + 128]
            dq_snd[8 * group_ + m] = beside(tile[0:32], tile[32:64], m % 2).astype(BF16)
        dq_last[:, group_ * 512 : group_ * 512 + 512] = dq[64:72]
        pq[at, :] = ds
        send_back(dq_snd, dq_rcv, 13, range(8 * group_, 8 * group_ + 8))

    def send_back(snd, rcv, phase, slots):
        for n in slots:
            if any(SLOTS[n]):
                remote(snd.at[n], rcv.at[j], phase, behind(SLOTS[n]))
            else:
                local(snd.at[n], rcv.at[j], recv_sems.at[phase])

    for group_ in range(4):
        wait_all(do_sems.at[group_], do_rcv.at[pl.ds(512 * group_, 512)])
        value_gradient(group_)
        if group_ == 0:
            attend_back(0)
    for n in range(PWAYS):
        at = slice(128 * (n // 2), 128 * (n // 2) + 128)
        dv_snd[n] = beside(dvt[0:32, at], dvt[32:64, at], n % 2).astype(BF16)
    send_back(dv_snd, dv_rcv, 15, range(PWAYS))
    for group_ in (1, 2, 3):
        attend_back(group_)

    def key_gradient(group_):
        return dot(qt[...], pq[:, 512 * group_ : 512 * group_ + 512]) * LN2

    dk = key_gradient(0)
    for group_ in range(4):
        following = key_gradient(group_ + 1) if group_ < 3 else None
        for m in range(8):
            n = 8 * group_ + m
            at, here = slice(128 * (n // 2), 128 * (n // 2) + 128), slice(128 * (m // 2), 128 * (m // 2) + 128)
            rest = [dk[48:72, here], dq_last[:, at], dvt[64:72, at], jnp.zeros((8, 128), F32)]
            dk_snd[n] = beside(dk[0:48, here], jnp.concatenate(rest, axis=0), n % 2).astype(BF16)
        send_back(dk_snd, dk_rcv, 6, range(8 * group_, 8 * group_ + 8))
        dk = following

    reduce_second(r1_rcv, r1_z, owns1, 7)

    def halves(buffer, h):
        one, two = buffer[h].astype(F32), buffer[HEADS + h].astype(F32)
        first = lanes(one.shape) < 64
        return jnp.where(first, one, roll(two, 64)), jnp.where(first, roll(one, 64), two)

    def unpack_first(buffer, base):
        for pair in range(HEADS // 2):
            parts = []
            for h in (2 * pair, 2 * pair + 1):
                parts += [*halves(buffer, h), jnp.zeros((8, 128), F32)]
            at = base + 144 * pair
            dpt[at : at + 144] = jnp.concatenate(parts, axis=0).astype(BF16)

    wait_all(recv_sems.at[15], dv_rcv)
    unpack_first(dv_rcv, 2 * D)
    for c in range(3):
        at = slice(c * 384, (c + 1) * 384)
        adjt[at] = dot(wsp[at, 2 * D :], dpt[2 * D :])
    wait_all(recv_sems.at[13], dq_rcv)
    unpack_first(dq_rcv, 0)
    for c in range(3):
        at = slice(c * 384, (c + 1) * 384)
        adjt[at] += dot(wsp[at, 0:D], dpt[0:D])
    reduce_third(r1_z, r1_chunk, r1_out, chunk1, owns1, 7)
    wait_all(recv_sems.at[6], dk_rcv)

    last = [[], []]
    for pair in range(HEADS // 2):
        parts = []
        for h in (2 * pair, 2 * pair + 1):
            left, right = halves(dk_rcv, h)
            parts += [left, right[0:24]]
            last[0].append(right[24:32])
            last[1].append(right[32:40])
        at = D + 144 * pair
        dpt[at : at + 144] = jnp.concatenate(parts, axis=0).astype(BF16)
    last = [jnp.concatenate(parts, axis=0).astype(BF16) for parts in last]

    for c in range(3):
        at = slice(c * 384, (c + 1) * 384)
        adjt[at] += (
            dot(wsp[at, D : 2 * D], dpt[D : 2 * D]) + dot(w_last[0, at], last[0]) + dot(w_last[1, at], last[1])
        )
    packed = []
    mask = block_mask((128, 128))
    for g in range(GROUPS):
        at = slice(g * 128, (g + 1) * 128)
        full = jnp.where(mask, dot_nt(normed1[at].astype(BF16), adjt[at].astype(BF16)), 0.0)
        packed.append(full[0:32] + full[32:64] + full[64:96] + full[96:128])
    flat = jnp.concatenate(packed, axis=0).astype(BF16)
    for o in range(6):
        r2_snd[o] = flat[48 * o : 48 * o + 48]
    owner = 2 * px + pc
    owns2 = owner < 6
    row = [s for s in SLOTS if s[1] == 0]
    sheet = [s for s in SPACE if s[0] == 0 and s[2] == 0]
    for step in row:
        zz, jj = ahead(step)
        there = 2 * (jj >> 3) + (jj & 1)

        @pl.when(there < 6)
        def _():
            if any(step):
                remote(r2_snd.at[there], r2_rcv.at[owner], 10, (zz, jj))
            else:
                local(r2_snd.at[there], r2_rcv.at[owner], recv_sems.at[10])

    adj_normed = jnp.concatenate(
        [
            dot(bd[0, g * 128 : (g + 1) * 128, :], adjt[g * 128 : (g + 1) * 128].astype(BF16))
            for g in range(GROUPS)
        ],
        axis=0,
    )
    grad_mean = jnp.mean(adj_normed, axis=0, keepdims=True)
    grad_cross = jnp.mean(adj_normed * normed1[...], axis=0, keepdims=True)
    grad = (inverse1[0:1] * (adj_normed - grad_mean - normed1[...] * grad_cross)).T
    wait_all(recv_sems.at[5], ah_rcv)
    grad = ah_rcv[...].reshape(TOKENS, D).astype(F32) + grad
    vg[...] = grad.astype(BF16).reshape(2, 64, D)
    vg_out = pltpu.make_async_copy(vg, vg_ref, out_sems.at[0])
    vg_out.start()
    @pl.when(owns2)
    def _():
        wait_all(recv_sems.at[10], r2_rcv)
        own = 4 * z + py
        r2_z[own] = jnp.sum(r2_rcv[...].astype(F32), axis=0).astype(BF16)
        for step in sheet:
            remote(r2_z.at[own], r2_z.at[own], 11, ahead(step))

    wait_all(send_sems.at[0], vid_mid.at[pl.ds(0, 6)])
    wait_all(send_sems.at[1], ct_mid.at[pl.ds(0, 6)])
    wait_all(send_sems.at[2], qkv_snd.at[pl.ds(0, PWAYS - 1)])
    wait_all(send_sems.at[3], att_snd.at[pl.ds(0, PATCHES - 16)])
    wait_all(send_sems.at[4], do_rcv.at[pl.ds(0, PATCHES - 16)])
    wait_all(send_sems.at[5], ah_snd.at[pl.ds(0, 6)])
    wait_all(send_sems.at[6], dk_snd.at[pl.ds(0, PWAYS - 1)])
    wait_all(send_sems.at[15], dv_snd.at[pl.ds(0, PWAYS - 1)])
    wait_all(send_sems.at[13], dq_snd.at[pl.ds(0, PWAYS - 1)])
    wait_all(recv_sems.at[9], r1_out)
    @pl.when(owns2)
    def _():
        wait_all(recv_sems.at[11], r2_z.at[pl.ds(0, 15)])
        r2_chunk[...] = (jnp.sum(r2_z[...].astype(F32), axis=0) / 128.0).astype(BF16)
        dst = red_ref.at[pl.ds(pl.multiple_of(48 * owner, 16), 48)]
        for step in row:
            if any(step):
                remote(r2_chunk, dst, 12, ahead(step))
            else:
                local(r2_chunk, dst, recv_sems.at[12])

    tools = layout_tools()
    for n in range(3):
        lay_out(tools, r1_out[n * ROWS : (n + 1) * ROWS], terms.at[n])
    red1 = pltpu.make_async_copy(terms, terms_ref, out_sems.at[1])
    red1.start()
    reduce_sent(r1_snd, r1_rcv, r1_z, 27, owns1, 7)
    @pl.when(owns2)
    def _():
        wait_all(send_sems.at[10], r2_snd.at[pl.ds(0, 5)])
        wait_all(send_sems.at[11], r2_z.at[pl.ds(0, 15)])
        wait_all(send_sems.at[12], r2_rcv.at[pl.ds(0, 7)])

    @pl.when(jnp.logical_not(owns2))
    def _():
        wait_all(send_sems.at[10], r2_snd)

    wait_all(recv_sems.at[12], red_ref)
    red1.wait()
    vg_out.wait()


def unpack_kernel(sin_h, terms_h, vg_in, vg_out, sout, tin, tout, sin, packed, terms, vg, in_sems, out_sems):
    loads = [pltpu.make_async_copy(sin_h, packed, in_sems.at[0])]
    loads += [pltpu.make_async_copy(terms_h.at[n], terms.at[n], in_sems.at[n + 1]) for n in range(3)]
    loads.append(pltpu.make_async_copy(vg_in, vg, in_sems.at[4]))
    for copy in loads:
        copy.start()
    stores = [pltpu.make_async_copy(terms.at[n], out, out_sems.at[n]) for n, out in enumerate((sout, tin, tout, sin))]
    stores.append(pltpu.make_async_copy(vg, vg_out, out_sems.at[4]))
    tools = layout_tools()
    loads[0].wait()
    lay_out(tools, packed[...], terms.at[3])
    stores[3].start()
    for n, at in ((1, 0), (2, 1), (3, 2), (4, 4)):
        loads[n].wait()
        stores[at].start()
    for store in stores:
        store.wait()


def per_device(
    video,
    cotangent,
    frame_mask,
    spatial_project,
    spatial_output,
    temporal_project,
    temporal_output,
    spatial_inward,
    spatial_outward,
    temporal_inward,
    temporal_outward,
):
    vm = pltpu.VMEM
    dma = pltpu.SemaphoreType.DMA
    scratch = [
        vm((D, 3 * D), BF16), vm((D, D), BF16), vm((D, 3 * D), BF16), vm((D, D), BF16),
        vm((4, BLOCK, BLOCK, NBLOCK), F32), vm((D, 128), F32), vm((4, D, 128), BF16),
        vm((2, 64, D), BF16), vm((2, 64, D), BF16), vm((FRAMES, 16, D), BF16), vm((FRAMES, 16, D), BF16),
        vm((D, TOKENS), F32), vm((8, TOKENS), F32), vm((TOKENS, D), BF16), vm((TOKENS, 3 * D), F32),
        vm((PWAYS, 112, 128), BF16), vm((PWAYS, 112, 128), BF16), vm((512, 512), BF16), vm((512, 384), BF16),
        vm((PATCHES, 128), BF16), vm((PATCHES, 128), BF16), vm((PATCHES, 128), BF16),
        vm((PATCHES, 128), BF16), vm((FRAMES, HEADS, 16, 128), BF16), vm((TOKENS, D), BF16),
        vm((TOKENS, D), F32), vm((TOKENS, D), BF16), vm((TOKENS, D + 128), BF16),
        vm((TOKENS, D), F32), vm((TOKENS, D), F32), vm((TOKENS, 3 * D), BF16),
        vm((TOKENS, D), BF16), vm((TOKENS, 3 * D), BF16),
        vm((HEADS, TOKENS, TOKENS), F32), vm((HEADS, TOKENS, TOKENS), F32),
        vm((HEADS, TOKENS, TOKENS), BF16), vm((HEADS, TOKENS, TOKENS), BF16),
        vm((FRAMES, 16, D), BF16), vm((2, 64, D), BF16),
        vm((FRAMES, HEADS, 16, 128), BF16), vm((PATCHES, 128), BF16),
        vm((80, PATCHES), BF16), vm((80, PATCHES), F32), vm((PATCHES, PATCHES), BF16),
        vm((PWAYS, 48, 128), BF16), vm((PWAYS, 48, 128), BF16), vm((PWAYS, 32, 128), BF16), vm((PWAYS, 32, 128), BF16),
        vm((PWAYS, 32, 128), BF16), vm((PWAYS, 32, 128), BF16), vm((8, PATCHES), F32), vm((2, D, 128), BF16),
        vm((2, 64, D), BF16),
        vm((3 * D, TOKENS), BF16), vm((D, TOKENS), F32),
        vm((27, 32, 128), BF16), vm((PWAYS, 32, 128), BF16), vm((ZWAYS, 32, 128), F32),
        vm((32, 128), BF16), vm((3 * ROWS, 128), BF16),
        vm((6, 48, 128), BF16), vm((8, 48, 128), BF16), vm((16, 48, 128), BF16),
        vm((48, 128), BF16), vm((3, BLOCK, BLOCK, NBLOCK), F32),
        dma((12,)), dma((3,)), dma((16,)), dma((16,)), dma((4,)), dma((4,)),
    ]
    anyspec = pl.BlockSpec(memory_space=pl.ANY)
    blocks = [r.transpose(1, 2, 0) for r in (spatial_inward, spatial_outward, temporal_inward, temporal_outward)]
    grad, terms, red = pl.pallas_call(
        kernel,
        out_shape=(
            jax.ShapeDtypeStruct((2, 64, D), BF16),
            jax.ShapeDtypeStruct((3, BLOCK, BLOCK, NBLOCK), F32),
            jax.ShapeDtypeStruct((ROWS, 128), BF16),
        ),
        in_specs=[pl.BlockSpec(memory_space=pltpu.SMEM)] + [anyspec] * 10,
        out_specs=(anyspec,) * 3,
        scratch_shapes=scratch,
        compiler_params=pltpu.CompilerParams(
            collective_id=0, has_side_effects=True, vmem_limit_bytes=62 * 1024 * 1024
        ),
        name="block_backward",
    )(
        frame_mask, video, cotangent, spatial_project, spatial_output, temporal_project, temporal_output,
        *blocks,
    )
    term = jax.ShapeDtypeStruct((BLOCK, BLOCK, NBLOCK), F32)
    grad, sout, tin, tout, sin = pl.pallas_call(
        unpack_kernel,
        out_shape=(jax.ShapeDtypeStruct((2, 64, D), BF16), term, term, term, term),
        in_specs=[anyspec] * 3,
        out_specs=(anyspec,) * 5,
        scratch_shapes=[
            vm((ROWS, 128), BF16), vm((4, BLOCK, BLOCK, NBLOCK), F32), vm((2, 64, D), BF16), dma((5,)), dma((5,)),
        ],
        compiler_params=pltpu.CompilerParams(vmem_limit_bytes=62 * 1024 * 1024),
        name="unpack_terms",
    )(red, terms, grad)
    sin, sout, tin, tout = (r.transpose(2, 0, 1) for r in (sin, sout, tin, tout))
    return grad, sin, sout, tin, tout


def solution(mesh):
    split = P("frame", "patch", None)
    in_specs = (split, split) + (P(),) * 9
    out_specs = (split,) + (P(),) * 4
    return jax.shard_map(
        per_device, mesh=mesh, in_specs=in_specs, out_specs=out_specs, check_vma=False
    )
```

```python
import itertools
import math

import jax
import jax.numpy as jnp
from jax import lax
from jax.experimental import pallas as pl
from jax.experimental.pallas import tpu as pltpu
from jax.sharding import PartitionSpec as P

D = 1152
HEADS = 16
HEAD_DIM = 72
BLOCK = 32
GROUPS = D // 128
FRAMES = 8
PATCHES = 2048
ZWAYS = 4
PWAYS = 32
DEVICES = ZWAYS * PWAYS
TOKENS = 128
ROWS = D // 4
NBLOCK = D // 32

EPSILON = 1e-06
NEGATIVE = -1e30
SCALE = 1.0 / math.sqrt(HEAD_DIM)
LOG2E = math.log2(math.e)
LN2 = math.log(2.0)

F32 = jnp.float32
BF16 = jnp.bfloat16
MESH = pl.DeviceIdType.MESH


def hops(step):
    return min(step[0], 4 - step[0]) + min(step[1], 4 - step[1]) + min(step[3], 4 - step[3])


PLANE = sorted(
    [s for s in itertools.product(range(4), range(4), range(2), [0]) if any(s)], key=lambda s: -hops(s)
)
SPACE = sorted(
    [s for s in itertools.product(range(4), range(4), range(2), range(4)) if any(s)],
    key=lambda s: -hops(s),
)
SLOTS = PLANE + [(0, 0, 0, 0)]
SLOT_OF = {s[:3]: n for n, s in enumerate(SLOTS)}


def dot(a, b):
    return lax.dot_general(a, b, (((1,), (0,)), ((), ())), preferred_element_type=F32)


def dot_nt(a, b):
    return lax.dot_general(a, b, (((1,), (1,)), ((), ())), preferred_element_type=F32)


def dot_tn(a, b):
    return lax.dot_general(a, b, (((0,), (0,)), ((), ())), preferred_element_type=F32)


def lanes(shape):
    return lax.broadcasted_iota(jnp.int32, shape, len(shape) - 1)


def rows(shape):
    return lax.broadcasted_iota(jnp.int32, shape, 0)


def roll(x, amount):
    amount = amount % 128
    return x if amount == 0 else pltpu.roll(x, amount, 1)


def normalize(x):
    centered = x - jnp.mean(x, axis=-1, keepdims=True)
    inverse = lax.rsqrt(jnp.mean(centered * centered, axis=-1, keepdims=True) + EPSILON)
    return centered * inverse, inverse


def normalize_backward(adjoint, normed, inverse):
    grad_mean = jnp.mean(adjoint, axis=-1, keepdims=True)
    grad_cross = jnp.mean(adjoint * normed, axis=-1, keepdims=True)
    return inverse * (adjoint - grad_mean - normed * grad_cross)


def group(x, g):
    return x[:, g * 128 : (g + 1) * 128]


def rotate(x, blocks):
    return jnp.concatenate(
        [dot(group(x, g), blocks[g * 128 : (g + 1) * 128, :]) for g in range(GROUPS)], axis=1
    )


def rotate_transposed(x, blocks):
    return jnp.concatenate(
        [dot_nt(group(x, g), blocks[g * 128 : (g + 1) * 128, :]) for g in range(GROUPS)], axis=1
    )


def block_mask(shape):
    return (rows(shape) // BLOCK) % 4 == lanes(shape) // BLOCK


def rotation_gradient(left, right):
    mask = block_mask((128, 128))
    packed = []
    for g in range(GROUPS):
        full = jnp.where(mask, dot_tn(group(left, g), group(right, g)), 0.0)
        packed.append(full[0:32] + full[32:64] + full[64:96] + full[96:128])
    return packed


def layout_tools():
    shape = (BLOCK, 40, ROWS)
    b = lax.broadcasted_iota(jnp.int32, shape, 0)
    n = lax.broadcasted_iota(jnp.int32, shape, 1)
    from_row = lax.broadcasted_iota(jnp.int32, shape, 2)
    pick = jnp.where(from_row == (n >> 2) * BLOCK + b, 1.0, 0.0).reshape(BLOCK * 40, ROWS).astype(BF16)
    shape = (BLOCK, 40, 128)
    n = lax.broadcasted_iota(jnp.int32, shape, 1)
    own = ((n & 3) == (lax.broadcasted_iota(jnp.int32, shape, 2) >> 5)).reshape(BLOCK * 40, 128)
    repeat = jnp.where(lanes((128, 128)) % BLOCK == rows((128, 128)) % BLOCK, 1.0, 0.0).astype(BF16)
    return pick, own, repeat


def lay_out(tools, term, out):
    pick, own, repeat = tools
    lane = lanes((40, 128)) >> 5
    wide = dot(pick, term)
    wide = dot(jnp.where(own, wide, 0.0).astype(BF16), repeat)
    for m in range(8):
        four = jnp.zeros((40, 128), F32)
        for s in range(4):
            at = (4 * m + s) * 40
            four = jnp.where(lane == s, wide[at : at + 40], four)
        out[4 * m : 4 * m + 4] = four.T[:, 0:NBLOCK].reshape(4, BLOCK, NBLOCK)


def kernel(
    mask_ref, video, cotangent, wsp_h, wso_h, wtp_h, wto_h, rsi_h, rso_h, rti_h, rto_h,
    vg_ref, terms_ref, red_ref,
    wsp, wso, wtp, wto, r4, bd32, bd,
    vid, cot, vid_mid, ct_mid,
    normed1, inverse1, rot_b, proj,
    qkv_snd, qkv_rcv, beside_snd, fold, kx, qx, vx,
    att_snd, att_rcv, att1, top, aot, daz,
    normed2, proj2, att2_b, dproj_b,
    t_s, t_dp, t_p, t_ds,
    ah_snd, ah_rcv, do_snd, do_rcv, qt, dvt, pq,
    dk_snd, dk_rcv, dv_snd, dv_rcv, dq_snd, dq_rcv, dq_last, w_last, vg, dpt, adjt,
    r1_snd, r1_rcv, r1_z, r1_chunk, r1_out,
    r2_snd, r2_rcv, r2_z, r2_chunk, r3_snd, r3_rcv, r3_z, r3_chunk, terms,
    load_sems, out_sems, send_sems, recv_sems, qkv_sems, do_sems,
):
    z = lax.axis_index("frame")
    j = lax.axis_index("patch")
    px, py, pc = j >> 3, (j >> 1) & 3, j & 1
    xs = [((px + d) & 3) * 8 for d in range(4)]
    ys = [((py + d) & 3) * 2 for d in range(4)]
    cs = [(pc + d) & 1 for d in range(2)]
    zs = [(z + d) & 3 for d in range(4)]
    xys = [[a + b for b in ys] for a in xs]

    def ahead(step):
        return zs[step[3]], xys[step[0]][step[1]] + cs[step[2]]

    def behind(step):
        return zs[-step[3] & 3], xys[-step[0] & 3][-step[1] & 3] + cs[step[2]]

    def load(src, dst, n):
        return pltpu.make_async_copy(src, dst, load_sems.at[n])

    early = [load(video, vid, 0), load(rsi_h, r4.at[0], 1)]
    early += [
        load(wsp_h.at[:, pl.ds(c * D, D)], wsp.at[:, pl.ds(c * D, D)], n) for c, n in enumerate((2, 10, 11))
    ]
    late = [
        load(cotangent, cot, 3), load(rso_h, r4.at[1], 4), load(rti_h, r4.at[2], 5),
        load(rto_h, r4.at[3], 6), load(wto_h, wto, 7), load(wso_h, wso, 8), load(wtp_h, wtp, 9),
    ]
    for copy in early:
        copy.start()

    barrier = pltpu.get_barrier_semaphore()
    near = PLANE + [(0, 0, 0, d) for d in (2, 1, 3)]
    for step in near:
        pl.semaphore_signal(barrier, inc=1, device_id=ahead(step), device_id_type=MESH)

    def local(src, dst, sem):
        pltpu.make_async_copy(src, dst, sem).start()

    def remote(src, dst, phase, there, recv_sem=None):
        pltpu.make_async_remote_copy(
            src_ref=src, dst_ref=dst, send_sem=send_sems.at[phase],
            recv_sem=recv_sems.at[phase] if recv_sem is None else recv_sem,
            device_id=there, device_id_type=MESH,
        ).start()

    def wait_all(sem, buffer):
        pltpu.make_async_copy(buffer, buffer, sem).wait()

    def make_blocks(index):
        shape = (128, 512)
        spread = jnp.where(
            jnp.logical_and(
                rows(shape) // BLOCK == lanes(shape) // 128, rows(shape) % BLOCK == lanes(shape) % BLOCK
            ),
            1.0, 0.0,
        ).astype(BF16)
        shape = (NBLOCK, 128)
        own = rows(shape) % 4 == lanes(shape) // BLOCK
        for m in range(8):
            four = r4[index, 4 * m : 4 * m + 4].reshape(128, NBLOCK).astype(BF16)
            wide = dot_tn(four, spread)
            for s in range(4):
                bd32[pl.ds(4 * m + s, NBLOCK, stride=BLOCK), :] = jnp.where(own, group(wide, s), 0.0)
        bd[index] = bd32[...].astype(BF16)

    shape = (512, 384)
    source, target = rows(shape), lanes(shape)
    quarter, lane_in = source >> 7, source & 127
    to_pair = jnp.where(lane_in < 64, (quarter & 1) * 128 + (quarter >> 1) * 64 + lane_in, -1)
    to_last = jnp.where(jnp.logical_and(lane_in >= 64, lane_in < 88), 256 + quarter * 32 + lane_in - 64, -1)
    hit = jnp.logical_or(target == to_pair, target == to_last)
    fold[...] = jnp.where(hit, 1.0, 0.0).astype(BF16)

    early[0].wait()
    normed, _ = normalize(vid[...].reshape(TOKENS, D).astype(F32))
    early[1].wait()
    make_blocks(0)
    rot_b[...] = rotate(normed.astype(BF16), bd.at[0]).astype(BF16)

    for c in range(3):
        at = slice(c * D, (c + 1) * D)
        early[2 + c].wait()
        proj[:, at] = dot(rot_b[...], wsp[:, at])
    for copy in late:
        copy.start()

    lane = lanes((TOKENS, 128))
    qscale = jnp.where(lane < HEAD_DIM, SCALE * LOG2E, 1.0)
    for h in range(HEADS):
        t, off = (HEAD_DIM * h) // 128, (HEAD_DIM * h) % 128

        def pick(section, to):
            first = proj[:, section * D + t * 128 : section * D + (t + 1) * 128]
            if off + HEAD_DIM > 128:
                second = proj[:, section * D + (t + 1) * 128 : section * D + (t + 2) * 128]
                first = jnp.where(lane >= off, first, second)
            return roll(first, to - off)

        q, k, v = pick(0, 0), pick(1, 72), pick(2, 16)
        low = (jnp.where(lane < 72, q, k) * qscale).astype(BF16)
        high = jnp.where(lane < 16, k, jnp.where(lane < 88, v, 0.0)).astype(BF16)
        for f in range(2):
            item = f * HEADS + h
            qkv_snd[item, 0:64] = low[64 * f : 64 * (f + 1)]
            for e in range(4):
                at = 64 * f + 16 * e
                beside_snd[16 * item : 16 * item + 16, 128 * e : 128 * e + 128] = high[at : at + 16]
    folded = dot(beside_snd[...], fold[...]).astype(BF16)
    for part in range(3):
        qkv_snd[:, 64 + 16 * part : 80 + 16 * part] = group(folded, part).reshape(PWAYS, 16, 128)

    pl.semaphore_wait(barrier, len(near))

    for n, step in enumerate(SLOTS):
        dst = qkv_rcv.at[n]
        if any(step):
            zz, jj = ahead(step)
            remote(qkv_snd.at[jj], dst, 2, (zz, jj), qkv_sems.at[n // 8])
        else:
            local(qkv_snd.at[j], dst, qkv_sems.at[n // 8])

    late[0].wait()
    for phase, src, dst in ((1, cot, ct_mid), (0, vid, vid_mid)):
        for d in (2, 1, 3, 0):
            for f in range(2):
                piece = src.at[f, pl.ds(pl.multiple_of(zs[d] * 16, 16), 16)]
                if d:
                    remote(piece, dst.at[2 * z + f], phase, (zs[d], j))
                else:
                    local(piece, dst.at[2 * z + f], recv_sems.at[phase])

    for n in (1, 2, 3):
        late[n].wait()
        make_blocks(n)

    columns = vid[...].reshape(TOKENS, D).astype(F32).T
    columns = columns - jnp.mean(columns, axis=0, keepdims=True)
    inverse = lax.rsqrt(jnp.mean(columns * columns, axis=0, keepdims=True) + EPSILON)
    normed1[...] = columns * inverse
    inverse1[...] = jnp.broadcast_to(inverse, (8, 128))

    shape = (D, 128)
    column = HEAD_DIM * (lanes(shape) >> 3) + 64 + (lanes(shape) & 7)
    select = jnp.where(rows(shape) == column, 1.0, 0.0).astype(BF16)
    for n, section in enumerate((0, 2)):
        w_last[n] = dot(wsp[:, section * D : (section + 1) * D], select).astype(BF16)

    wait_all(recv_sems.at[1], ct_mid)
    frame_row = rows((TOKENS, 1)) // 16
    valid = jnp.zeros((TOKENS, 1), F32)
    for f in range(FRAMES):
        valid = jnp.where(frame_row == f, mask_ref[f].astype(F32), valid)
    top[...] = ct_mid[...].reshape(TOKENS, D).astype(F32) * valid
    late[4].wait()
    aot[...] = dot_nt(top[...].astype(BF16), wto[...]).astype(BF16)
    daz[:, 0:D] = rotate_transposed(aot[...], bd.at[3]).astype(BF16)
    daz[:, D:] = jnp.zeros((TOKENS, 128), BF16)

    lane2 = lanes((256, 128))
    ones = jnp.where(jnp.logical_and(lane2 >= 72, lane2 < 76), 1.0, 0.0)

    def prepare(i, carry):
        at = pl.ds(pl.multiple_of(i * 256, 256), 256)
        low, high = [], []
        for m in range(4):
            slot = qkv_rcv[4 * i + m].astype(F32)
            low.append(slot[0:64])
            mid, last = slot[64:96], slot[96:112]
            high.append(
                jnp.where(
                    lanes((64, 128)) < 64,
                    jnp.concatenate([mid, roll(mid, 64)], axis=0),
                    jnp.concatenate([roll(last, 64 - 32 * e) for e in range(4)], axis=0),
                )
            )
        t0, t1 = jnp.concatenate(low, axis=0), jnp.concatenate(high, axis=0)
        k = roll(jnp.where(lane2 >= 72, t0, t1), -72)
        kx[at, :] = jnp.where(lane2 < 72, k, ones).astype(BF16)
        vx[at, :] = jnp.where(lane2 < 72, roll(t1, -16), ones).astype(BF16)
        qx[at, :] = jnp.where(lane2 < 72, t0, 0.0).astype(BF16)
        return carry

    for g in range(4):
        wait_all(qkv_sems.at[g], qkv_rcv.at[pl.ds(8 * g, 8)])
        lax.fori_loop(2 * g, 2 * g + 2, prepare, 0)

    def attend_span(start, count):
        spans = [pl.ds(start + s * 256, 256) for s in range(count)]
        highs = []
        for s, at in enumerate(spans):
            scores = dot_nt(qx[at, :], kx[...])
            highs.append(jnp.max(scores, axis=-1, keepdims=True))
            pq[256 * s : 256 * s + 256, :] = jnp.exp2(scores - highs[-1]).astype(BF16)
        both_out = dot(pq[0 : 256 * count, :], vx[...])
        for s, (at, high_score) in enumerate(zip(spans, highs)):
            out = both_out[256 * s : 256 * s + 256]
            total = out[:, 72:73]
            att_snd[at, :] = jnp.where(lane2 < 72, out / total, 0.0).astype(BF16)
            neg = -(high_score + jnp.log(total) * LOG2E)
            hi = neg.astype(BF16).astype(F32)
            mid = (neg - hi).astype(BF16).astype(F32)
            lo = neg - hi - mid
            old = qx[at, :].astype(F32)
            new = jnp.where(
                lane2 == 72, hi, jnp.where(lane2 == 73, mid, jnp.where(lane2 == 74, lo, old))
            )
            qx[at, :] = new.astype(BF16)

    def send_attended(slots):
        for n in slots:
            for d in (2, 1, 3, 0):
                zz, jj = zs[d], behind(SLOTS[n])[1]
                src = att_snd.at[pl.ds(pl.multiple_of(64 * n + 16 * zz, 16), 16)]
                dst = att_rcv.at[2 * z + (j >> 4), j & 15]
                if d or any(SLOTS[n]):
                    remote(src, dst, 3, (zz, jj))
                else:
                    local(src, dst, recv_sems.at[3])

    def attend(i, carry):
        attend_span(pl.multiple_of(i * 512, 512), 2)
        for ii in range(1, 4):

            @pl.when(i == ii)
            def _():
                send_attended(range(8 * ii, 8 * ii + 8))

        return carry

    for half in range(2):
        attend_span(256 * half, 1)
        send_attended(range(4 * half, 4 * half + 4))
    lax.fori_loop(1, 4, attend, 0)

    wait_all(recv_sems.at[0], vid_mid)
    wait_all(recv_sems.at[3], att_rcv)

    def add_piece(tiles, at, piece):
        tiles[at] = piece if tiles[at] is None else tiles[at] + piece

    def place(tiles, h, value):
        t, off = (HEAD_DIM * h) // 128, (HEAD_DIM * h) % 128
        if off + HEAD_DIM > 128:
            add_piece(tiles, t, jnp.where(lane >= off, value, 0.0))
            add_piece(tiles, t + 1, jnp.where(lane < off, value, 0.0))
        else:
            add_piece(tiles, t, value)

    tiles = [None] * GROUPS
    for h in range(HEADS):
        place(tiles, h, roll(att_rcv[:, h].reshape(TOKENS, 128).astype(F32), (HEAD_DIM * h) % 128))
    for t in range(GROUPS):
        att1[:, t * 128 : (t + 1) * 128] = tiles[t].astype(BF16)

    late[5].wait()
    outrot = rotate(att1[...], bd.at[1]).astype(BF16)
    hidden = vid_mid[...].reshape(TOKENS, D).astype(F32) + dot(outrot, wso[...])
    hidden = hidden.astype(BF16).astype(F32)
    normed, inverse2 = normalize(hidden)
    normed2[...] = normed
    rot_b[...] = rotate(normed.astype(BF16), bd.at[2]).astype(BF16)
    late[6].wait()

    for c in range(3):
        at = slice(c * D, (c + 1) * D)
        proj2[:, at] = dot(rot_b[...], wtp[:, at]).astype(BF16)

    square = (TOKENS, TOKENS)
    same_patch = rows(square) % 16 == lanes(square) % 16
    same_frame = rows(square) // 16 == lanes(square) // 16
    key_valid = jnp.zeros(square, F32)
    for f in range(FRAMES):
        key_valid = jnp.where(rows(square) // 16 == f, mask_ref[f].astype(F32), key_valid)
    allowed = jnp.logical_and(same_patch, jnp.logical_or(key_valid == 1.0, same_frame))
    bias = jnp.where(allowed, 0.0, NEGATIVE)

    def window(h, section):
        t, off = (HEAD_DIM * h) // 128, (HEAD_DIM * h) % 128
        width = 256 if off + HEAD_DIM > 128 else 128
        return slice(section * D + t * 128, section * D + t * 128 + width)

    def own_lanes(h):
        off = (HEAD_DIM * h) % 128
        l = lanes((1, 256 if off + HEAD_DIM > 128 else 128))
        return jnp.where(jnp.logical_and(l >= off, l < off + HEAD_DIM), 1.0, 0.0)

    for h in range(HEADS):
        own = own_lanes(h).astype(BF16)
        t_s[h] = dot_nt(proj2[:, window(h, 1)], proj2[:, window(h, 0)] * own)
        t_dp[h] = dot_nt(proj2[:, window(h, 2)], daz[:, window(h, 0)] * own)

    for h in range(HEADS):
        scores = t_s[h] * SCALE + bias
        e = jnp.exp(scores - jnp.max(scores, axis=0, keepdims=True))
        p = e * (1.0 / jnp.sum(e, axis=0, keepdims=True))
        dp = t_dp[h]
        t_p[h] = p.astype(BF16)
        t_ds[h] = (p * (dp - jnp.sum(p * dp, axis=0, keepdims=True))).astype(BF16)

    def gather(section, dst, base):
        tiles = [None] * (GROUPS + 1)
        for h in range(HEADS):
            own = own_lanes(h)
            own_b = own.astype(BF16)
            if section == 0:
                part = dot_tn(t_ds[h], proj2[:, window(h, 1)]) * (own * SCALE)
            elif section == 1:
                part = dot(t_ds[h], proj2[:, window(h, 0)] * own_b) * SCALE
            elif section == 2:
                part = dot(t_p[h], daz[:, window(h, 0)] * own_b)
            else:
                part = dot_tn(t_p[h], proj2[:, window(h, 2)]) * own
            t = (HEAD_DIM * h) // 128
            for w in range(part.shape[1] // 128):
                add_piece(tiles, t + w, group(part, w))
        for t in range(GROUPS):
            dst[:, base + t * 128 : base + (t + 1) * 128] = tiles[t].astype(BF16)

    for section in range(3):
        gather(section, dproj_b, section * D)

    adj_rot2 = jnp.concatenate(
        [dot_nt(dproj_b[...], wtp[c * 384 : (c + 1) * 384, :]).astype(BF16) for c in range(3)], axis=1
    )
    adj_normed = rotate_transposed(adj_rot2, bd.at[2])
    adj_hidden = top[...] + normalize_backward(adj_normed, normed2[...], inverse2)
    adj_hidden_b = adj_hidden.astype(BF16)
    ah_snd[...] = adj_hidden_b.reshape(FRAMES, 16, D)
    aho = dot_nt(adj_hidden_b, wso[...]).astype(BF16)
    adj_att1 = rotate_transposed(aho, bd.at[1])
    for h in range(HEADS):
        t, off = (HEAD_DIM * h) // 128, (HEAD_DIM * h) % 128
        first = group(adj_att1, t)
        if off + HEAD_DIM > 128:
            first = jnp.where(lane >= off, first, group(adj_att1, t + 1))
        piece = jnp.where(lane < 72, roll(first, -off), 0.0).astype(BF16)
        do_snd[:, h] = piece.reshape(FRAMES, 16, 128)

    for step in [slot[:3] + (d,) for slot in SLOTS for d in (2, 1, 3, 0)]:
        zz, jj = ahead(step)
        src = do_snd.at[2 * zz + (jj >> 4), jj & 15]
        n = SLOT_OF[step[:3]]
        dst = do_rcv.at[pl.ds(pl.multiple_of(64 * n + 16 * z, 16), 16)]
        if any(step):
            remote(src, dst, 4, (zz, jj), do_sems.at[n // 8])
        else:
            local(src, dst, do_sems.at[n // 8])
    for d in (2, 1, 3, 0):
        for f in range(2):
            src = ah_snd.at[2 * zs[d] + f]
            dst = ah_rcv.at[f, pl.ds(pl.multiple_of(z * 16, 16), 16)]
            if d:
                remote(src, dst, 5, (zs[d], j))
            else:
                local(src, dst, recv_sems.at[5])

    gather(3, att2_b, 0)
    for n, packed in enumerate((
        rotation_gradient(att1[...], aho),
        rotation_gradient(normed2[...].astype(BF16), adj_rot2),
        rotation_gradient(att2_b[...], aot[...]),
    )):
        for g in range(GROUPS):
            r1_snd[n * GROUPS + g] = packed[g].astype(BF16)

    def reduce_first(snd, rcv, chunk_of, owns, phase):
        for step in SLOTS:
            zz, jj = ahead(step)

            @pl.when(owns(jj))
            def _():
                if any(step):
                    remote(snd.at[chunk_of(jj)], rcv.at[j], phase, (zz, jj))
                else:
                    local(snd.at[chunk_of(jj)], rcv.at[j], recv_sems.at[phase])

    def reduce_second(rcv, zbuf, owns, phase):
        @pl.when(owns(j))
        def _():
            wait_all(recv_sems.at[phase], rcv)
            zbuf[z] = jnp.sum(rcv[...].astype(F32), axis=0)
            for d in (2, 1, 3):
                remote(zbuf.at[z], zbuf.at[z], phase + 1, (zs[d], j))

    def reduce_third(zbuf, chunk, out, chunk_of, owns, phase):
        size = chunk.shape[0]

        @pl.when(owns(j))
        def _():
            wait_all(recv_sems.at[phase + 1], zbuf.at[pl.ds(0, ZWAYS - 1)])
            chunk[...] = (((zbuf[0] + zbuf[1]) + (zbuf[2] + zbuf[3])) / 128.0).astype(BF16)
            dst = out.at[pl.ds(pl.multiple_of(chunk_of(j) * size, size), size)]
            for step in SLOTS:
                if any(step):
                    remote(chunk, dst, phase + 2, ahead(step))
                else:
                    local(chunk, dst, recv_sems.at[phase + 2])

    def reduce_sent(snd, rcv, zbuf, owners, owns, phase):
        @pl.when(owns(j))
        def _():
            wait_all(send_sems.at[phase], snd.at[pl.ds(0, owners - 1)])
            wait_all(send_sems.at[phase + 1], zbuf.at[pl.ds(0, ZWAYS - 1)])
            wait_all(send_sems.at[phase + 2], rcv.at[pl.ds(0, PWAYS - 1)])

        @pl.when(jnp.logical_not(owns(j)))
        def _():
            wait_all(send_sems.at[phase], snd)

    def chunk1(jj):
        return jj

    def owns1(jj):
        return jj < 27

    reduce_first(r1_snd, r1_rcv, chunk1, owns1, 7)

    def probabilities(i, carry):
        for s in range(2):
            at = pl.ds(pl.multiple_of(i * 512 + s * 256, 256), 256)
            pq[at, :] = jnp.exp2(dot_nt(qx[at, :], kx[...])).astype(BF16)
        return carry

    lax.fori_loop(0, 4, probabilities, 0)

    def prepare_queries(i, carry):
        at = pl.ds(pl.multiple_of(i * 256, 256), 256)
        qt[:, at] = qx[at, :].astype(F32).T[0:80].astype(BF16)
        return carry

    lax.fori_loop(0, 8, prepare_queries, 0)

    def beside(left, right, odd):
        left, right = (roll(left, 64), right) if odd else (left, roll(right, 64))
        return jnp.where(lanes(left.shape) < 64, left, right)

    def value_gradient(group_):
        at = pl.ds(group_ * 512, 512)
        dv = dot(do_rcv[at, :].astype(F32).T[0:80].astype(BF16), pq[at, :])
        if group_ == 0:
            dvt[...] = dv
        else:
            dvt[...] += dv

    def attend_back(group_):
        at = pl.ds(group_ * 512, 512)
        lane5 = lanes((512, 128))
        g = do_rcv[at, :].astype(F32)
        delta = -jnp.sum(g * att_snd[at, :].astype(F32), axis=-1, keepdims=True)
        hi = delta.astype(BF16).astype(F32)
        lo = delta - hi
        dox = jnp.where(lane5 == 72, hi, jnp.where(lane5 == 73, lo, g)).astype(BF16)
        ds = (pq[at, :].astype(F32) * dot_nt(dox, vx[...])).astype(BF16)
        dq = dot(ds, kx[...]).T * SCALE
        for m in range(8):
            tile = dq[:, 128 * (m // 2) : 128 * (m // 2) + 128]
            dq_snd[8 * group_ + m] = beside(tile[0:32], tile[32:64], m % 2).astype(BF16)
        dq_last[:, group_ * 512 : group_ * 512 + 512] = dq[64:72]
        pq[at, :] = ds
        send_back(dq_snd, dq_rcv, 13, range(8 * group_, 8 * group_ + 8))

    def send_back(snd, rcv, phase, slots):
        for n in slots:
            if any(SLOTS[n]):
                remote(snd.at[n], rcv.at[j], phase, behind(SLOTS[n]))
            else:
                local(snd.at[n], rcv.at[j], recv_sems.at[phase])

    for group_ in range(4):
        wait_all(do_sems.at[group_], do_rcv.at[pl.ds(512 * group_, 512)])
        value_gradient(group_)
        if group_ == 0:
            attend_back(0)
    for n in range(PWAYS):
        at = slice(128 * (n // 2), 128 * (n // 2) + 128)
        dv_snd[n] = beside(dvt[0:32, at], dvt[32:64, at], n % 2).astype(BF16)
    send_back(dv_snd, dv_rcv, 15, range(PWAYS))
    for group_ in (1, 2, 3):
        attend_back(group_)

    def key_gradient(group_):
        return dot(qt[...], pq[:, 512 * group_ : 512 * group_ + 512]) * LN2

    dk = key_gradient(0)
    for group_ in range(4):
        following = key_gradient(group_ + 1) if group_ < 3 else None
        for m in range(8):
            n = 8 * group_ + m
            at, here = slice(128 * (n // 2), 128 * (n // 2) + 128), slice(128 * (m // 2), 128 * (m // 2) + 128)
            rest = [dk[48:72, here], dq_last[:, at], dvt[64:72, at], jnp.zeros((8, 128), F32)]
            dk_snd[n] = beside(dk[0:48, here], jnp.concatenate(rest, axis=0), n % 2).astype(BF16)
        send_back(dk_snd, dk_rcv, 6, range(8 * group_, 8 * group_ + 8))
        dk = following

    reduce_second(r1_rcv, r1_z, owns1, 7)

    def halves(buffer, h):
        one, two = buffer[h].astype(F32), buffer[HEADS + h].astype(F32)
        first = lanes(one.shape) < 64
        return jnp.where(first, one, roll(two, 64)), jnp.where(first, roll(one, 64), two)

    def unpack_first(buffer, base):
        for pair in range(HEADS // 2):
            parts = []
            for h in (2 * pair, 2 * pair + 1):
                parts += [*halves(buffer, h), jnp.zeros((8, 128), F32)]
            at = base + 144 * pair
            dpt[at : at + 144] = jnp.concatenate(parts, axis=0).astype(BF16)

    wait_all(recv_sems.at[15], dv_rcv)
    unpack_first(dv_rcv, 2 * D)
    for c in range(3):
        at = slice(c * 384, (c + 1) * 384)
        adjt[at] = dot(wsp[at, 2 * D :], dpt[2 * D :])
    wait_all(recv_sems.at[13], dq_rcv)
    unpack_first(dq_rcv, 0)
    for c in range(3):
        at = slice(c * 384, (c + 1) * 384)
        adjt[at] += dot(wsp[at, 0:D], dpt[0:D])
    reduce_third(r1_z, r1_chunk, r1_out, chunk1, owns1, 7)
    wait_all(recv_sems.at[6], dk_rcv)

    last = [[], []]
    for pair in range(HEADS // 2):
        parts = []
        for h in (2 * pair, 2 * pair + 1):
            left, right = halves(dk_rcv, h)
            parts += [left, right[0:24]]
            last[0].append(right[24:32])
            last[1].append(right[32:40])
        at = D + 144 * pair
        dpt[at : at + 144] = jnp.concatenate(parts, axis=0).astype(BF16)
    last = [jnp.concatenate(parts, axis=0).astype(BF16) for parts in last]

    for c in range(3):
        at = slice(c * 384, (c + 1) * 384)
        adjt[at] += (
            dot(wsp[at, D : 2 * D], dpt[D : 2 * D]) + dot(w_last[0, at], last[0]) + dot(w_last[1, at], last[1])
        )
    packed = []
    mask = block_mask((128, 128))
    for g in range(GROUPS):
        at = slice(g * 128, (g + 1) * 128)
        full = jnp.where(mask, dot_nt(normed1[at].astype(BF16), adjt[at].astype(BF16)), 0.0)
        packed.append(full[0:32] + full[32:64] + full[64:96] + full[96:128])
    flat = jnp.concatenate(packed, axis=0).astype(BF16)
    for o in range(8):
        r2_snd[o] = flat[32 * o : 32 * o + 32]
    for o in range(2):
        r3_snd[o] = flat[256 + 16 * o : 272 + 16 * o]
    owner = 2 * px + pc
    more = (owner & 3) == 0
    row = [s for s in SLOTS if s[1] == 0]
    sheet = [s for s in SPACE if s[0] == 0 and s[2] == 0]
    for step in row:
        zz, jj = ahead(step)
        there = 2 * (jj >> 3) + (jj & 1)
        if any(step):
            remote(r2_snd.at[there], r2_rcv.at[owner], 10, (zz, jj))
        else:
            local(r2_snd.at[there], r2_rcv.at[owner], recv_sems.at[10])

        @pl.when((there & 3) == 0)
        def _():
            if any(step):
                remote(r3_snd.at[there >> 2], r3_rcv.at[owner], 14, (zz, jj))
            else:
                local(r3_snd.at[there >> 2], r3_rcv.at[owner], recv_sems.at[14])

    adj_normed = jnp.concatenate(
        [
            dot(bd[0, g * 128 : (g + 1) * 128, :], adjt[g * 128 : (g + 1) * 128].astype(BF16))
            for g in range(GROUPS)
        ],
        axis=0,
    )
    grad_mean = jnp.mean(adj_normed, axis=0, keepdims=True)
    grad_cross = jnp.mean(adj_normed * normed1[...], axis=0, keepdims=True)
    grad = (inverse1[0:1] * (adj_normed - grad_mean - normed1[...] * grad_cross)).T
    wait_all(recv_sems.at[5], ah_rcv)
    grad = ah_rcv[...].reshape(TOKENS, D).astype(F32) + grad
    vg[...] = grad.astype(BF16).reshape(2, 64, D)
    vg_out = pltpu.make_async_copy(vg, vg_ref, out_sems.at[0])
    vg_out.start()
    def sheet_sum(rcv, zbuf, phase_in, phase):
        wait_all(recv_sems.at[phase_in], rcv)
        own = 4 * z + py
        zbuf[own] = jnp.sum(rcv[...].astype(F32), axis=0).astype(BF16)
        for step in sheet:
            remote(zbuf.at[own], zbuf.at[own], phase, ahead(step))

    sheet_sum(r2_rcv, r2_z, 10, 11)

    @pl.when(more)
    def _():
        sheet_sum(r3_rcv, r3_z, 14, 16)

    wait_all(send_sems.at[0], vid_mid.at[pl.ds(0, 6)])
    wait_all(send_sems.at[1], ct_mid.at[pl.ds(0, 6)])
    wait_all(send_sems.at[2], qkv_snd.at[pl.ds(0, PWAYS - 1)])
    wait_all(send_sems.at[3], att_snd.at[pl.ds(0, PATCHES - 16)])
    wait_all(send_sems.at[4], do_rcv.at[pl.ds(0, PATCHES - 16)])
    wait_all(send_sems.at[5], ah_snd.at[pl.ds(0, 6)])
    wait_all(send_sems.at[6], dk_snd.at[pl.ds(0, PWAYS - 1)])
    wait_all(send_sems.at[15], dv_snd.at[pl.ds(0, PWAYS - 1)])
    wait_all(send_sems.at[13], dq_snd.at[pl.ds(0, PWAYS - 1)])
    wait_all(recv_sems.at[9], r1_out)
    def row_spread(zbuf, chunk, dst, phase_in, phase):
        wait_all(recv_sems.at[phase_in], zbuf.at[pl.ds(0, 15)])
        chunk[...] = (jnp.sum(zbuf[...].astype(F32), axis=0) / 128.0).astype(BF16)
        for step in row:
            if any(step):
                remote(chunk, dst, phase, ahead(step))
            else:
                local(chunk, dst, recv_sems.at[phase])

    row_spread(r2_z, r2_chunk, red_ref.at[pl.ds(pl.multiple_of(32 * owner, 32), 32)], 11, 12)

    @pl.when(more)
    def _():
        row_spread(r3_z, r3_chunk, red_ref.at[pl.ds(pl.multiple_of(256 + 16 * (owner >> 2), 16), 16)], 16, 17)

    tools = layout_tools()
    for n in range(3):
        lay_out(tools, r1_out[n * ROWS : (n + 1) * ROWS], terms.at[n])
    red1 = pltpu.make_async_copy(terms, terms_ref, out_sems.at[1])
    red1.start()
    reduce_sent(r1_snd, r1_rcv, r1_z, 27, owns1, 7)
    wait_all(send_sems.at[10], r2_snd.at[pl.ds(0, 7)])
    wait_all(send_sems.at[11], r2_z.at[pl.ds(0, 15)])
    wait_all(send_sems.at[12], r2_rcv.at[pl.ds(0, 7)])

    @pl.when(more)
    def _():
        wait_all(send_sems.at[14], r3_snd.at[0])
        wait_all(send_sems.at[16], r3_z.at[pl.ds(0, 15)])
        wait_all(send_sems.at[17], r3_rcv.at[pl.ds(0, 7)])

    @pl.when(jnp.logical_not(more))
    def _():
        wait_all(send_sems.at[14], r3_snd)

    wait_all(recv_sems.at[12], red_ref.at[pl.ds(0, 256)])
    wait_all(recv_sems.at[17], red_ref.at[pl.ds(256, 32)])
    red1.wait()
    vg_out.wait()


def unpack_kernel(sin_h, terms_h, vg_in, vg_out, sout, tin, tout, sin, packed, terms, vg, in_sems, out_sems):
    loads = [pltpu.make_async_copy(sin_h, packed, in_sems.at[0])]
    loads += [pltpu.make_async_copy(terms_h.at[n], terms.at[n], in_sems.at[n + 1]) for n in range(3)]
    loads.append(pltpu.make_async_copy(vg_in, vg, in_sems.at[4]))
    for copy in loads:
        copy.start()
    stores = [pltpu.make_async_copy(terms.at[n], out, out_sems.at[n]) for n, out in enumerate((sout, tin, tout, sin))]
    stores.append(pltpu.make_async_copy(vg, vg_out, out_sems.at[4]))
    tools = layout_tools()
    loads[0].wait()
    lay_out(tools, packed[...], terms.at[3])
    stores[3].start()
    for n, at in ((1, 0), (2, 1), (3, 2), (4, 4)):
        loads[n].wait()
        stores[at].start()
    for store in stores:
        store.wait()


def per_device(
    video,
    cotangent,
    frame_mask,
    spatial_project,
    spatial_output,
    temporal_project,
    temporal_output,
    spatial_inward,
    spatial_outward,
    temporal_inward,
    temporal_outward,
):
    vm = pltpu.VMEM
    dma = pltpu.SemaphoreType.DMA
    scratch = [
        vm((D, 3 * D), BF16), vm((D, D), BF16), vm((D, 3 * D), BF16), vm((D, D), BF16),
        vm((4, BLOCK, BLOCK, NBLOCK), F32), vm((D, 128), F32), vm((4, D, 128), BF16),
        vm((2, 64, D), BF16), vm((2, 64, D), BF16), vm((FRAMES, 16, D), BF16), vm((FRAMES, 16, D), BF16),
        vm((D, TOKENS), F32), vm((8, TOKENS), F32), vm((TOKENS, D), BF16), vm((TOKENS, 3 * D), F32),
        vm((PWAYS, 112, 128), BF16), vm((PWAYS, 112, 128), BF16), vm((512, 512), BF16), vm((512, 384), BF16),
        vm((PATCHES, 128), BF16), vm((PATCHES, 128), BF16), vm((PATCHES, 128), BF16),
        vm((PATCHES, 128), BF16), vm((FRAMES, HEADS, 16, 128), BF16), vm((TOKENS, D), BF16),
        vm((TOKENS, D), F32), vm((TOKENS, D), BF16), vm((TOKENS, D + 128), BF16),
        vm((TOKENS, D), F32), vm((TOKENS, 3 * D), BF16),
        vm((TOKENS, D), BF16), vm((TOKENS, 3 * D), BF16),
        vm((HEADS, TOKENS, TOKENS), F32), vm((HEADS, TOKENS, TOKENS), F32),
        vm((HEADS, TOKENS, TOKENS), BF16), vm((HEADS, TOKENS, TOKENS), BF16),
        vm((FRAMES, 16, D), BF16), vm((2, 64, D), BF16),
        vm((FRAMES, HEADS, 16, 128), BF16), vm((PATCHES, 128), BF16),
        vm((80, PATCHES), BF16), vm((80, PATCHES), F32), vm((PATCHES, PATCHES), BF16),
        vm((PWAYS, 48, 128), BF16), vm((PWAYS, 48, 128), BF16), vm((PWAYS, 32, 128), BF16), vm((PWAYS, 32, 128), BF16),
        vm((PWAYS, 32, 128), BF16), vm((PWAYS, 32, 128), BF16), vm((8, PATCHES), F32), vm((2, D, 128), BF16),
        vm((2, 64, D), BF16),
        vm((3 * D, TOKENS), BF16), vm((D, TOKENS), F32),
        vm((27, 32, 128), BF16), vm((PWAYS, 32, 128), BF16), vm((ZWAYS, 32, 128), F32),
        vm((32, 128), BF16), vm((3 * ROWS, 128), BF16),
        vm((8, 32, 128), BF16), vm((8, 32, 128), BF16), vm((16, 32, 128), BF16), vm((32, 128), BF16),
        vm((2, 16, 128), BF16), vm((8, 16, 128), BF16), vm((16, 16, 128), BF16), vm((16, 128), BF16),
        vm((3, BLOCK, BLOCK, NBLOCK), F32),
        dma((12,)), dma((3,)), dma((18,)), dma((18,)), dma((4,)), dma((4,)),
    ]
    anyspec = pl.BlockSpec(memory_space=pl.ANY)
    blocks = [r.transpose(1, 2, 0) for r in (spatial_inward, spatial_outward, temporal_inward, temporal_outward)]
    grad, terms, red = pl.pallas_call(
        kernel,
        out_shape=(
            jax.ShapeDtypeStruct((2, 64, D), BF16),
            jax.ShapeDtypeStruct((3, BLOCK, BLOCK, NBLOCK), F32),
            jax.ShapeDtypeStruct((ROWS, 128), BF16),
        ),
        in_specs=[pl.BlockSpec(memory_space=pltpu.SMEM)] + [anyspec] * 10,
        out_specs=(anyspec,) * 3,
        scratch_shapes=scratch,
        compiler_params=pltpu.CompilerParams(
            collective_id=0, has_side_effects=True, vmem_limit_bytes=62 * 1024 * 1024
        ),
        name="block_backward",
    )(
        frame_mask, video, cotangent, spatial_project, spatial_output, temporal_project, temporal_output,
        *blocks,
    )
    term = jax.ShapeDtypeStruct((BLOCK, BLOCK, NBLOCK), F32)
    grad, sout, tin, tout, sin = pl.pallas_call(
        unpack_kernel,
        out_shape=(jax.ShapeDtypeStruct((2, 64, D), BF16), term, term, term, term),
        in_specs=[anyspec] * 3,
        out_specs=(anyspec,) * 5,
        scratch_shapes=[
            vm((ROWS, 128), BF16), vm((4, BLOCK, BLOCK, NBLOCK), F32), vm((2, 64, D), BF16), dma((5,)), dma((5,)),
        ],
        compiler_params=pltpu.CompilerParams(vmem_limit_bytes=62 * 1024 * 1024),
        name="unpack_terms",
    )(red, terms, grad)
    sin, sout, tin, tout = (r.transpose(2, 0, 1) for r in (sin, sout, tin, tout))
    return grad, sin, sout, tin, tout


def solution(mesh):
    split = P("frame", "patch", None)
    in_specs = (split, split) + (P(),) * 9
    out_specs = (split,) + (P(),) * 4
    return jax.shard_map(
        per_device, mesh=mesh, in_specs=in_specs, out_specs=out_specs, check_vma=False
    )
```

```python
import itertools
import math

import jax
import jax.numpy as jnp
from jax import lax
from jax.experimental import pallas as pl
from jax.experimental.pallas import tpu as pltpu
from jax.sharding import PartitionSpec as P

D = 1152
HEADS = 16
HEAD_DIM = 72
BLOCK = 32
GROUPS = D // 128
FRAMES = 8
PATCHES = 2048
ZWAYS = 4
PWAYS = 32
DEVICES = ZWAYS * PWAYS
TOKENS = 128
ROWS = D // 4
NBLOCK = D // 32

EPSILON = 1e-06
NEGATIVE = -1e30
SCALE = 1.0 / math.sqrt(HEAD_DIM)
LOG2E = math.log2(math.e)
LN2 = math.log(2.0)

F32 = jnp.float32
BF16 = jnp.bfloat16
MESH = pl.DeviceIdType.MESH


def hops(step):
    return min(step[0], 4 - step[0]) + min(step[1], 4 - step[1]) + min(step[3], 4 - step[3])


PLANE = sorted(
    [s for s in itertools.product(range(4), range(4), range(2), [0]) if any(s)], key=lambda s: -hops(s)
)
SPACE = sorted(
    [s for s in itertools.product(range(4), range(4), range(2), range(4)) if any(s)],
    key=lambda s: -hops(s),
)
SLOTS = PLANE + [(0, 0, 0, 0)]
SLOT_OF = {s[:3]: n for n, s in enumerate(SLOTS)}


def dot(a, b):
    return lax.dot_general(a, b, (((1,), (0,)), ((), ())), preferred_element_type=F32)


def dot_nt(a, b):
    return lax.dot_general(a, b, (((1,), (1,)), ((), ())), preferred_element_type=F32)


def dot_tn(a, b):
    return lax.dot_general(a, b, (((0,), (0,)), ((), ())), preferred_element_type=F32)


def lanes(shape):
    return lax.broadcasted_iota(jnp.int32, shape, len(shape) - 1)


def rows(shape):
    return lax.broadcasted_iota(jnp.int32, shape, 0)


def roll(x, amount):
    amount = amount % 128
    return x if amount == 0 else pltpu.roll(x, amount, 1)


def normalize(x):
    centered = x - jnp.mean(x, axis=-1, keepdims=True)
    inverse = lax.rsqrt(jnp.mean(centered * centered, axis=-1, keepdims=True) + EPSILON)
    return centered * inverse, inverse


def normalize_backward(adjoint, normed, inverse):
    grad_mean = jnp.mean(adjoint, axis=-1, keepdims=True)
    grad_cross = jnp.mean(adjoint * normed, axis=-1, keepdims=True)
    return inverse * (adjoint - grad_mean - normed * grad_cross)


def group(x, g):
    return x[:, g * 128 : (g + 1) * 128]


def rotate(x, blocks):
    return jnp.concatenate(
        [dot(group(x, g), blocks[g * 128 : (g + 1) * 128, :]) for g in range(GROUPS)], axis=1
    )


def rotate_transposed(x, blocks):
    return jnp.concatenate(
        [dot_nt(group(x, g), blocks[g * 128 : (g + 1) * 128, :]) for g in range(GROUPS)], axis=1
    )


def block_mask(shape):
    return (rows(shape) // BLOCK) % 4 == lanes(shape) // BLOCK


def rotation_gradient(left, right):
    mask = block_mask((128, 128))
    packed = []
    for g in range(GROUPS):
        full = jnp.where(mask, dot_tn(group(left, g), group(right, g)), 0.0)
        packed.append(full[0:32] + full[32:64] + full[64:96] + full[96:128])
    return packed


def layout_tools():
    shape = (BLOCK, 40, ROWS)
    b = lax.broadcasted_iota(jnp.int32, shape, 0)
    n = lax.broadcasted_iota(jnp.int32, shape, 1)
    from_row = lax.broadcasted_iota(jnp.int32, shape, 2)
    pick = jnp.where(from_row == (n >> 2) * BLOCK + b, 1.0, 0.0).reshape(BLOCK * 40, ROWS).astype(BF16)
    shape = (BLOCK, 40, 128)
    n = lax.broadcasted_iota(jnp.int32, shape, 1)
    own = ((n & 3) == (lax.broadcasted_iota(jnp.int32, shape, 2) >> 5)).reshape(BLOCK * 40, 128)
    repeat = jnp.where(lanes((128, 128)) % BLOCK == rows((128, 128)) % BLOCK, 1.0, 0.0).astype(BF16)
    return pick, own, repeat


def lay_out(tools, term, out):
    pick, own, repeat = tools
    lane = lanes((40, 128)) >> 5
    wide = dot(pick, term)
    wide = dot(jnp.where(own, wide, 0.0).astype(BF16), repeat)
    for m in range(8):
        four = jnp.zeros((40, 128), F32)
        for s in range(4):
            at = (4 * m + s) * 40
            four = jnp.where(lane == s, wide[at : at + 40], four)
        out[4 * m : 4 * m + 4] = four.T[:, 0:NBLOCK].reshape(4, BLOCK, NBLOCK)


def kernel(
    mask_ref, video, cotangent, wsp_h, wso_h, wtp_h, wto_h, rsi_h, rso_h, rti_h, rto_h,
    vg_ref, terms_ref, red_ref,
    wsp, wso, wtp, wto, r4, bd32, bd,
    vid, cot, vid_mid, ct_mid,
    normed1, inverse1, rot_b, proj,
    qkv_snd, qkv_rcv, beside_snd, fold, kx, qx, vx,
    att_snd, att_rcv, att1, top, aot, daz,
    normed2, proj2, att2_b, dproj_b,
    t_s, t_dp, t_p, t_ds,
    ah_snd, ah_rcv, do_snd, do_rcv, qt, dvt, pq,
    dk_snd, dk_rcv, dv_snd, dv_rcv, dq_snd, dq_rcv, dq_last, w_last, vg, dpt, adjt,
    r1_snd, r1_rcv, r1_z, r1_chunk, r1_out,
    r2_snd, r2_rcv, r2_z, r2_chunk, r3_snd, r3_rcv, r3_z, r3_chunk, terms,
    load_sems, out_sems, send_sems, recv_sems, qkv_sems, do_sems,
):
    z = lax.axis_index("frame")
    j = lax.axis_index("patch")
    px, py, pc = j >> 3, (j >> 1) & 3, j & 1
    xs = [((px + d) & 3) * 8 for d in range(4)]
    ys = [((py + d) & 3) * 2 for d in range(4)]
    cs = [(pc + d) & 1 for d in range(2)]
    zs = [(z + d) & 3 for d in range(4)]
    xys = [[a + b for b in ys] for a in xs]

    def ahead(step):
        return zs[step[3]], xys[step[0]][step[1]] + cs[step[2]]

    def behind(step):
        return zs[-step[3] & 3], xys[-step[0] & 3][-step[1] & 3] + cs[step[2]]

    def load(src, dst, n):
        return pltpu.make_async_copy(src, dst, load_sems.at[n])

    early = [load(video, vid, 0), load(rsi_h, r4.at[0], 1)]
    early += [
        load(wsp_h.at[:, pl.ds(c * D, D)], wsp.at[:, pl.ds(c * D, D)], n) for c, n in enumerate((2, 10, 11))
    ]
    late = [
        load(cotangent, cot, 3), load(rso_h, r4.at[1], 4), load(rti_h, r4.at[2], 5),
        load(rto_h, r4.at[3], 6), load(wto_h, wto, 7), load(wso_h, wso, 8), load(wtp_h, wtp, 9),
    ]
    for copy in early:
        copy.start()

    barrier = pltpu.get_barrier_semaphore()
    near = PLANE + [(0, 0, 0, d) for d in (2, 1, 3)]
    for step in near:
        pl.semaphore_signal(barrier, inc=1, device_id=ahead(step), device_id_type=MESH)

    def local(src, dst, sem):
        pltpu.make_async_copy(src, dst, sem).start()

    def remote(src, dst, phase, there, recv_sem=None):
        pltpu.make_async_remote_copy(
            src_ref=src, dst_ref=dst, send_sem=send_sems.at[phase],
            recv_sem=recv_sems.at[phase] if recv_sem is None else recv_sem,
            device_id=there, device_id_type=MESH,
        ).start()

    def wait_all(sem, buffer):
        pltpu.make_async_copy(buffer, buffer, sem).wait()

    def make_blocks(index):
        shape = (128, 512)
        spread = jnp.where(
            jnp.logical_and(
                rows(shape) // BLOCK == lanes(shape) // 128, rows(shape) % BLOCK == lanes(shape) % BLOCK
            ),
            1.0, 0.0,
        ).astype(BF16)
        shape = (NBLOCK, 128)
        own = rows(shape) % 4 == lanes(shape) // BLOCK
        for m in range(8):
            four = r4[index, 4 * m : 4 * m + 4].reshape(128, NBLOCK).astype(BF16)
            wide = dot_tn(four, spread)
            for s in range(4):
                bd32[pl.ds(4 * m + s, NBLOCK, stride=BLOCK), :] = jnp.where(own, group(wide, s), 0.0)
        bd[index] = bd32[...].astype(BF16)

    shape = (512, 384)
    source, target = rows(shape), lanes(shape)
    quarter, lane_in = source >> 7, source & 127
    to_pair = jnp.where(lane_in < 64, (quarter & 1) * 128 + (quarter >> 1) * 64 + lane_in, -1)
    to_last = jnp.where(jnp.logical_and(lane_in >= 64, lane_in < 88), 256 + quarter * 32 + lane_in - 64, -1)
    hit = jnp.logical_or(target == to_pair, target == to_last)
    fold[...] = jnp.where(hit, 1.0, 0.0).astype(BF16)

    early[0].wait()
    normed, _ = normalize(vid[...].reshape(TOKENS, D).astype(F32))
    early[1].wait()
    make_blocks(0)
    rot_b[...] = rotate(normed.astype(BF16), bd.at[0]).astype(BF16)

    for c in range(3):
        at = slice(c * D, (c + 1) * D)
        early[2 + c].wait()
        proj[:, at] = dot(rot_b[...], wsp[:, at])
    for copy in late:
        copy.start()

    lane = lanes((TOKENS, 128))
    qscale = jnp.where(lane < HEAD_DIM, SCALE * LOG2E, 1.0)
    for h in range(HEADS):
        t, off = (HEAD_DIM * h) // 128, (HEAD_DIM * h) % 128

        def pick(section, to):
            first = proj[:, section * D + t * 128 : section * D + (t + 1) * 128]
            if off + HEAD_DIM > 128:
                second = proj[:, section * D + (t + 1) * 128 : section * D + (t + 2) * 128]
                first = jnp.where(lane >= off, first, second)
            return roll(first, to - off)

        q, k, v = pick(0, 0), pick(1, 72), pick(2, 16)
        low = (jnp.where(lane < 72, q, k) * qscale).astype(BF16)
        high = jnp.where(lane < 16, k, jnp.where(lane < 88, v, 0.0)).astype(BF16)
        for f in range(2):
            item = f * HEADS + h
            qkv_snd[item, 0:64] = low[64 * f : 64 * (f + 1)]
            for e in range(4):
                at = 64 * f + 16 * e
                beside_snd[16 * item : 16 * item + 16, 128 * e : 128 * e + 128] = high[at : at + 16]
    folded = dot(beside_snd[...], fold[...]).astype(BF16)
    for part in range(3):
        qkv_snd[:, 64 + 16 * part : 80 + 16 * part] = group(folded, part).reshape(PWAYS, 16, 128)

    pl.semaphore_wait(barrier, len(near))

    for n, step in enumerate(SLOTS):
        dst = qkv_rcv.at[n]
        if any(step):
            zz, jj = ahead(step)
            remote(qkv_snd.at[jj], dst, 2, (zz, jj), qkv_sems.at[n // 8])
        else:
            local(qkv_snd.at[j], dst, qkv_sems.at[n // 8])

    late[0].wait()
    for phase, src, dst in ((1, cot, ct_mid), (0, vid, vid_mid)):
        for d in (2, 1, 3, 0):
            for f in range(2):
                piece = src.at[f, pl.ds(pl.multiple_of(zs[d] * 16, 16), 16)]
                if d:
                    remote(piece, dst.at[2 * z + f], phase, (zs[d], j))
                else:
                    local(piece, dst.at[2 * z + f], recv_sems.at[phase])

    for n in (1, 2, 3):
        late[n].wait()
        make_blocks(n)

    columns = vid[...].reshape(TOKENS, D).astype(F32).T
    columns = columns - jnp.mean(columns, axis=0, keepdims=True)
    inverse = lax.rsqrt(jnp.mean(columns * columns, axis=0, keepdims=True) + EPSILON)
    normed1[...] = columns * inverse
    inverse1[...] = jnp.broadcast_to(inverse, (8, 128))

    shape = (D, 128)
    column = HEAD_DIM * (lanes(shape) >> 3) + 64 + (lanes(shape) & 7)
    select = jnp.where(rows(shape) == column, 1.0, 0.0).astype(BF16)
    for n, section in enumerate((0, 2)):
        w_last[n] = dot(wsp[:, section * D : (section + 1) * D], select).astype(BF16)

    wait_all(recv_sems.at[1], ct_mid)
    frame_row = rows((TOKENS, 1)) // 16
    valid = jnp.zeros((TOKENS, 1), F32)
    for f in range(FRAMES):
        valid = jnp.where(frame_row == f, mask_ref[f].astype(F32), valid)
    top[...] = ct_mid[...].reshape(TOKENS, D).astype(F32) * valid
    late[4].wait()
    aot[...] = dot_nt(top[...].astype(BF16), wto[...]).astype(BF16)
    daz[:, 0:D] = rotate_transposed(aot[...], bd.at[3]).astype(BF16)
    daz[:, D:] = jnp.zeros((TOKENS, 128), BF16)

    lane2 = lanes((256, 128))
    ones = jnp.where(jnp.logical_and(lane2 >= 72, lane2 < 76), 1.0, 0.0)

    def prepare(i, carry):
        at = pl.ds(pl.multiple_of(i * 256, 256), 256)
        low, high = [], []
        for m in range(4):
            slot = qkv_rcv[4 * i + m].astype(F32)
            low.append(slot[0:64])
            mid, last = slot[64:96], slot[96:112]
            high.append(
                jnp.where(
                    lanes((64, 128)) < 64,
                    jnp.concatenate([mid, roll(mid, 64)], axis=0),
                    jnp.concatenate([roll(last, 64 - 32 * e) for e in range(4)], axis=0),
                )
            )
        t0, t1 = jnp.concatenate(low, axis=0), jnp.concatenate(high, axis=0)
        k = roll(jnp.where(lane2 >= 72, t0, t1), -72)
        kx[at, :] = jnp.where(lane2 < 72, k, ones).astype(BF16)
        vx[at, :] = jnp.where(lane2 < 72, roll(t1, -16), ones).astype(BF16)
        qx[at, :] = jnp.where(lane2 < 72, t0, 0.0).astype(BF16)
        return carry

    for g in range(4):
        wait_all(qkv_sems.at[g], qkv_rcv.at[pl.ds(8 * g, 8)])
        lax.fori_loop(2 * g, 2 * g + 2, prepare, 0)

    def attend_span(start, count):
        spans = [pl.ds(start + s * 256, 256) for s in range(count)]
        highs = []
        for s, at in enumerate(spans):
            scores = dot_nt(qx[at, :], kx[...])
            highs.append(jnp.max(scores, axis=-1, keepdims=True))
            pq[256 * s : 256 * s + 256, :] = jnp.exp2(scores - highs[-1]).astype(BF16)
        both_out = dot(pq[0 : 256 * count, :], vx[...])
        for s, (at, high_score) in enumerate(zip(spans, highs)):
            out = both_out[256 * s : 256 * s + 256]
            total = out[:, 72:73]
            att_snd[at, :] = jnp.where(lane2 < 72, out / total, 0.0).astype(BF16)
            neg = -(high_score + jnp.log(total) * LOG2E)
            hi = neg.astype(BF16).astype(F32)
            mid = (neg - hi).astype(BF16).astype(F32)
            lo = neg - hi - mid
            old = qx[at, :].astype(F32)
            new = jnp.where(
                lane2 == 72, hi, jnp.where(lane2 == 73, mid, jnp.where(lane2 == 74, lo, old))
            )
            qx[at, :] = new.astype(BF16)

    def send_attended(slots):
        for n in slots:
            for d in (2, 1, 3, 0):
                zz, jj = zs[d], behind(SLOTS[n])[1]
                src = att_snd.at[pl.ds(pl.multiple_of(64 * n + 16 * zz, 16), 16)]
                dst = att_rcv.at[2 * z + (j >> 4), j & 15]
                if d or any(SLOTS[n]):
                    remote(src, dst, 3, (zz, jj))
                else:
                    local(src, dst, recv_sems.at[3])

    def attend(i, carry):
        attend_span(pl.multiple_of(i * 512, 512), 2)
        for ii in range(1, 4):

            @pl.when(i == ii)
            def _():
                send_attended(range(8 * ii, 8 * ii + 8))

        return carry

    for half in range(2):
        attend_span(256 * half, 1)
        send_attended(range(4 * half, 4 * half + 4))
    lax.fori_loop(1, 4, attend, 0)

    wait_all(recv_sems.at[0], vid_mid)
    wait_all(recv_sems.at[3], att_rcv)

    def add_piece(tiles, at, piece):
        tiles[at] = piece if tiles[at] is None else tiles[at] + piece

    def place(tiles, h, value):
        t, off = (HEAD_DIM * h) // 128, (HEAD_DIM * h) % 128
        if off + HEAD_DIM > 128:
            add_piece(tiles, t, jnp.where(lane >= off, value, 0.0))
            add_piece(tiles, t + 1, jnp.where(lane < off, value, 0.0))
        else:
            add_piece(tiles, t, value)

    tiles = [None] * GROUPS
    for h in range(HEADS):
        place(tiles, h, roll(att_rcv[:, h].reshape(TOKENS, 128).astype(F32), (HEAD_DIM * h) % 128))
    for t in range(GROUPS):
        att1[:, t * 128 : (t + 1) * 128] = tiles[t].astype(BF16)

    late[5].wait()
    outrot = rotate(att1[...], bd.at[1]).astype(BF16)
    hidden = vid_mid[...].reshape(TOKENS, D).astype(F32) + dot(outrot, wso[...])
    hidden = hidden.astype(BF16).astype(F32)
    normed, inverse2 = normalize(hidden)
    normed2[...] = normed
    rot_b[...] = rotate(normed.astype(BF16), bd.at[2]).astype(BF16)
    late[6].wait()

    for c in range(3):
        at = slice(c * D, (c + 1) * D)
        proj2[:, at] = dot(rot_b[...], wtp[:, at]).astype(BF16)

    square = (TOKENS, TOKENS)
    same_patch = rows(square) % 16 == lanes(square) % 16
    same_frame = rows(square) // 16 == lanes(square) // 16
    key_valid = jnp.zeros(square, F32)
    for f in range(FRAMES):
        key_valid = jnp.where(rows(square) // 16 == f, mask_ref[f].astype(F32), key_valid)
    allowed = jnp.logical_and(same_patch, jnp.logical_or(key_valid == 1.0, same_frame))
    bias = jnp.where(allowed, 0.0, NEGATIVE)

    def window(h, section):
        t, off = (HEAD_DIM * h) // 128, (HEAD_DIM * h) % 128
        width = 256 if off + HEAD_DIM > 128 else 128
        return slice(section * D + t * 128, section * D + t * 128 + width)

    def own_lanes(h):
        off = (HEAD_DIM * h) % 128
        l = lanes((1, 256 if off + HEAD_DIM > 128 else 128))
        return jnp.where(jnp.logical_and(l >= off, l < off + HEAD_DIM), 1.0, 0.0)

    for h in range(HEADS):
        own = own_lanes(h).astype(BF16)
        t_s[h] = dot_nt(proj2[:, window(h, 1)], proj2[:, window(h, 0)] * own)
        t_dp[h] = dot_nt(proj2[:, window(h, 2)], daz[:, window(h, 0)] * own)

    for h in range(HEADS):
        scores = t_s[h] * SCALE + bias
        e = jnp.exp(scores - jnp.max(scores, axis=0, keepdims=True))
        p = e * (1.0 / jnp.sum(e, axis=0, keepdims=True))
        dp = t_dp[h]
        t_p[h] = p.astype(BF16)
        t_ds[h] = (p * (dp - jnp.sum(p * dp, axis=0, keepdims=True))).astype(BF16)

    def gather(section, dst, base):
        tiles = [None] * (GROUPS + 1)
        for h in range(HEADS):
            own = own_lanes(h)
            own_b = own.astype(BF16)
            if section == 0:
                part = dot_tn(t_ds[h], proj2[:, window(h, 1)]) * (own * SCALE)
            elif section == 1:
                part = dot(t_ds[h], proj2[:, window(h, 0)] * own_b) * SCALE
            elif section == 2:
                part = dot(t_p[h], daz[:, window(h, 0)] * own_b)
            else:
                part = dot_tn(t_p[h], proj2[:, window(h, 2)]) * own
            t = (HEAD_DIM * h) // 128
            for w in range(part.shape[1] // 128):
                add_piece(tiles, t + w, group(part, w))
        for t in range(GROUPS):
            dst[:, base + t * 128 : base + (t + 1) * 128] = tiles[t].astype(BF16)

    for section in range(3):
        gather(section, dproj_b, section * D)

    adj_rot2 = jnp.concatenate(
        [dot_nt(dproj_b[...], wtp[c * 384 : (c + 1) * 384, :]).astype(BF16) for c in range(3)], axis=1
    )
    adj_normed = rotate_transposed(adj_rot2, bd.at[2])
    adj_hidden = top[...] + normalize_backward(adj_normed, normed2[...], inverse2)
    adj_hidden_b = adj_hidden.astype(BF16)
    ah_snd[...] = adj_hidden_b.reshape(FRAMES, 16, D)
    aho = dot_nt(adj_hidden_b, wso[...]).astype(BF16)
    adj_att1 = rotate_transposed(aho, bd.at[1])
    for h in range(HEADS):
        t, off = (HEAD_DIM * h) // 128, (HEAD_DIM * h) % 128
        first = group(adj_att1, t)
        if off + HEAD_DIM > 128:
            first = jnp.where(lane >= off, first, group(adj_att1, t + 1))
        piece = jnp.where(lane < 72, roll(first, -off), 0.0).astype(BF16)
        do_snd[:, h] = piece.reshape(FRAMES, 16, 128)

    for step in [SLOTS[8 * g + m][:3] + (d,) for g in (3, 2, 1, 0) for m in range(8) for d in (2, 1, 3, 0)]:
        zz, jj = ahead(step)
        src = do_snd.at[2 * zz + (jj >> 4), jj & 15]
        n = SLOT_OF[step[:3]]
        dst = do_rcv.at[pl.ds(pl.multiple_of(64 * n + 16 * z, 16), 16)]
        if any(step):
            remote(src, dst, 4, (zz, jj), do_sems.at[n // 8])
        else:
            local(src, dst, do_sems.at[n // 8])
    for d in (2, 1, 3, 0):
        for f in range(2):
            src = ah_snd.at[2 * zs[d] + f]
            dst = ah_rcv.at[f, pl.ds(pl.multiple_of(z * 16, 16), 16)]
            if d:
                remote(src, dst, 5, (zs[d], j))
            else:
                local(src, dst, recv_sems.at[5])

    gather(3, att2_b, 0)
    for n, packed in enumerate((
        rotation_gradient(att1[...], aho),
        rotation_gradient(normed2[...].astype(BF16), adj_rot2),
        rotation_gradient(att2_b[...], aot[...]),
    )):
        for g in range(GROUPS):
            r1_snd[n * GROUPS + g] = packed[g].astype(BF16)

    def reduce_first(snd, rcv, chunk_of, owns, phase):
        for step in SLOTS:
            zz, jj = ahead(step)

            @pl.when(owns(jj))
            def _():
                if any(step):
                    remote(snd.at[chunk_of(jj)], rcv.at[j], phase, (zz, jj))
                else:
                    local(snd.at[chunk_of(jj)], rcv.at[j], recv_sems.at[phase])

    def reduce_second(rcv, zbuf, owns, phase):
        @pl.when(owns(j))
        def _():
            wait_all(recv_sems.at[phase], rcv)
            zbuf[z] = jnp.sum(rcv[...].astype(F32), axis=0)
            for d in (2, 1, 3):
                remote(zbuf.at[z], zbuf.at[z], phase + 1, (zs[d], j))

    def reduce_third(zbuf, chunk, out, chunk_of, owns, phase):
        size = chunk.shape[0]

        @pl.when(owns(j))
        def _():
            wait_all(recv_sems.at[phase + 1], zbuf.at[pl.ds(0, ZWAYS - 1)])
            chunk[...] = (((zbuf[0] + zbuf[1]) + (zbuf[2] + zbuf[3])) / 128.0).astype(BF16)
            dst = out.at[pl.ds(pl.multiple_of(chunk_of(j) * size, size), size)]
            for step in SLOTS:
                if any(step):
                    remote(chunk, dst, phase + 2, ahead(step))
                else:
                    local(chunk, dst, recv_sems.at[phase + 2])

    def reduce_sent(snd, rcv, zbuf, owners, owns, phase):
        @pl.when(owns(j))
        def _():
            wait_all(send_sems.at[phase], snd.at[pl.ds(0, owners - 1)])
            wait_all(send_sems.at[phase + 1], zbuf.at[pl.ds(0, ZWAYS - 1)])
            wait_all(send_sems.at[phase + 2], rcv.at[pl.ds(0, PWAYS - 1)])

        @pl.when(jnp.logical_not(owns(j)))
        def _():
            wait_all(send_sems.at[phase], snd)

    def chunk1(jj):
        return jj

    def owns1(jj):
        return jj < 27

    reduce_first(r1_snd, r1_rcv, chunk1, owns1, 7)

    def probabilities(i, carry):
        for s in range(2):
            at = pl.ds(pl.multiple_of(i * 512 + s * 256, 256), 256)
            pq[at, :] = jnp.exp2(dot_nt(qx[at, :], kx[...])).astype(BF16)
        return carry

    lax.fori_loop(0, 4, probabilities, 0)

    def prepare_queries(i, carry):
        at = pl.ds(pl.multiple_of(i * 256, 256), 256)
        qt[:, at] = qx[at, :].astype(F32).T[0:80].astype(BF16)
        return carry

    lax.fori_loop(0, 8, prepare_queries, 0)

    def beside(left, right, odd):
        left, right = (roll(left, 64), right) if odd else (left, roll(right, 64))
        return jnp.where(lanes(left.shape) < 64, left, right)

    def value_gradient(group_):
        at = pl.ds(group_ * 512, 512)
        dv = dot(do_rcv[at, :].astype(F32).T[0:80].astype(BF16), pq[at, :])
        if group_ == 3:
            dvt[...] = dv
        else:
            dvt[...] += dv

    def attend_back(group_):
        at = pl.ds(group_ * 512, 512)
        lane5 = lanes((512, 128))
        g = do_rcv[at, :].astype(F32)
        delta = -jnp.sum(g * att_snd[at, :].astype(F32), axis=-1, keepdims=True)
        hi = delta.astype(BF16).astype(F32)
        lo = delta - hi
        dox = jnp.where(lane5 == 72, hi, jnp.where(lane5 == 73, lo, g)).astype(BF16)
        ds = (pq[at, :].astype(F32) * dot_nt(dox, vx[...])).astype(BF16)
        dq = dot(ds, kx[...]).T * SCALE
        for m in range(8):
            tile = dq[:, 128 * (m // 2) : 128 * (m // 2) + 128]
            dq_snd[8 * group_ + m] = beside(tile[0:32], tile[32:64], m % 2).astype(BF16)
        dq_last[:, group_ * 512 : group_ * 512 + 512] = dq[64:72]
        pq[at, :] = ds
        send_back(dq_snd, dq_rcv, 13, range(8 * group_, 8 * group_ + 8))

    def send_back(snd, rcv, phase, slots):
        for n in slots:
            if any(SLOTS[n]):
                remote(snd.at[n], rcv.at[j], phase, behind(SLOTS[n]))
            else:
                local(snd.at[n], rcv.at[j], recv_sems.at[phase])

    for group_ in (3, 2, 1, 0):
        wait_all(do_sems.at[group_], do_rcv.at[pl.ds(512 * group_, 512)])
        value_gradient(group_)
        if group_ >= 2:
            attend_back(group_)
    for n in range(PWAYS):
        at = slice(128 * (n // 2), 128 * (n // 2) + 128)
        dv_snd[n] = beside(dvt[0:32, at], dvt[32:64, at], n % 2).astype(BF16)
    send_back(dv_snd, dv_rcv, 15, range(PWAYS))
    for group_ in (1, 0):
        attend_back(group_)

    def key_gradient(group_):
        return dot(qt[...], pq[:, 512 * group_ : 512 * group_ + 512]) * LN2

    dk = key_gradient(0)
    for group_ in range(4):
        following = key_gradient(group_ + 1) if group_ < 3 else None
        for m in range(8):
            n = 8 * group_ + m
            at, here = slice(128 * (n // 2), 128 * (n // 2) + 128), slice(128 * (m // 2), 128 * (m // 2) + 128)
            rest = [dk[48:72, here], dq_last[:, at], dvt[64:72, at], jnp.zeros((8, 128), F32)]
            dk_snd[n] = beside(dk[0:48, here], jnp.concatenate(rest, axis=0), n % 2).astype(BF16)
        send_back(dk_snd, dk_rcv, 6, range(8 * group_, 8 * group_ + 8))
        dk = following

    reduce_second(r1_rcv, r1_z, owns1, 7)

    def halves(buffer, h):
        one, two = buffer[h].astype(F32), buffer[HEADS + h].astype(F32)
        first = lanes(one.shape) < 64
        return jnp.where(first, one, roll(two, 64)), jnp.where(first, roll(one, 64), two)

    def unpack_first(buffer, base):
        for pair in range(HEADS // 2):
            parts = []
            for h in (2 * pair, 2 * pair + 1):
                parts += [*halves(buffer, h), jnp.zeros((8, 128), F32)]
            at = base + 144 * pair
            dpt[at : at + 144] = jnp.concatenate(parts, axis=0).astype(BF16)

    wait_all(recv_sems.at[15], dv_rcv)
    unpack_first(dv_rcv, 2 * D)
    for c in range(3):
        at = slice(c * 384, (c + 1) * 384)
        adjt[at] = dot(wsp[at, 2 * D :], dpt[2 * D :])
    wait_all(recv_sems.at[13], dq_rcv)
    unpack_first(dq_rcv, 0)
    for c in range(3):
        at = slice(c * 384, (c + 1) * 384)
        adjt[at] += dot(wsp[at, 0:D], dpt[0:D])
    reduce_third(r1_z, r1_chunk, r1_out, chunk1, owns1, 7)
    wait_all(recv_sems.at[6], dk_rcv)

    last = [[], []]
    for pair in range(HEADS // 2):
        parts = []
        for h in (2 * pair, 2 * pair + 1):
            left, right = halves(dk_rcv, h)
            parts += [left, right[0:24]]
            last[0].append(right[24:32])
            last[1].append(right[32:40])
        at = D + 144 * pair
        dpt[at : at + 144] = jnp.concatenate(parts, axis=0).astype(BF16)
    last = [jnp.concatenate(parts, axis=0).astype(BF16) for parts in last]

    for c in range(3):
        at = slice(c * 384, (c + 1) * 384)
        adjt[at] += (
            dot(wsp[at, D : 2 * D], dpt[D : 2 * D]) + dot(w_last[0, at], last[0]) + dot(w_last[1, at], last[1])
        )
    packed = []
    mask = block_mask((128, 128))
    for g in range(GROUPS):
        at = slice(g * 128, (g + 1) * 128)
        full = jnp.where(mask, dot_nt(normed1[at].astype(BF16), adjt[at].astype(BF16)), 0.0)
        packed.append(full[0:32] + full[32:64] + full[64:96] + full[96:128])
    flat = jnp.concatenate(packed, axis=0).astype(BF16)
    for o in range(8):
        r2_snd[o] = flat[32 * o : 32 * o + 32]
    for o in range(2):
        r3_snd[o] = flat[256 + 16 * o : 272 + 16 * o]
    owner = 2 * px + pc
    more = (owner & 3) == 0
    row = [s for s in SLOTS if s[1] == 0]
    sheet = [s for s in SPACE if s[0] == 0 and s[2] == 0]
    for step in row:
        zz, jj = ahead(step)
        there = 2 * (jj >> 3) + (jj & 1)
        if any(step):
            remote(r2_snd.at[there], r2_rcv.at[owner], 10, (zz, jj))
        else:
            local(r2_snd.at[there], r2_rcv.at[owner], recv_sems.at[10])

        @pl.when((there & 3) == 0)
        def _():
            if any(step):
                remote(r3_snd.at[there >> 2], r3_rcv.at[owner], 14, (zz, jj))
            else:
                local(r3_snd.at[there >> 2], r3_rcv.at[owner], recv_sems.at[14])

    adj_normed = jnp.concatenate(
        [
            dot(bd[0, g * 128 : (g + 1) * 128, :], adjt[g * 128 : (g + 1) * 128].astype(BF16))
            for g in range(GROUPS)
        ],
        axis=0,
    )
    grad_mean = jnp.mean(adj_normed, axis=0, keepdims=True)
    grad_cross = jnp.mean(adj_normed * normed1[...], axis=0, keepdims=True)
    grad = (inverse1[0:1] * (adj_normed - grad_mean - normed1[...] * grad_cross)).T
    wait_all(recv_sems.at[5], ah_rcv)
    grad = ah_rcv[...].reshape(TOKENS, D).astype(F32) + grad
    vg[...] = grad.astype(BF16).reshape(2, 64, D)
    vg_out = pltpu.make_async_copy(vg, vg_ref, out_sems.at[0])
    vg_out.start()
    def sheet_sum(rcv, zbuf, phase_in, phase):
        wait_all(recv_sems.at[phase_in], rcv)
        own = 4 * z + py
        zbuf[own] = jnp.sum(rcv[...].astype(F32), axis=0).astype(BF16)
        for step in sheet:
            remote(zbuf.at[own], zbuf.at[own], phase, ahead(step))

    sheet_sum(r2_rcv, r2_z, 10, 11)

    @pl.when(more)
    def _():
        sheet_sum(r3_rcv, r3_z, 14, 16)

    wait_all(send_sems.at[0], vid_mid.at[pl.ds(0, 6)])
    wait_all(send_sems.at[1], ct_mid.at[pl.ds(0, 6)])
    wait_all(send_sems.at[2], qkv_snd.at[pl.ds(0, PWAYS - 1)])
    wait_all(send_sems.at[3], att_snd.at[pl.ds(0, PATCHES - 16)])
    wait_all(send_sems.at[4], do_rcv.at[pl.ds(0, PATCHES - 16)])
    wait_all(send_sems.at[5], ah_snd.at[pl.ds(0, 6)])
    wait_all(send_sems.at[6], dk_snd.at[pl.ds(0, PWAYS - 1)])
    wait_all(send_sems.at[15], dv_snd.at[pl.ds(0, PWAYS - 1)])
    wait_all(send_sems.at[13], dq_snd.at[pl.ds(0, PWAYS - 1)])
    wait_all(recv_sems.at[9], r1_out)
    def row_spread(zbuf, chunk, dst, phase_in, phase):
        wait_all(recv_sems.at[phase_in], zbuf.at[pl.ds(0, 15)])
        chunk[...] = (jnp.sum(zbuf[...].astype(F32), axis=0) / 128.0).astype(BF16)
        for step in row:
            if any(step):
                remote(chunk, dst, phase, ahead(step))
            else:
                local(chunk, dst, recv_sems.at[phase])

    row_spread(r2_z, r2_chunk, red_ref.at[pl.ds(pl.multiple_of(32 * owner, 32), 32)], 11, 12)

    @pl.when(more)
    def _():
        row_spread(r3_z, r3_chunk, red_ref.at[pl.ds(pl.multiple_of(256 + 16 * (owner >> 2), 16), 16)], 16, 17)

    tools = layout_tools()
    for n in range(3):
        lay_out(tools, r1_out[n * ROWS : (n + 1) * ROWS], terms.at[n])
    red1 = pltpu.make_async_copy(terms, terms_ref, out_sems.at[1])
    red1.start()
    reduce_sent(r1_snd, r1_rcv, r1_z, 27, owns1, 7)
    wait_all(send_sems.at[10], r2_snd.at[pl.ds(0, 7)])
    wait_all(send_sems.at[11], r2_z.at[pl.ds(0, 15)])
    wait_all(send_sems.at[12], r2_rcv.at[pl.ds(0, 7)])

    @pl.when(more)
    def _():
        wait_all(send_sems.at[14], r3_snd.at[0])
        wait_all(send_sems.at[16], r3_z.at[pl.ds(0, 15)])
        wait_all(send_sems.at[17], r3_rcv.at[pl.ds(0, 7)])

    @pl.when(jnp.logical_not(more))
    def _():
        wait_all(send_sems.at[14], r3_snd)

    wait_all(recv_sems.at[12], red_ref.at[pl.ds(0, 256)])
    wait_all(recv_sems.at[17], red_ref.at[pl.ds(256, 32)])
    red1.wait()
    vg_out.wait()


def unpack_kernel(sin_h, terms_h, vg_in, vg_out, sout, tin, tout, sin, packed, terms, vg, in_sems, out_sems):
    loads = [pltpu.make_async_copy(sin_h, packed, in_sems.at[0])]
    loads += [pltpu.make_async_copy(terms_h.at[n], terms.at[n], in_sems.at[n + 1]) for n in range(3)]
    loads.append(pltpu.make_async_copy(vg_in, vg, in_sems.at[4]))
    for copy in loads:
        copy.start()
    stores = [pltpu.make_async_copy(terms.at[n], out, out_sems.at[n]) for n, out in enumerate((sout, tin, tout, sin))]
    stores.append(pltpu.make_async_copy(vg, vg_out, out_sems.at[4]))
    tools = layout_tools()
    loads[0].wait()
    lay_out(tools, packed[...], terms.at[3])
    stores[3].start()
    for n, at in ((1, 0), (2, 1), (3, 2), (4, 4)):
        loads[n].wait()
        stores[at].start()
    for store in stores:
        store.wait()


def per_device(
    video,
    cotangent,
    frame_mask,
    spatial_project,
    spatial_output,
    temporal_project,
    temporal_output,
    spatial_inward,
    spatial_outward,
    temporal_inward,
    temporal_outward,
):
    vm = pltpu.VMEM
    dma = pltpu.SemaphoreType.DMA
    scratch = [
        vm((D, 3 * D), BF16), vm((D, D), BF16), vm((D, 3 * D), BF16), vm((D, D), BF16),
        vm((4, BLOCK, BLOCK, NBLOCK), F32), vm((D, 128), F32), vm((4, D, 128), BF16),
        vm((2, 64, D), BF16), vm((2, 64, D), BF16), vm((FRAMES, 16, D), BF16), vm((FRAMES, 16, D), BF16),
        vm((D, TOKENS), F32), vm((8, TOKENS), F32), vm((TOKENS, D), BF16), vm((TOKENS, 3 * D), F32),
        vm((PWAYS, 112, 128), BF16), vm((PWAYS, 112, 128), BF16), vm((512, 512), BF16), vm((512, 384), BF16),
        vm((PATCHES, 128), BF16), vm((PATCHES, 128), BF16), vm((PATCHES, 128), BF16),
        vm((PATCHES, 128), BF16), vm((FRAMES, HEADS, 16, 128), BF16), vm((TOKENS, D), BF16),
        vm((TOKENS, D), F32), vm((TOKENS, D), BF16), vm((TOKENS, D + 128), BF16),
        vm((TOKENS, D), F32), vm((TOKENS, 3 * D), BF16),
        vm((TOKENS, D), BF16), vm((TOKENS, 3 * D), BF16),
        vm((HEADS, TOKENS, TOKENS), F32), vm((HEADS, TOKENS, TOKENS), F32),
        vm((HEADS, TOKENS, TOKENS), BF16), vm((HEADS, TOKENS, TOKENS), BF16),
        vm((FRAMES, 16, D), BF16), vm((2, 64, D), BF16),
        vm((FRAMES, HEADS, 16, 128), BF16), vm((PATCHES, 128), BF16),
        vm((80, PATCHES), BF16), vm((80, PATCHES), F32), vm((PATCHES, PATCHES), BF16),
        vm((PWAYS, 48, 128), BF16), vm((PWAYS, 48, 128), BF16), vm((PWAYS, 32, 128), BF16), vm((PWAYS, 32, 128), BF16),
        vm((PWAYS, 32, 128), BF16), vm((PWAYS, 32, 128), BF16), vm((8, PATCHES), F32), vm((2, D, 128), BF16),
        vm((2, 64, D), BF16),
        vm((3 * D, TOKENS), BF16), vm((D, TOKENS), F32),
        vm((27, 32, 128), BF16), vm((PWAYS, 32, 128), BF16), vm((ZWAYS, 32, 128), F32),
        vm((32, 128), BF16), vm((3 * ROWS, 128), BF16),
        vm((8, 32, 128), BF16), vm((8, 32, 128), BF16), vm((16, 32, 128), BF16), vm((32, 128), BF16),
        vm((2, 16, 128), BF16), vm((8, 16, 128), BF16), vm((16, 16, 128), BF16), vm((16, 128), BF16),
        vm((3, BLOCK, BLOCK, NBLOCK), F32),
        dma((12,)), dma((3,)), dma((18,)), dma((18,)), dma((4,)), dma((4,)),
    ]
    anyspec = pl.BlockSpec(memory_space=pl.ANY)
    blocks = [r.transpose(1, 2, 0) for r in (spatial_inward, spatial_outward, temporal_inward, temporal_outward)]
    grad, terms, red = pl.pallas_call(
        kernel,
        out_shape=(
            jax.ShapeDtypeStruct((2, 64, D), BF16),
            jax.ShapeDtypeStruct((3, BLOCK, BLOCK, NBLOCK), F32),
            jax.ShapeDtypeStruct((ROWS, 128), BF16),
        ),
        in_specs=[pl.BlockSpec(memory_space=pltpu.SMEM)] + [anyspec] * 10,
        out_specs=(anyspec,) * 3,
        scratch_shapes=scratch,
        compiler_params=pltpu.CompilerParams(
            collective_id=0, has_side_effects=True, vmem_limit_bytes=62 * 1024 * 1024
        ),
        name="block_backward",
    )(
        frame_mask, video, cotangent, spatial_project, spatial_output, temporal_project, temporal_output,
        *blocks,
    )
    term = jax.ShapeDtypeStruct((BLOCK, BLOCK, NBLOCK), F32)
    grad, sout, tin, tout, sin = pl.pallas_call(
        unpack_kernel,
        out_shape=(jax.ShapeDtypeStruct((2, 64, D), BF16), term, term, term, term),
        in_specs=[anyspec] * 3,
        out_specs=(anyspec,) * 5,
        scratch_shapes=[
            vm((ROWS, 128), BF16), vm((4, BLOCK, BLOCK, NBLOCK), F32), vm((2, 64, D), BF16), dma((5,)), dma((5,)),
        ],
        compiler_params=pltpu.CompilerParams(vmem_limit_bytes=62 * 1024 * 1024),
        name="unpack_terms",
    )(red, terms, grad)
    sin, sout, tin, tout = (r.transpose(2, 0, 1) for r in (sin, sout, tin, tout))
    return grad, sin, sout, tin, tout


def solution(mesh):
    split = P("frame", "patch", None)
    in_specs = (split, split) + (P(),) * 9
    out_specs = (split,) + (P(),) * 4
    return jax.shard_map(
        per_device, mesh=mesh, in_specs=in_specs, out_specs=out_specs, check_vma=False
    )
```
